128 devices in a mesh: boot: 4 (over x_hi, core), slab: 32 (over y, x_lo, z).
Axes of the slice: x: 4 (x_hi: 2, x_lo: 2; x = x_hi * 2 + x_lo), y: 4, z: 4, core: 2. Of those that a mesh axis runs over, the one named last changes fastest.
Arguments:
- params: bfloat16 [2, 200, 262144], P(None, None, 'slab'), may hold values from -6 to 6
- predicted: bfloat16 [200, 4096], P(None, 'slab'), may hold values from -6 to 6
- perturbation: bfloat16 [200, 4096], P(None, 'slab'), may hold values from -6 to 6
- observed: bfloat16 [4096], P('slab'), may hold values from -6 to 6
- obs_sd: bfloat16 [4096], P('slab'), may hold values from 0.5 to 2
- members: int32 [16, 200], P('boot'), may hold values from 0 to 199
- block_map: int32 [2048, 64], P('slab'), may hold values from 0 to 4095
Outputs:
- posterior: float32 [2, 200, 262144], P(None, None, 'slab')
The draws below stay inside these ranges and needn't reach their ends.
Inputs may be any that keep to these rules, and one draw needn't show every extreme that they name: Row r lists the 200 members, with repetition, of resample r. `block_map`: row k lists the 64 data whose gains are kept for cells k * 128 to k * 128 + 127.
All inputs are finite; a program needn't handle non-finite values.
Results may differ from the reference program's by a relative error of at most 0.00065.
Values may be sent and summed in bfloat16 or wider, within the bound.
No kernel may reach another device: no remote copies, remote signals or barrier semaphores. Data moves between devices by JAX's collectives and lax.ppermute only.
A program may use at most 256 MiB of HBM per device.

```python
import math
import jax
import jax.numpy as jnp
from jax import lax

M = 200
ND = 4096
NB = 16
BLK = 128
NNZ = 64
CELLS = 262144
NBLK = 2048


factor_count = 12


decay_ratio = 0.75


def unit_entries(key_part, shape):
    return jax.random.normal(key_part, shape, jnp.float32)


def draw_predicted(key, part):
    key = jax.random.fold_in(key, 11)
    key_scale, key_bulk, key_load, key_shape = jax.random.split(key, 4)
    lowest_scale = 0.02
    member_scale = jnp.exp(jax.random.uniform(key_scale, (M, 1), jnp.float32, math.log(lowest_scale), math.log(1.5)))
    result = member_scale * unit_entries(key_bulk, (M, ND))
    loadings = unit_entries(key_load, (M, factor_count))
    patterns = unit_entries(key_shape, (factor_count, ND))
    for index in range(factor_count):
        weight_now = decay_ratio ** index
        result = result + weight_now * loadings[:, index:index + 1] * patterns[index:index + 1, :]
    result = jnp.clip(result, -6.0, 6.0)
    return result.astype(jnp.bfloat16)


def plant(drawn, stream_key, smallest, top_value):
    dims = drawn.shape
    index_at = [jax.random.randint(jax.random.fold_in(stream_key, axis), (), 0, dims[axis]) for axis in range(len(dims))]
    drawn = drawn.at[tuple(index_at)].set(smallest)
    longest = dims.index(max(dims))
    index_at[longest] = (index_at[longest] + 1) % dims[longest]
    return drawn.at[tuple(index_at)].set(top_value)


def levels(stream_key, dims, shards, least, high):
    level, own = 1.0, jax.random.fold_in(stream_key, 6)
    for position, parts in shards:
        draws = jnp.exp(jax.random.uniform(jax.random.fold_in(own, position), (parts,), jnp.float32, least / len(shards), high / len(shards)))
        level = level * jnp.repeat(draws, dims[position] // parts).reshape([-1 if axis == position else 1 for axis in range(len(dims))])
    return level


def gaussian(rng, extent, scale, most, shards=(), kind=jnp.bfloat16):
    loudness = levels(rng, extent, shards, -0.22, 0.18) if shards else 1.0
    drawn = jax.random.normal(rng, extent, jnp.float32) * scale * loudness
    return jnp.minimum(jnp.maximum(drawn, -most), most).astype(kind)


def setup_inputs(seed: int = 0) -> dict:
    arg_keys = jax.random.split(jax.random.key(seed), 8)
    params = gaussian(arg_keys[0], (2, M, CELLS), 1.0, 6.0, ((2, 32),))
    predicted = draw_predicted(jax.random.fold_in(arg_keys[7], 71), 0)
    perturbation = gaussian(arg_keys[2], (M, ND), 1.0, 6.0, ((1, 32),))
    observed = gaussian(arg_keys[3], (ND,), 1.0, 6.0, ((0, 32),))
    obs_sd = jnp.clip(jnp.exp(math.log(2.0) - 1.3862944 * jax.random.uniform(arg_keys[4], (ND,), jnp.float32) ** levels(arg_keys[4], (ND,), ((0, 32),), -0.2, 0.2)), 0.5, 2.0).astype(jnp.bfloat16)
    members = plant(jax.random.randint(arg_keys[5], (NB, M), 0, M), jax.random.fold_in(arg_keys[5], 1), 0, M - 1).astype(jnp.int32)
    block_map = plant(jax.random.randint(arg_keys[6], (NBLK, NNZ), 0, ND), jax.random.fold_in(arg_keys[6], 1), 0, ND - 1).astype(jnp.int32)
    return dict(params=params, predicted=predicted, perturbation=perturbation, observed=observed, obs_sd=obs_sd, members=members, block_map=block_map)


screen_floor = 1e-05
highest = lax.Precision.HIGHEST

def centering(members_count):
    return (jnp.eye(members_count, dtype=jnp.float32) - 1.0 / members_count) / math.sqrt(members_count - 1)

def projector(chosen, center):
    members_count = center.shape[0]
    onehot = (jnp.arange(members_count, dtype=jnp.int32)[:, None] == chosen.astype(jnp.int32)[None, :]).astype(jnp.float32)
    return jnp.dot(onehot, center, precision=highest)

def member_map(gram_matrix, proj_matrix):
    members_count = gram_matrix.shape[0]
    inner = jnp.dot(gram_matrix, proj_matrix, precision=highest)
    system = jnp.eye(members_count, dtype=jnp.float32) + jnp.dot(proj_matrix.T, inner, precision=highest)
    factor = jnp.linalg.cholesky(system)
    solved = jax.scipy.linalg.cho_solve((factor, True), proj_matrix.T)
    return jnp.dot(proj_matrix, solved, precision=highest)

def reference(params, predicted, perturbation, observed, obs_sd, members, block_map):
    noise = obs_sd.astype(jnp.float32)
    ensemble = predicted.astype(jnp.float32)
    scaled = ensemble / noise
    weighted = scaled / noise
    gram_matrix = jnp.dot(scaled, scaled.T, precision=highest)
    innovation = (observed.astype(jnp.float32) + noise * perturbation.astype(jnp.float32) - ensemble).astype(jnp.bfloat16)
    center = centering(M)
    blocks = params.astype(jnp.float32).reshape(2, M, NBLK, BLK)

    def gain_of(proj_matrix):
        mapping = member_map(gram_matrix, proj_matrix)
        columns = jnp.dot(mapping, weighted, precision=highest).astype(jnp.bfloat16)
        selected = jnp.take(columns, block_map, axis=1).astype(jnp.float32)
        return jnp.einsum('pmkc,mkj->pjkc', blocks, selected, precision=highest)
    full_gain = gain_of(center)

    def add_spread(total, chosen):
        return (total + jnp.square(gain_of(projector(chosen, center)) - full_gain), None)
    spread, _ = lax.scan(add_spread, jnp.zeros_like(full_gain), members)
    spread = spread / NB
    squared = full_gain * full_gain
    screened = (squared / (squared + spread + screen_floor) * full_gain).astype(jnp.bfloat16)
    chosen_innov = jnp.take(innovation, block_map, axis=1).astype(jnp.float32)
    change = jnp.einsum('pjkc,mkj->pmkc', screened.astype(jnp.float32), chosen_innov, precision=highest)
    return params.astype(jnp.float32) + change.reshape(2, M, CELLS)
```

```python
from functools import partial
import math

import jax
import jax.numpy as jnp
from jax import lax
from jax.experimental import pallas as pl
from jax.experimental.pallas import tpu as pltpu
from jax.sharding import PartitionSpec as P

M = 200
NB = 16
BLK = 128
NNZ = 64
MP = 256
HALF = 104
SHIFT = 96
ROWS = 112
PIV = 40
SYS = 9
MAPS = 17
GROUP = 8

screen_floor = 1e-05
f32 = jnp.float32
bf16 = jnp.bfloat16


def iota(shape, dim):
    return lax.broadcasted_iota(jnp.int32, shape, dim)


def split3(x):
    hi = x.astype(bf16).astype(f32)
    rest = x - hi
    mid = rest.astype(bf16).astype(f32)
    return hi, mid, rest - mid


def lhs6(c):
    hi, mid, lo = split3(c)
    left = hi + pltpu.roll(hi, PIV, 1) + pltpu.roll(hi, 2 * PIV, 1)
    right = mid + pltpu.roll(mid, PIV, 1) + pltpu.roll(lo, 2 * PIV, 1)
    return jnp.concatenate([left, right], axis=1).astype(bf16)


def rhs6(r):
    hi, mid, lo = split3(r)
    pad = jnp.zeros((BLK - 3 * PIV, MP), f32)
    return jnp.concatenate([hi, mid, lo, pad, hi, mid, hi, pad], axis=0).astype(bf16)


def dot(a, b):
    return jnp.dot(a, b, preferred_element_type=f32)


def member_rows(first, second):
    low = jnp.concatenate([first[:HALF], second[HALF - SHIFT:HALF - SHIFT + BLK - HALF]], axis=0)
    rest = second[BLK - SHIFT:HALF]
    return low, rest


def counts(members_ref, s):
    row = members_ref[pl.ds(s, 1), :]
    hit = jnp.where(iota((M, MP), 0) == row, 1.0, 0.0)
    down = jnp.sum(hit, axis=1, keepdims=True)
    across = jnp.sum(jnp.where(iota((M, MP), 0) == iota((M, MP), 1), down, 0.0), axis=0, keepdims=True)
    return jnp.sqrt(down), jnp.sqrt(across)


def map_kernel(core_ref, own_ref, other_ref, members_ref, full_ref, res_ref, gram_ref, sys_ref, piv_ref):
    core = core_ref[0]

    def chunk(i):
        own = own_ref[i].astype(f32)
        other = other_ref[i].astype(f32)
        first = jnp.where(core == 0, own, other)
        second = jnp.where(core == 0, other, own)
        low, rest = member_rows(first, second)
        sd = own[HALF:HALF + 1]
        ens = jnp.concatenate([low, rest, jnp.zeros((MP - M, BLK), f32)], axis=0)
        return ens, ens / (sd * sd)

    gram_ref[...] = jnp.zeros((MP, MP), f32)

    def add_gram(i, carry):
        a0, w0 = chunk(2 * i)
        a1, w1 = chunk(2 * i + 1)
        ens = jnp.concatenate([a0, a1], axis=1).astype(bf16)
        parts = split3(jnp.concatenate([w0, w1], axis=1))
        total = gram_ref[...]
        for part in parts:
            total = total + lax.dot_general(part.astype(bf16), ens, (((1,), (1,)), ((), ())), preferred_element_type=f32)
        gram_ref[...] = total
        return carry

    lax.fori_loop(0, own_ref.shape[0] // 2, add_gram, 0)

    row = iota((M, MP), 0)
    lane = iota((M, MP), 1)

    def build(s, carry):
        down, across = counts(members_ref, s)
        h = gram_ref[:M, :] * (down * (1.0 / (M - 1))) * across
        ud = down * (1.0 / math.sqrt(M))
        ua = across * (1.0 / math.sqrt(M))
        hu = jnp.sum(h * ua, axis=1, keepdims=True)
        uh = jnp.sum(h * ud, axis=0, keepdims=True)
        uhu = jnp.sum(hu * ud, axis=0, keepdims=True)
        h = h - ud * (uh - 0.5 * uhu * ua) - (hu - 0.5 * uhu * ud) * ua
        sys_ref[s] = h + jnp.where(row == lane, 1.0, 0.0)
        return carry

    lax.fori_loop(0, SYS, build, 0)

    prow = iota((PIV, MP), 0)
    plane = iota((PIV, MP), 1)
    drow = iota((PIV, BLK), 0)
    dlane = iota((PIV, BLK), 1)

    def panel_step(kp, carry):
        k0 = kp * PIV
        back = lax.rem(MP - k0, MP)
        ds = []
        for s in range(SYS):
            panel = sys_ref[s, pl.ds(pl.multiple_of(k0, 8), PIV), :]
            ds.append(jnp.where(dlane < PIV, pltpu.roll(panel, back, 1)[:, :BLK], 0.0))
        for t in range(PIV):
            at_lane = dlane == t
            at_row = drow == t
            for s in range(SYS):
                d = ds[s]
                col = d[:, t:t + 1]
                scale = 1.0 / d[t:t + 1, t:t + 1]
                line = jnp.where(dlane[:1] == t, 1.0, d[t:t + 1, :]) * scale
                new = jnp.where(at_lane, 0.0, d) - col * line
                ds[s] = jnp.where(at_row, line, new)
        for s in range(SYS):
            piv_ref[s] = ds[s]

        def update(s, inner):
            a = sys_ref[s]
            panel = sys_ref[s, pl.ds(pl.multiple_of(k0, 8), PIV), :]
            inside = (plane >= k0) & (plane < k0 + PIV)
            panel = jnp.where(plane == prow + k0, 1.0, jnp.where(inside, 0.0, panel))
            r = dot(lhs6(piv_ref[s]), rhs6(panel))
            c = jnp.where(iota((M, BLK), 1) < PIV, pltpu.roll(a, back, 1)[:, :BLK], 0.0)
            kept = jnp.where((lane >= k0) & (lane < k0 + PIV), 0.0, a)
            sys_ref[s] = kept - dot(lhs6(c), rhs6(r))
            sys_ref[s, pl.ds(pl.multiple_of(k0, 8), PIV), :] = r
            return inner

        lax.fori_loop(0, SYS, update, 0)
        return carry

    lax.fori_loop(0, M // PIV, panel_step, 0)

    def finish(s):
        down, across = counts(members_ref, s)
        ud = down * (1.0 / math.sqrt(M))
        ua = across * (1.0 / math.sqrt(M))
        return (sys_ref[s] - ud * ua) * (down * (1.0 / (M - 1))) * across

    full_ref[...] = finish(0)

    def finish_res(s, carry):
        res_ref[s] = finish(s + 1)
        return carry

    lax.fori_loop(0, SYS - 1, finish_res, 0)


def select_kernel(core_ref, map_ref, own_ref, other_ref, iown_ref, iother_ref, psel_ref, isel_ref, ptab_ref, itab_ref, line_ref):
    core = core_ref[0]
    blocks = map_ref.shape[0]

    def table(i, carry):
        for a_ref, b_ref, t_ref in ((own_ref, other_ref, ptab_ref), (iown_ref, iother_ref, itab_ref)):
            own = a_ref[i].astype(f32)
            other = b_ref[i].astype(f32)
            first = jnp.where(core == 0, own, other)
            second = jnp.where(core == 0, other, own)
            low, rest = member_rows(first, second)
            high = jnp.concatenate([rest, own[HALF:ROWS], jnp.zeros((2 * BLK - M - (ROWS - HALF), BLK), f32)], axis=0)
            base = pl.multiple_of(i * (2 * BLK), 8)
            t_ref[pl.ds(base, BLK, stride=2), :] = low.T
            t_ref[pl.ds(base + 1, BLK, stride=2), :] = high.T
        return carry

    lax.fori_loop(0, own_ref.shape[0], table, 0)

    def pick(t_ref, k, out_ref, at):
        for j in range(NNZ):
            line_ref[2 * j:2 * j + 2, :] = t_ref[pl.ds(2 * map_ref[k, j], 2), :]
        both = jnp.concatenate([line_ref[pl.ds(0, NNZ, stride=2), :], line_ref[pl.ds(1, NNZ, stride=2), :]], axis=1)
        out_ref[pl.ds(pl.multiple_of(at * NNZ, NNZ), NNZ), :] = both.astype(bf16)

    def pick_pred(k, carry):
        pick(ptab_ref, core * (blocks // 2) + k, psel_ref, k)
        return carry

    lax.fori_loop(0, blocks // 2, pick_pred, 0)

    def pick_innov(k, carry):
        pick(itab_ref, k, isel_ref, k)
        return carry

    lax.fori_loop(0, blocks, pick_innov, 0)


def gain_kernel(core_ref, psel_ref, full_ref, mine_ref, theirs_ref, params_ref, out_ref, maps_ref, cols_ref):
    @pl.when(pl.program_id(0) == 0)
    def _():
        def place(r, value):
            pad = jnp.zeros((MP - M, MP), f32)
            for n, part in enumerate(split3(value)):
                maps_ref[r, n * MP:(n + 1) * MP, :] = jnp.concatenate([part, pad], axis=0).astype(bf16)

        place(0, full_ref[...])

        def place_both(r, carry):
            place(1 + r, mine_ref[r])
            place(SYS + r, theirs_ref[r])
            return carry

        lax.fori_loop(0, SYS - 1, place_both, 0)

    x = psel_ref[...]
    sd = x[:, M:M + 1].astype(f32)
    weight = 1.0 / (sd * sd)

    def column(r, carry):
        total = dot(x, maps_ref[r, 0:MP, :]) + dot(x, maps_ref[r, MP:2 * MP, :]) + dot(x, maps_ref[r, 2 * MP:3 * MP, :])
        total = (total * weight).astype(bf16)
        for g in range(GROUP):
            cols_ref[g, pl.ds(pl.multiple_of(r * NNZ, NNZ), NNZ), :] = total[g * NNZ:(g + 1) * NNZ]
        return carry

    lax.fori_loop(0, MAPS, column, 0)

    def gains(g, carry):
        at = pl.ds(pl.multiple_of(g * BLK, BLK), BLK)
        cells = jnp.concatenate([params_ref[0, :, at], params_ref[1, :, at]], axis=1)
        every = dot(cols_ref[g][:, :M], cells)
        full = every[:NNZ]
        spread = jnp.zeros_like(full)
        for r in range(1, MAPS):
            off = every[r * NNZ:(r + 1) * NNZ] - full
            spread = spread + off * off
        squared = full * full
        out_ref[g] = (squared / (squared + spread * (1.0 / NB) + screen_floor) * full).astype(bf16)
        return carry

    lax.fori_loop(0, GROUP, gains, 0)


def change_kernel(half_ref, isel_ref, screened_ref, params_ref, *rest):
    out_ref = rest[-1]
    for g in range(GROUP):
        change = lax.dot_general(
            isel_ref[g * NNZ:(g + 1) * NNZ, :], screened_ref[g], (((0,), (0,)), ((), ())), preferred_element_type=f32
        )
        at = slice(g * BLK, (g + 1) * BLK)
        for p in range(2):
            out_ref[p, :, at] = params_ref[p, :, at].astype(f32) + change[:M, p * BLK:(p + 1) * BLK]


vmem = pl.BlockSpec(memory_space=pltpu.VMEM)
smem = pl.BlockSpec(memory_space=pltpu.SMEM)
limit = pltpu.CompilerParams(vmem_limit_bytes=56 * 1024 * 1024)


def make_maps(core, own, other, members):
    return pl.pallas_call(
        map_kernel,
        out_shape=(jax.ShapeDtypeStruct((M, MP), f32), jax.ShapeDtypeStruct((SYS - 1, M, MP), f32)),
        in_specs=[smem, vmem, vmem, vmem],
        out_specs=(vmem, vmem),
        scratch_shapes=[
            pltpu.VMEM((MP, MP), f32),
            pltpu.VMEM((SYS, M, MP), f32),
            pltpu.VMEM((SYS, PIV, BLK), f32),
        ],
        compiler_params=limit,
        cost_estimate=pl.CostEstimate(flops=20_000_000_000, bytes_accessed=8_000_000, transcendentals=0),
        name="maps",
    )(core, own, other, members)


def select(core, block_map, own, other, iown, iother):
    blocks = block_map.shape[0]
    data = own.shape[0] * BLK
    return pl.pallas_call(
        select_kernel,
        out_shape=(
            jax.ShapeDtypeStruct((blocks // 2 * NNZ, MP), bf16),
            jax.ShapeDtypeStruct((blocks * NNZ, MP), bf16),
        ),
        in_specs=[smem, smem, vmem, vmem, vmem, vmem],
        out_specs=(vmem, vmem),
        scratch_shapes=[
            pltpu.VMEM((2 * data, BLK), f32),
            pltpu.VMEM((2 * data, BLK), f32),
            pltpu.VMEM((2 * NNZ, BLK), f32),
        ],
        compiler_params=limit,
        cost_estimate=pl.CostEstimate(flops=10_000_000_000, bytes_accessed=8_000_000, transcendentals=0),
        name="select",
    )(core, block_map, own, other, iown, iother)


def make_screened(core, psel, full, mine, theirs, params):
    blocks = params.shape[2] // BLK // 2
    steps = blocks // GROUP
    return pl.pallas_call(
        gain_kernel,
        out_shape=jax.ShapeDtypeStruct((blocks, NNZ, 2 * BLK), bf16),
        grid_spec=pltpu.PrefetchScalarGridSpec(
            num_scalar_prefetch=1,
            grid=(steps,),
            in_specs=[
                pl.BlockSpec((GROUP * NNZ, MP), lambda i, c: (i, 0)),
                pl.BlockSpec((M, MP), lambda i, c: (0, 0)),
                pl.BlockSpec((SYS - 1, M, MP), lambda i, c: (0, 0, 0)),
                pl.BlockSpec((SYS - 1, M, MP), lambda i, c: (0, 0, 0)),
                pl.BlockSpec((2, M, GROUP * BLK), lambda i, c: (0, 0, c[0] * steps + i)),
            ],
            out_specs=pl.BlockSpec((GROUP, NNZ, 2 * BLK), lambda i, c: (i, 0, 0)),
            scratch_shapes=[
                pltpu.VMEM((MAPS, 3 * MP, MP), bf16),
                pltpu.VMEM((GROUP, MAPS * NNZ, MP), bf16),
            ],
        ),
        compiler_params=limit,
        cost_estimate=pl.CostEstimate(flops=20_000_000_000, bytes_accessed=8_000_000, transcendentals=0),
        name="gains",
    )(core, psel, full, mine, theirs, params)


def update(half, isel, screened, params, so_far=None):
    blocks = params.shape[2] // BLK // 2
    steps = blocks // GROUP
    cells = pl.BlockSpec((2, M, GROUP * BLK), lambda i, c: (0, 0, c[0] * steps + i))
    in_specs = [
        pl.BlockSpec((GROUP * NNZ, MP), lambda i, c: (c[0] * steps + i, 0)),
        pl.BlockSpec((GROUP, NNZ, 2 * BLK), lambda i, c: (i, 0, 0)),
        cells,
    ]
    operands = (half, isel, screened, params)
    if so_far is not None:
        in_specs.append(pl.BlockSpec(memory_space=pl.ANY))
        operands = operands + (so_far,)
    return pl.pallas_call(
        change_kernel,
        out_shape=jax.ShapeDtypeStruct(params.shape, f32),
        grid_spec=pltpu.PrefetchScalarGridSpec(
            num_scalar_prefetch=1, grid=(steps,), in_specs=in_specs, out_specs=cells
        ),
        input_output_aliases={} if so_far is None else {4: 0},
        compiler_params=limit,
        cost_estimate=pl.CostEstimate(flops=5_000_000_000, bytes_accessed=10_000_000, transcendentals=0),
        name="change",
    )(*operands)


def on_device(params, predicted, perturbation, observed, obs_sd, members, block_map):
    boot = lax.axis_index("boot")
    core = lax.rem(boot, 2)
    core_arg = core.reshape(1).astype(jnp.int32)
    slabs = lax.axis_size("slab")
    pair = [(i, i ^ 1) for i in range(4)]
    far = [(i, i ^ 2) for i in range(4)]

    def share(rows):
        part = lax.dynamic_slice_in_dim(rows, core * SHIFT, HALF, 0)
        tail = jnp.zeros((ROWS - HALF - 1, rows.shape[1]), bf16)
        return jnp.concatenate([part, obs_sd[None], tail], axis=0)

    def spread_out(part):
        whole = jnp.broadcast_to(part[None], (slabs,) + part.shape)
        own = lax.all_to_all(whole, "slab", 0, 0)
        return own, lax.ppermute(own, "boot", pair)

    noise = obs_sd.astype(f32)
    innovation = (observed.astype(f32) + noise * perturbation.astype(f32) - predicted.astype(f32)).astype(bf16)

    far_members = lax.ppermute(members, "boot", far)
    every = jnp.arange(M, dtype=jnp.int32)[None]
    lists = jnp.concatenate([every, members, far_members], axis=0)
    lists = jnp.pad(lists, ((0, 16 - SYS), (0, MP - M)), constant_values=-1)

    own, other = spread_out(share(predicted))
    innov_part, other = lax.optimization_barrier((share(innovation), other))
    iown, iother = spread_out(innov_part)

    full, mine = make_maps(core_arg, own, other, lists)
    block_map, mine = lax.optimization_barrier((block_map, mine))
    theirs = lax.ppermute(mine, "boot", pair)
    psel, isel = select(core_arg, block_map, own, other, iown, iother)
    screened = make_screened(core_arg, psel, full, mine, theirs, params)
    screened_other = lax.ppermute(screened, "boot", pair)
    partial_out = update(core_arg, isel, screened, params)
    return update(1 - core_arg, isel, screened_other, params, partial_out)


def solution(mesh):
    return jax.shard_map(
        on_device,
        mesh=mesh,
        in_specs=(
            P(None, None, "slab"),
            P(None, "slab"),
            P(None, "slab"),
            P("slab"),
            P("slab"),
            P("boot", None),
            P("slab", None),
        ),
        out_specs=P(None, None, "slab"),
        check_vma=False,
    )
```

```python
from functools import partial
import math

import jax
import jax.numpy as jnp
from jax import lax
from jax.experimental import pallas as pl
from jax.experimental.pallas import tpu as pltpu
from jax.sharding import PartitionSpec as P

M = 200
NB = 16
BLK = 128
NNZ = 64
MP = 256
HALF = 104
SHIFT = 96
ROWS = 112
PIV = 40
SYS = 9
PACK = 3
ROWS_M = 208
MAPS = 17
GROUP = 8

screen_floor = 1e-05
f32 = jnp.float32
bf16 = jnp.bfloat16


def iota(shape, dim):
    return lax.broadcasted_iota(jnp.int32, shape, dim)


def split3(x):
    hi = x.astype(bf16).astype(f32)
    rest = x - hi
    mid = rest.astype(bf16).astype(f32)
    return hi, mid, rest - mid


def lhs6(c):
    hi, mid, lo = split3(c)
    left = hi + pltpu.roll(hi, PIV, 1) + pltpu.roll(hi, 2 * PIV, 1)
    right = mid + pltpu.roll(mid, PIV, 1) + pltpu.roll(lo, 2 * PIV, 1)
    return jnp.concatenate([left, right], axis=1).astype(bf16)


def rhs6(r):
    hi, mid, lo = split3(r)
    pad = jnp.zeros((BLK - 3 * PIV, MP), f32)
    return jnp.concatenate([hi, mid, lo, pad, hi, mid, hi, pad], axis=0).astype(bf16)


def dot(a, b):
    return jnp.dot(a, b, preferred_element_type=f32)


def counts(members_ref, s):
    row = members_ref[pl.ds(s, 1), :]
    hit = jnp.where(iota((M, MP), 0) == row, 1.0, 0.0)
    down = jnp.sum(hit, axis=1, keepdims=True)
    across = jnp.sum(jnp.where(iota((M, MP), 0) == iota((M, MP), 1), down, 0.0), axis=0, keepdims=True)
    return jnp.sqrt(down), jnp.sqrt(across)


def pack_kernel(core_ref, pred_ref, pert_ref, obs_ref, sd_ref, ens_ref, innov_ref):
    core = core_ref[0]
    sd = sd_ref[...].astype(f32)
    ens = pred_ref[...].astype(f32)
    innov = obs_ref[...].astype(f32) + sd * pert_ref[...].astype(f32) - ens
    tail = jnp.concatenate([sd, jnp.zeros((ROWS - HALF - 1, BLK), f32)], axis=0)
    for rows, out_ref in ((ens, ens_ref), (innov, innov_ref)):
        part = jnp.where(core == 0, rows[:HALF], rows[SHIFT:SHIFT + HALF])
        part = jnp.concatenate([part, tail], axis=0).astype(bf16)
        for i in range(out_ref.shape[0]):
            out_ref[i] = part


def members_first(core, own, other):
    first = jnp.where(core == 0, own, other)
    second = jnp.where(core == 0, other, own)
    low = jnp.concatenate([first[:HALF], second[HALF - SHIFT:BLK - SHIFT]], axis=0)
    high = jnp.concatenate([second[BLK - SHIFT:HALF], own[HALF:ROWS], jnp.zeros((MP - M - (ROWS - HALF), BLK), f32)], axis=0)
    return low, high


def fill_table(t_ref, i, low, high):
    base = pl.multiple_of(i * (2 * BLK), 8)
    t_ref[pl.ds(base, BLK, stride=2), :] = low
    t_ref[pl.ds(base + 1, BLK, stride=2), :] = high


def pick(t_ref, map_ref, k, line_ref):
    for j in range(NNZ):
        line_ref[2 * j:2 * j + 2, :] = t_ref[pl.ds(2 * map_ref[k, j], 2), :]
    both = [line_ref[pl.ds(n, NNZ, stride=2), :] for n in range(2)]
    return jnp.concatenate(both, axis=1).astype(bf16)


def map_kernel(core_ref, map_ref, own_ref, other_ref, members_ref, full_ref, res_ref, psel_ref, ens_ref, parts_ref, table_ref, line_ref, *sys_refs):
    core = core_ref[0]
    blocks = map_ref.shape[0]

    def chunk(i, carry):
        own = own_ref[i].astype(f32)
        low, high = members_first(core, own, other_ref[i].astype(f32))
        sd = own[HALF:HALF + 1]
        at = pl.ds(pl.multiple_of(i * BLK, BLK), BLK)
        rows = jnp.concatenate([low, high[:ROWS_M - BLK]], axis=0)
        for n, part in enumerate(split3(rows * (1.0 / (sd * sd)))):
            parts_ref[n, :, at] = part.astype(bf16)
        low, high = low.T, high.T
        ens_ref[at, :] = jnp.concatenate([low, high], axis=1).astype(bf16)
        fill_table(table_ref, i, low, high)
        return carry

    lax.fori_loop(0, own_ref.shape[0], chunk, 0, unroll=4)

    gram = 0.0
    for n in (2, 1, 0):
        gram = gram + dot(parts_ref[n], ens_ref[...])
    gram = gram[:M]

    def pick_own(k, carry):
        psel_ref[pl.ds(pl.multiple_of(k * NNZ, NNZ), NNZ), :] = pick(
            table_ref, map_ref, core * (blocks // 2) + k, line_ref
        )
        return carry

    lax.fori_loop(0, blocks // 2, pick_own, 0)

    row = iota((M, MP), 0)
    lane = iota((M, MP), 1)
    for s in range(SYS):
        down, across = counts(members_ref, s)
        h = gram * (down * (1.0 / (M - 1))) * across
        ud = down * (1.0 / math.sqrt(M))
        ua = across * (1.0 / math.sqrt(M))
        hu = jnp.sum(h * ua, axis=1, keepdims=True)
        uh = jnp.sum(h * ud, axis=0, keepdims=True)
        uhu = jnp.sum(hu * ud, axis=0, keepdims=True)
        h = h - ud * (uh - 0.5 * uhu * ua) - (hu - 0.5 * uhu * ud) * ua
        sys_refs[s][...] = h + jnp.where(row == lane, 1.0, 0.0)

    prow = iota((PIV, MP), 0)
    plane = iota((PIV, MP), 1)
    dlane = iota((PIV, BLK), 1)
    trow = iota((8, BLK), 0)
    tlane = iota((8, BLK), 1)
    first = jnp.minimum(tlane // PIV, PACK - 1) * PIV
    inner = tlane - first

    def panel_step(kp, carry):
        k0 = kp * PIV
        at = pl.ds(pl.multiple_of(k0, 8), PIV)
        packs = []
        for g in range(SYS // PACK):
            pack = jnp.zeros((PIV, BLK), f32)
            for q in range(PACK):
                moved = pltpu.roll(sys_refs[PACK * g + q][at, :], lax.rem(MP - k0 + q * PIV, MP), 1)[:, :BLK]
                pack = jnp.where((dlane >= q * PIV) & (dlane < (q + 1) * PIV), moved, pack)
            packs.append(pack)
        starts = packs
        tiles = [[pack[8 * i:8 * i + 8] for i in range(PIV // 8)] for pack in packs]
        for j in range(PIV // 8):
            cols = [
                [[jnp.take_along_axis(tile, first + 8 * j + u, axis=1) for u in range(8)] for tile in group]
                for group in tiles
            ]
            for u in range(8):
                at_lane = inner == 8 * j + u
                for group, col in zip(tiles, cols):
                    lead = col[j][u]
                    scale = 1.0 / lead[u:u + 1]
                    t = group[j]
                    line = jnp.where(at_lane[:1], 1.0, t[u:u + 1]) * scale
                    group[j] = jnp.where(trow == u, line, jnp.where(at_lane, 0.0, t) - lead * line)
                    for v in range(u + 1, 8):
                        c = col[j][v]
                        line = c[u:u + 1] * scale
                        col[j][v] = jnp.where(trow == u, line, c - lead * line)
            done = (inner >= 8 * j) & (inner < 8 * j + 8)
            for group, col in zip(tiles, cols):
                for i in range(PIV // 8):
                    if i != j:
                        tile = jnp.where(done, 0.0, group[i])
                        for u in range(8):
                            tile = tile - col[i][u] * group[j][u:u + 1]
                        group[i] = tile
        packs = [jnp.concatenate(group, axis=0) for group in tiles]
        inside = (lane >= k0) & (lane < k0 + PIV)
        pad = jnp.zeros((BLK - 3 * PIV, MP), f32)
        inverses, blocks_, panels, wanted, lines = [], [], [], [], []
        for s in range(SYS):
            back = (BLK - (s % PACK) * PIV) % BLK
            for kept, source in ((inverses, packs), (blocks_, starts)):
                moved = source[s // PACK]
                if back:
                    moved = pltpu.roll(moved, back, 1)
                kept.append(lhs6(jnp.where(dlane < PIV, moved, 0.0)))
            panels.append(sys_refs[s][at, :])
            wanted.append(jnp.where(plane == prow + k0, -1.0, jnp.where(inside[:PIV], 0.0, panels[s])))
        for s in range(SYS):
            lines.append(dot(inverses[s], rhs6(wanted[s])))
        for s in range(SYS):
            lines[s] = lines[s] + dot(inverses[s], rhs6(wanted[s] - dot(blocks_[s], rhs6(lines[s]))))
        for s in range(SYS):
            hi, mid, lo = split3(panels[s])
            left = jnp.concatenate([hi, hi, hi, pad, mid, mid, lo, pad], axis=0).astype(bf16)
            change = lax.dot_general(left, rhs6(lines[s]), (((0,), (0,)), ((), ())), preferred_element_type=f32)
            sys_refs[s][...] = jnp.where(inside, 0.0, sys_refs[s][...]) - change[:M]
            sys_refs[s][at, :] = lines[s]
        return carry

    lax.fori_loop(0, M // PIV, panel_step, 0)

    for s in range(SYS):
        down, across = counts(members_ref, s)
        both = down * across
        value = (-sys_refs[s][...] - both * (1.0 / M)) * (both * (1.0 / (M - 1)))
        if s == 0:
            full_ref[...] = value
        else:
            res_ref[s - 1] = value


def select_kernel(core_ref, map_ref, own_ref, other_ref, isel_ref, table_ref, line_ref):
    core = core_ref[0]

    def chunk(i, carry):
        low, high = members_first(core, own_ref[i].astype(f32), other_ref[i].astype(f32))
        fill_table(table_ref, i, low.T, high.T)
        return carry

    lax.fori_loop(0, own_ref.shape[0], chunk, 0, unroll=4)

    def pick_all(k, carry):
        isel_ref[pl.ds(pl.multiple_of(k * NNZ, NNZ), NNZ), :] = pick(table_ref, map_ref, k, line_ref)
        return carry

    lax.fori_loop(0, map_ref.shape[0], pick_all, 0)


def gain_kernel(core_ref, psel_ref, full_ref, mine_ref, theirs_ref, params_ref, out_ref, maps_ref, cols_ref):
    @pl.when(pl.program_id(0) == 0)
    def _():
        def place(r, value):
            pad = jnp.zeros((MP - M, MP), f32)
            for n, part in enumerate(split3(value)):
                maps_ref[r, n * MP:(n + 1) * MP, :] = jnp.concatenate([part, pad], axis=0).astype(bf16)

        place(0, full_ref[...])

        def place_both(r, carry):
            place(1 + r, mine_ref[r])
            place(SYS + r, theirs_ref[r])
            return carry

        lax.fori_loop(0, SYS - 1, place_both, 0)

    x = psel_ref[...]
    sd = x[:, M:M + 1].astype(f32)
    weight = 1.0 / (sd * sd)

    x3 = jnp.concatenate([x, x, x], axis=1)

    def column(r, carry):
        total = dot(x3, maps_ref[r])
        total = (total * weight).astype(bf16)
        for g in range(GROUP):
            cols_ref[g, pl.ds(pl.multiple_of(r * NNZ, NNZ), NNZ), :] = total[g * NNZ:(g + 1) * NNZ]
        return carry

    lax.fori_loop(0, MAPS, column, 0, unroll=True)

    def gains(g, carry):
        at = pl.ds(pl.multiple_of(g * BLK, BLK), BLK)
        cells = jnp.concatenate([params_ref[0, :, at], params_ref[1, :, at]], axis=1)
        every = dot(cols_ref[g][:, :M], cells)
        full = every[:NNZ]
        spread = jnp.zeros_like(full)
        for r in range(1, MAPS):
            off = every[r * NNZ:(r + 1) * NNZ] - full
            spread = spread + off * off
        squared = full * full
        out_ref[g] = (squared / (squared + spread * (1.0 / NB) + screen_floor) * full).astype(bf16)
        return carry

    lax.fori_loop(0, GROUP, gains, 0, unroll=4)


def change_kernel(half_ref, isel_ref, screened_ref, params_ref, *rest):
    out_ref = rest[-1]
    for g in range(GROUP):
        change = lax.dot_general(
            isel_ref[g * NNZ:(g + 1) * NNZ, :], screened_ref[g], (((0,), (0,)), ((), ())), preferred_element_type=f32
        )
        at = slice(g * BLK, (g + 1) * BLK)
        for p in range(2):
            out_ref[p, :, at] = params_ref[p, :, at].astype(f32) + change[:M, p * BLK:(p + 1) * BLK]


vmem = pl.BlockSpec(memory_space=pltpu.VMEM)
smem = pl.BlockSpec(memory_space=pltpu.SMEM)
limit = pltpu.CompilerParams(vmem_limit_bytes=56 * 1024 * 1024)


def pack(core, predicted, perturbation, observed, obs_sd, slabs):
    whole = jax.ShapeDtypeStruct((slabs, ROWS, BLK), bf16)
    return pl.pallas_call(
        pack_kernel,
        out_shape=(whole, whole),
        in_specs=[smem, vmem, vmem, vmem, vmem],
        out_specs=(vmem, vmem),
        compiler_params=limit,
        name="pack",
    )(core, predicted, perturbation, observed[None], obs_sd[None])


def make_maps(core, block_map, own, other, members):
    blocks = block_map.shape[0]
    data = own.shape[0] * BLK
    return pl.pallas_call(
        map_kernel,
        out_shape=(
            jax.ShapeDtypeStruct((M, MP), f32),
            jax.ShapeDtypeStruct((SYS - 1, M, MP), f32),
            jax.ShapeDtypeStruct((blocks // 2 * NNZ, MP), bf16),
        ),
        in_specs=[smem, smem, vmem, vmem, vmem],
        out_specs=(vmem, vmem, vmem),
        scratch_shapes=[
            pltpu.VMEM((data, MP), bf16),
            pltpu.VMEM((3, ROWS_M, data), bf16),
            pltpu.VMEM((2 * data, BLK), f32),
            pltpu.VMEM((2 * NNZ, BLK), f32),
        ] + [pltpu.VMEM((M, MP), f32)] * SYS,
        compiler_params=limit,
        cost_estimate=pl.CostEstimate(flops=20_000_000_000, bytes_accessed=8_000_000, transcendentals=0),
        name="maps",
    )(core, block_map, own, other, members)


def select(core, block_map, own, other):
    blocks = block_map.shape[0]
    data = own.shape[0] * BLK
    return pl.pallas_call(
        select_kernel,
        out_shape=jax.ShapeDtypeStruct((blocks * NNZ, MP), bf16),
        in_specs=[smem, smem, vmem, vmem],
        out_specs=vmem,
        scratch_shapes=[pltpu.VMEM((2 * data, BLK), f32), pltpu.VMEM((2 * NNZ, BLK), f32)],
        compiler_params=limit,
        cost_estimate=pl.CostEstimate(flops=10_000_000_000, bytes_accessed=8_000_000, transcendentals=0),
        name="select",
    )(core, block_map, own, other)


def make_screened(core, psel, full, mine, theirs, params):
    blocks = params.shape[2] // BLK // 2
    steps = blocks // GROUP
    return pl.pallas_call(
        gain_kernel,
        out_shape=jax.ShapeDtypeStruct((blocks, NNZ, 2 * BLK), bf16),
        grid_spec=pltpu.PrefetchScalarGridSpec(
            num_scalar_prefetch=1,
            grid=(steps,),
            in_specs=[
                pl.BlockSpec((GROUP * NNZ, MP), lambda i, c: (i, 0)),
                pl.BlockSpec((M, MP), lambda i, c: (0, 0)),
                pl.BlockSpec((SYS - 1, M, MP), lambda i, c: (0, 0, 0)),
                pl.BlockSpec((SYS - 1, M, MP), lambda i, c: (0, 0, 0)),
                pl.BlockSpec((2, M, GROUP * BLK), lambda i, c: (0, 0, c[0] * steps + i)),
            ],
            out_specs=pl.BlockSpec((GROUP, NNZ, 2 * BLK), lambda i, c: (i, 0, 0)),
            scratch_shapes=[
                pltpu.VMEM((MAPS, 3 * MP, MP), bf16),
                pltpu.VMEM((GROUP, MAPS * NNZ, MP), bf16),
            ],
        ),
        compiler_params=limit,
        cost_estimate=pl.CostEstimate(flops=20_000_000_000, bytes_accessed=8_000_000, transcendentals=0),
        name="gains",
    )(core, psel, full, mine, theirs, params)


def update(half, isel, screened, params, so_far=None):
    blocks = params.shape[2] // BLK // 2
    steps = blocks // GROUP
    cells = pl.BlockSpec((2, M, GROUP * BLK), lambda i, c: (0, 0, c[0] * steps + i))
    in_specs = [
        pl.BlockSpec((GROUP * NNZ, MP), lambda i, c: (c[0] * steps + i, 0)),
        pl.BlockSpec((GROUP, NNZ, 2 * BLK), lambda i, c: (i, 0, 0)),
        cells,
    ]
    operands = (half, isel, screened, params)
    if so_far is not None:
        in_specs.append(pl.BlockSpec(memory_space=pl.ANY))
        operands = operands + (so_far,)
    return pl.pallas_call(
        change_kernel,
        out_shape=jax.ShapeDtypeStruct(params.shape, f32),
        grid_spec=pltpu.PrefetchScalarGridSpec(
            num_scalar_prefetch=1, grid=(steps,), in_specs=in_specs, out_specs=cells
        ),
        input_output_aliases={} if so_far is None else {4: 0},
        compiler_params=limit,
        cost_estimate=pl.CostEstimate(flops=5_000_000_000, bytes_accessed=10_000_000, transcendentals=0),
        name="change",
    )(*operands)


def on_device(params, predicted, perturbation, observed, obs_sd, members, block_map):
    boot = lax.axis_index("boot")
    core = lax.rem(boot, 2)
    core_arg = core.reshape(1).astype(jnp.int32)
    slabs = lax.axis_size("slab")
    pair = [(i, i ^ 1) for i in range(4)]
    far = [(i, i ^ 2) for i in range(4)]

    def exchange(whole):
        own = lax.all_to_all(whole, "slab", 0, 0)
        return own, lax.ppermute(own, "boot", pair)

    far_members = lax.ppermute(members, "boot", far)
    whole, innov_whole = pack(core_arg, predicted, perturbation, observed, obs_sd, slabs)
    whole, far_members = lax.optimization_barrier((whole, far_members))
    every = jnp.arange(M, dtype=jnp.int32)[None]
    lists = jnp.concatenate([every, members, far_members], axis=0)
    lists = jnp.pad(lists, ((0, 16 - SYS), (0, MP - M)), constant_values=-1)

    own, other = exchange(whole)
    innov_whole, other = lax.optimization_barrier((innov_whole, other))
    iown, iother = exchange(innov_whole)

    full, mine, psel = make_maps(core_arg, block_map, own, other, lists)
    late_map, mine = lax.optimization_barrier((block_map, mine))
    theirs = lax.ppermute(mine, "boot", pair)
    isel = select(core_arg, late_map, iown, iother)
    screened = make_screened(core_arg, psel, full, mine, theirs, params)
    screened_other = lax.ppermute(screened, "boot", pair)
    partial_out = update(core_arg, isel, screened, params)
    return update(1 - core_arg, isel, screened_other, params, partial_out)


def solution(mesh):
    return jax.shard_map(
        on_device,
        mesh=mesh,
        in_specs=(
            P(None, None, "slab"),
            P(None, "slab"),
            P(None, "slab"),
            P("slab"),
            P("slab"),
            P("boot", None),
            P("slab", None),
        ),
        out_specs=P(None, None, "slab"),
        check_vma=False,
    )
```

```python
from functools import partial
import math

import jax
import jax.numpy as jnp
from jax import lax
from jax.experimental import pallas as pl
from jax.experimental.pallas import tpu as pltpu
from jax.sharding import PartitionSpec as P

M = 200
NB = 16
BLK = 128
NNZ = 64
MP = 256
ROWS = 208
PIV = 40
SYS = 9
PACK = 3
MAPS = 17
GROUP = 8

screen_floor = 1e-05
f32 = jnp.float32
bf16 = jnp.bfloat16


def iota(shape, dim):
    return lax.broadcasted_iota(jnp.int32, shape, dim)


def split3(x):
    hi = x.astype(bf16).astype(f32)
    rest = x - hi
    mid = rest.astype(bf16).astype(f32)
    return hi, mid, rest - mid


def lhs6(c):
    hi, mid, lo = split3(c)
    left = hi + pltpu.roll(hi, PIV, 1) + pltpu.roll(hi, 2 * PIV, 1)
    right = mid + pltpu.roll(mid, PIV, 1) + pltpu.roll(lo, 2 * PIV, 1)
    return jnp.concatenate([left, right], axis=1).astype(bf16)


def rhs6(r):
    hi, mid, lo = split3(r)
    pad = jnp.zeros((BLK - 3 * PIV, MP), f32)
    return jnp.concatenate([hi, mid, lo, pad, hi, mid, hi, pad], axis=0).astype(bf16)


def dot(a, b):
    return jnp.dot(a, b, preferred_element_type=f32)


def scaling(listed):
    lane = iota((M, MP), 1)
    if listed is None:
        down = jnp.ones((M, 1), f32)
        across = jnp.where(lane[:1] < M, 1.0, 0.0)
    else:
        down = jnp.sqrt(jnp.sum(jnp.where(iota((M, M), 0) == listed, 1.0, 0.0), axis=1, keepdims=True))
        across = jnp.sum(jnp.where(iota((M, MP), 0) == lane, down, 0.0), axis=0, keepdims=True)
    root = 1.0 / math.sqrt(M)
    return down * (1.0 / (M - 1)) * across, down * root, across * root


def pack_kernel(core_ref, pred_ref, pert_ref, obs_ref, sd_ref, out_ref):
    sd = sd_ref[...].astype(f32)
    ens = pred_ref[...].astype(f32)
    innov = obs_ref[...].astype(f32) + sd * pert_ref[...].astype(f32) - ens
    rows = jnp.where(core_ref[0] == 0, ens, innov)
    tail = jnp.concatenate([sd, jnp.zeros((ROWS - M - 1, BLK), f32)], axis=0)
    part = jnp.concatenate([rows, tail], axis=0).astype(bf16)
    for i in range(out_ref.shape[0]):
        out_ref[i] = part


def chunk_rows(keep_own, own_ref, other_ref, i):
    rows = jnp.where(keep_own, own_ref[i].astype(f32), other_ref[i].astype(f32))
    high = jnp.concatenate([rows[BLK:], jnp.zeros((MP - ROWS, BLK), f32)], axis=0)
    return rows, rows[:BLK], high


def fill_table(t_ref, i, low, high):
    base = pl.multiple_of(i * (2 * BLK), 8)
    t_ref[pl.ds(base, BLK, stride=2), :] = low
    t_ref[pl.ds(base + 1, BLK, stride=2), :] = high


def pick(t_ref, map_ref, k, line_ref):
    for j in range(NNZ):
        line_ref[2 * j:2 * j + 2, :] = t_ref[pl.ds(2 * map_ref[k, j], 2), :]
    both = [line_ref[pl.ds(n, NNZ, stride=2), :] for n in range(2)]
    return jnp.concatenate(both, axis=1).astype(bf16)


def map_kernel(core_ref, map_ref, own_ref, other_ref, near_ref, far_ref, full_ref, res_ref, psel_ref, ens_ref, parts_ref, table_ref, line_ref, scale_ref, *sys_refs):
    core = core_ref[0]
    near = near_ref.shape[0]
    blocks = map_ref.shape[0]

    def chunk(i, carry):
        rows, low, high = chunk_rows(core == 0, own_ref, other_ref, i)
        sd = rows[M:M + 1]
        at = pl.ds(pl.multiple_of(i * BLK, BLK), BLK)
        for n, part in enumerate(split3(rows * (1.0 / (sd * sd)))):
            parts_ref[n, :, at] = part.astype(bf16)
        low, high = low.T, high.T
        ens_ref[at, :] = jnp.concatenate([low, high], axis=1).astype(bf16)
        fill_table(table_ref, i, low, high)
        return carry

    lax.fori_loop(0, own_ref.shape[0], chunk, 0, unroll=4)

    gram = 0.0
    for n in (2, 1, 0):
        gram = gram + dot(parts_ref[n], ens_ref[...])
    gram = gram[:M]

    def pick_own(k, carry):
        psel_ref[pl.ds(pl.multiple_of(k * NNZ, NNZ), NNZ), :] = pick(
            table_ref, map_ref, core * (blocks // 2) + k, line_ref
        )
        return carry

    lax.fori_loop(0, blocks // 2, pick_own, 0)

    row = iota((M, MP), 0)
    lane = iota((M, MP), 1)
    for s in range(SYS):
        listed = None
        if s:
            listed = near_ref[s - 1:s, :] if s <= near else far_ref[s - 1 - near:s - near, :]
        scale, ud, ua = scaling(listed)
        scale_ref[s] = scale
        h = gram * scale
        hu = jnp.sum(h * ua, axis=1, keepdims=True)
        uh = jnp.sum(h * ud, axis=0, keepdims=True)
        uhu = jnp.sum(hu * ud, axis=0, keepdims=True)
        h = h - ud * (uh - 0.5 * uhu * ua) - (hu - 0.5 * uhu * ud) * ua
        sys_refs[s][...] = h + jnp.where(row == lane, 1.0, 0.0)

    prow = iota((PIV, MP), 0)
    plane = iota((PIV, MP), 1)
    dlane = iota((PIV, BLK), 1)
    trow = iota((8, BLK), 0)
    tlane = iota((8, BLK), 1)
    first = jnp.minimum(tlane // PIV, PACK - 1) * PIV
    inner = tlane - first

    def panel_step(kp, carry):
        k0 = kp * PIV
        at = pl.ds(pl.multiple_of(k0, 8), PIV)
        packs = []
        for g in range(SYS // PACK):
            pack = jnp.zeros((PIV, BLK), f32)
            for q in range(PACK):
                moved = pltpu.roll(sys_refs[PACK * g + q][at, :], lax.rem(MP - k0 + q * PIV, MP), 1)[:, :BLK]
                pack = jnp.where((dlane >= q * PIV) & (dlane < (q + 1) * PIV), moved, pack)
            packs.append(pack)
        starts = packs
        tiles = [[pack[8 * i:8 * i + 8] for i in range(PIV // 8)] for pack in packs]
        for j in range(PIV // 8):
            cols = [
                [[jnp.take_along_axis(tile, first + 8 * j + u, axis=1) for u in range(8)] for tile in group]
                for group in tiles
            ]
            for u in range(8):
                at_lane = inner == 8 * j + u
                for group, col in zip(tiles, cols):
                    lead = col[j][u]
                    scale = 1.0 / lead[u:u + 1]
                    t = group[j]
                    line = jnp.where(at_lane[:1], 1.0, t[u:u + 1]) * scale
                    group[j] = jnp.where(trow == u, line, jnp.where(at_lane, 0.0, t) - lead * line)
                    for v in range(u + 1, 8):
                        c = col[j][v]
                        line = c[u:u + 1] * scale
                        col[j][v] = jnp.where(trow == u, line, c - lead * line)
            done = (inner >= 8 * j) & (inner < 8 * j + 8)
            for group, col in zip(tiles, cols):
                for i in range(PIV // 8):
                    if i != j:
                        tile = jnp.where(done, 0.0, group[i])
                        for u in range(8):
                            tile = tile - col[i][u] * group[j][u:u + 1]
                        group[i] = tile
        packs = [jnp.concatenate(group, axis=0) for group in tiles]
        inside = (lane >= k0) & (lane < k0 + PIV)
        pad = jnp.zeros((BLK - 3 * PIV, MP), f32)
        inverses, blocks_, panels, wanted, lines = [], [], [], [], []
        for s in range(SYS):
            back = (BLK - (s % PACK) * PIV) % BLK
            for kept, source in ((inverses, packs), (blocks_, starts)):
                moved = source[s // PACK]
                if back:
                    moved = pltpu.roll(moved, back, 1)
                kept.append(lhs6(jnp.where(dlane < PIV, moved, 0.0)))
            panels.append(sys_refs[s][at, :])
            wanted.append(jnp.where(plane == prow + k0, -1.0, jnp.where(inside[:PIV], 0.0, panels[s])))
        for s in range(SYS):
            lines.append(dot(inverses[s], rhs6(wanted[s])))
        for s in range(SYS):
            lines[s] = lines[s] + dot(inverses[s], rhs6(wanted[s] - dot(blocks_[s], rhs6(lines[s]))))
        for s in range(SYS):
            hi, mid, lo = split3(panels[s])
            left = jnp.concatenate([hi, hi, hi, pad, mid, mid, lo, pad], axis=0).astype(bf16)
            change = lax.dot_general(left, rhs6(lines[s]), (((0,), (0,)), ((), ())), preferred_element_type=f32)
            sys_refs[s][...] = jnp.where(inside, 0.0, sys_refs[s][...]) - change[:M]
            sys_refs[s][at, :] = lines[s]
        return carry

    lax.fori_loop(0, M // PIV, panel_step, 0)

    for s in range(SYS):
        scale = scale_ref[s]
        value = (-sys_refs[s][...] - scale * ((M - 1) / M)) * scale
        if s == 0:
            full_ref[...] = value
        else:
            res_ref[s - 1] = value


def select_kernel(core_ref, map_ref, own_ref, other_ref, isel_ref, table_ref, line_ref):
    core = core_ref[0]

    def chunk(i, carry):
        _, low, high = chunk_rows(core == 1, own_ref, other_ref, i)
        fill_table(table_ref, i, low.T, high.T)
        return carry

    lax.fori_loop(0, own_ref.shape[0], chunk, 0, unroll=4)

    def pick_all(k, carry):
        isel_ref[pl.ds(pl.multiple_of(k * NNZ, NNZ), NNZ), :] = pick(table_ref, map_ref, k, line_ref)
        return carry

    lax.fori_loop(0, map_ref.shape[0], pick_all, 0)


def gain_kernel(core_ref, psel_ref, full_ref, mine_ref, theirs_ref, params_ref, out_ref, maps_ref, cols_ref):
    @pl.when(pl.program_id(0) == 0)
    def _():
        def place(r, value):
            pad = jnp.zeros((MP - M, MP), f32)
            for n, part in enumerate(split3(value)):
                maps_ref[r, n * MP:(n + 1) * MP, :] = jnp.concatenate([part, pad], axis=0).astype(bf16)

        place(0, full_ref[...])

        def place_both(r, carry):
            place(1 + r, mine_ref[r])
            place(SYS + r, theirs_ref[r])
            return carry

        lax.fori_loop(0, SYS - 1, place_both, 0)

    x = psel_ref[...]
    sd = x[:, M:M + 1].astype(f32)
    weight = 1.0 / (sd * sd)

    x3 = jnp.concatenate([x, x, x], axis=1)

    def column(r, carry):
        total = dot(x3, maps_ref[r])
        total = (total * weight).astype(bf16)
        for g in range(GROUP):
            cols_ref[g, pl.ds(pl.multiple_of(r * NNZ, NNZ), NNZ), :] = total[g * NNZ:(g + 1) * NNZ]
        return carry

    lax.fori_loop(0, MAPS, column, 0, unroll=True)

    def gains(g, carry):
        at = pl.ds(pl.multiple_of(g * BLK, BLK), BLK)
        cells = jnp.concatenate([params_ref[0, :, at], params_ref[1, :, at]], axis=1)
        every = dot(cols_ref[g][:, :M], cells)
        full = every[:NNZ]
        spread = jnp.zeros_like(full)
        for r in range(1, MAPS):
            off = every[r * NNZ:(r + 1) * NNZ] - full
            spread = spread + off * off
        squared = full * full
        out_ref[g] = (squared / (squared + spread * (1.0 / NB) + screen_floor) * full).astype(bf16)
        return carry

    lax.fori_loop(0, GROUP, gains, 0, unroll=4)


def change_kernel(half_ref, isel_ref, screened_ref, params_ref, *rest):
    out_ref = rest[-1]
    for g in range(GROUP):
        change = lax.dot_general(
            isel_ref[g * NNZ:(g + 1) * NNZ, :], screened_ref[g], (((0,), (0,)), ((), ())), preferred_element_type=f32
        )
        at = slice(g * BLK, (g + 1) * BLK)
        for p in range(2):
            out_ref[p, :, at] = params_ref[p, :, at].astype(f32) + change[:M, p * BLK:(p + 1) * BLK]


vmem = pl.BlockSpec(memory_space=pltpu.VMEM)
smem = pl.BlockSpec(memory_space=pltpu.SMEM)
limit = pltpu.CompilerParams(vmem_limit_bytes=56 * 1024 * 1024)


def pack(core, predicted, perturbation, observed, obs_sd, slabs):
    whole = jax.ShapeDtypeStruct((slabs, ROWS, BLK), bf16)
    return pl.pallas_call(
        pack_kernel,
        out_shape=whole,
        in_specs=[smem, vmem, vmem, vmem, vmem],
        out_specs=vmem,
        compiler_params=limit,
        name="pack",
    )(core, predicted, perturbation, observed[None], obs_sd[None])


def make_maps(core, block_map, own, other, near, far):
    blocks = block_map.shape[0]
    data = own.shape[0] * BLK
    return pl.pallas_call(
        map_kernel,
        out_shape=(
            jax.ShapeDtypeStruct((M, MP), f32),
            jax.ShapeDtypeStruct((SYS - 1, M, MP), f32),
            jax.ShapeDtypeStruct((blocks // 2 * NNZ, MP), bf16),
        ),
        in_specs=[smem, smem, vmem, vmem, vmem, vmem],
        out_specs=(vmem, vmem, vmem),
        scratch_shapes=[
            pltpu.VMEM((data, MP), bf16),
            pltpu.VMEM((3, ROWS, data), bf16),
            pltpu.VMEM((2 * data, BLK), f32),
            pltpu.VMEM((2 * NNZ, BLK), f32),
            pltpu.VMEM((SYS, M, MP), f32),
        ] + [pltpu.VMEM((M, MP), f32)] * SYS,
        compiler_params=limit,
        cost_estimate=pl.CostEstimate(flops=20_000_000_000, bytes_accessed=8_000_000, transcendentals=0),
        name="maps",
    )(core, block_map, own, other, near, far)


def select(core, block_map, own, other):
    blocks = block_map.shape[0]
    data = own.shape[0] * BLK
    return pl.pallas_call(
        select_kernel,
        out_shape=jax.ShapeDtypeStruct((blocks * NNZ, MP), bf16),
        in_specs=[smem, smem, vmem, vmem],
        out_specs=vmem,
        scratch_shapes=[pltpu.VMEM((2 * data, BLK), f32), pltpu.VMEM((2 * NNZ, BLK), f32)],
        compiler_params=limit,
        cost_estimate=pl.CostEstimate(flops=10_000_000_000, bytes_accessed=8_000_000, transcendentals=0),
        name="select",
    )(core, block_map, own, other)


def make_screened(core, psel, full, mine, theirs, params):
    blocks = params.shape[2] // BLK // 2
    steps = blocks // GROUP
    return pl.pallas_call(
        gain_kernel,
        out_shape=jax.ShapeDtypeStruct((blocks, NNZ, 2 * BLK), bf16),
        grid_spec=pltpu.PrefetchScalarGridSpec(
            num_scalar_prefetch=1,
            grid=(steps,),
            in_specs=[
                pl.BlockSpec((GROUP * NNZ, MP), lambda i, c: (i, 0)),
                pl.BlockSpec((M, MP), lambda i, c: (0, 0)),
                pl.BlockSpec((SYS - 1, M, MP), lambda i, c: (0, 0, 0)),
                pl.BlockSpec((SYS - 1, M, MP), lambda i, c: (0, 0, 0)),
                pl.BlockSpec((2, M, GROUP * BLK), lambda i, c: (0, 0, c[0] * steps + i)),
            ],
            out_specs=pl.BlockSpec((GROUP, NNZ, 2 * BLK), lambda i, c: (i, 0, 0)),
            scratch_shapes=[
                pltpu.VMEM((MAPS, 3 * MP, MP), bf16),
                pltpu.VMEM((GROUP, MAPS * NNZ, MP), bf16),
            ],
        ),
        compiler_params=limit,
        cost_estimate=pl.CostEstimate(flops=20_000_000_000, bytes_accessed=8_000_000, transcendentals=0),
        name="gains",
    )(core, psel, full, mine, theirs, params)


def update(half, isel, screened, params, so_far=None):
    blocks = params.shape[2] // BLK // 2
    steps = blocks // GROUP
    cells = pl.BlockSpec((2, M, GROUP * BLK), lambda i, c: (0, 0, c[0] * steps + i))
    in_specs = [
        pl.BlockSpec((GROUP * NNZ, MP), lambda i, c: (c[0] * steps + i, 0)),
        pl.BlockSpec((GROUP, NNZ, 2 * BLK), lambda i, c: (i, 0, 0)),
        cells,
    ]
    operands = (half, isel, screened, params)
    if so_far is not None:
        in_specs.append(pl.BlockSpec(memory_space=pl.ANY))
        operands = operands + (so_far,)
    return pl.pallas_call(
        change_kernel,
        out_shape=jax.ShapeDtypeStruct(params.shape, f32),
        grid_spec=pltpu.PrefetchScalarGridSpec(
            num_scalar_prefetch=1, grid=(steps,), in_specs=in_specs, out_specs=cells
        ),
        input_output_aliases={} if so_far is None else {4: 0},
        compiler_params=limit,
        cost_estimate=pl.CostEstimate(flops=5_000_000_000, bytes_accessed=10_000_000, transcendentals=0),
        name="change",
    )(*operands)


def on_device(params, predicted, perturbation, observed, obs_sd, members, block_map):
    boot = lax.axis_index("boot")
    core = lax.rem(boot, 2)
    core_arg = core.reshape(1).astype(jnp.int32)
    slabs = lax.axis_size("slab")
    pair = [(i, i ^ 1) for i in range(4)]
    far = [(i, i ^ 2) for i in range(4)]

    far_members = lax.ppermute(members, "boot", far)
    whole = pack(core_arg, predicted, perturbation, observed, obs_sd, slabs)
    whole, far_members = lax.optimization_barrier((whole, far_members))
    own = lax.all_to_all(whole, "slab", 0, 0)
    other = lax.ppermute(own, "boot", pair)

    full, mine, psel = make_maps(core_arg, block_map, own, other, members, far_members)
    late_map, mine = lax.optimization_barrier((block_map, mine))
    theirs = lax.ppermute(mine, "boot", pair)
    isel = select(core_arg, late_map, own, other)
    isel, psel = lax.optimization_barrier((isel, psel))
    screened = make_screened(core_arg, psel, full, mine, theirs, params)
    screened_other = lax.ppermute(screened, "boot", pair)
    partial_out = update(core_arg, isel, screened, params)
    return update(1 - core_arg, isel, screened_other, params, partial_out)


def solution(mesh):
    return jax.shard_map(
        on_device,
        mesh=mesh,
        in_specs=(
            P(None, None, "slab"),
            P(None, "slab"),
            P(None, "slab"),
            P("slab"),
            P("slab"),
            P("boot", None),
            P("slab", None),
        ),
        out_specs=P(None, None, "slab"),
        check_vma=False,
    )
```

```python
from functools import partial
import math

import jax
import jax.numpy as jnp
from jax import lax
from jax.experimental import pallas as pl
from jax.experimental.pallas import tpu as pltpu
from jax.sharding import PartitionSpec as P

M = 200
NB = 16
BLK = 128
NNZ = 64
MP = 256
ROWS = 208
PIV = 40
SYS = 9
PARTS = 4
PACK = 3
MAPS = 17
GROUP = 8

screen_floor = 1e-05
f32 = jnp.float32
bf16 = jnp.bfloat16


def iota(shape, dim):
    return lax.broadcasted_iota(jnp.int32, shape, dim)


def split3(x):
    hi = x.astype(bf16).astype(f32)
    rest = x - hi
    mid = rest.astype(bf16).astype(f32)
    return hi, mid, rest - mid


def lhs6(c):
    hi, mid, lo = split3(c)
    left = hi + pltpu.roll(hi, PIV, 1) + pltpu.roll(hi, 2 * PIV, 1)
    right = mid + pltpu.roll(mid, PIV, 1) + pltpu.roll(lo, 2 * PIV, 1)
    return jnp.concatenate([left, right], axis=1).astype(bf16)


def rhs6(r):
    hi, mid, lo = split3(r)
    pad = jnp.zeros((BLK - 3 * PIV, MP), f32)
    return jnp.concatenate([hi, mid, lo, pad, hi, mid, hi, pad], axis=0).astype(bf16)


def dot(a, b):
    return jnp.dot(a, b, preferred_element_type=f32)


def scaling(listed):
    lane = iota((M, MP), 1)
    if listed is None:
        down = jnp.ones((M, 1), f32)
        across = jnp.where(lane[:1] < M, 1.0, 0.0)
    else:
        down = jnp.sqrt(jnp.sum(jnp.where(iota((M, M), 0) == listed, 1.0, 0.0), axis=1, keepdims=True))
        across = jnp.sum(jnp.where(iota((M, MP), 0) == lane, down, 0.0), axis=0, keepdims=True)
    root = 1.0 / math.sqrt(M)
    return down * (1.0 / (M - 1)) * across, down * root, across * root


def pack_kernel(core_ref, pred_ref, pert_ref, obs_ref, sd_ref, out_ref):
    sd = sd_ref[...].astype(f32)
    ens = pred_ref[...].astype(f32)
    innov = obs_ref[...].astype(f32) + sd * pert_ref[...].astype(f32) - ens
    rows = jnp.where(core_ref[0] == 0, ens, innov)
    tail = jnp.concatenate([sd, jnp.zeros((ROWS - M - 1, BLK), f32)], axis=0)
    part = jnp.concatenate([rows, tail], axis=0).astype(bf16)
    for i in range(out_ref.shape[0]):
        out_ref[i] = part


def gathered(first, own_ref, other_ref, rows_ref, map_ref, index_ref, sems):
    index_copy = pltpu.make_async_copy(map_ref, index_ref, sems.at[PARTS])
    step = rows_ref.shape[0] // PARTS

    def copy(ref, n):
        at = pl.ds(n * step, step)
        return pltpu.make_async_copy(ref.at[at], rows_ref.at[at], sems.at[n])

    @pl.when(first)
    def _():
        for n in range(PARTS):
            copy(own_ref, n).start()

    @pl.when(jnp.logical_not(first))
    def _():
        for n in range(PARTS):
            copy(other_ref, n).start()

    index_copy.start()
    return lambda n: index_copy.wait() if n == PARTS else copy(own_ref, n).wait()


def chunk_rows(rows_ref, i):
    rows = rows_ref[i].astype(f32)
    high = jnp.concatenate([rows[BLK:], jnp.zeros((MP - ROWS, BLK), f32)], axis=0)
    return rows, rows[:BLK], high


def by_parts(count, wait, chunk):
    step = count // PARTS
    for n in range(PARTS):
        wait(n)
        lax.fori_loop(n * step, (n + 1) * step, chunk, 0, unroll=4)


def fill_table(t_ref, i, low, high):
    base = pl.multiple_of(i * (2 * BLK), 8)
    t_ref[pl.ds(base, BLK, stride=2), :] = low
    t_ref[pl.ds(base + 1, BLK, stride=2), :] = high


def pick(t_ref, map_ref, k, line_ref):
    for j in range(NNZ):
        line_ref[2 * j:2 * j + 2, :] = t_ref[pl.ds(2 * map_ref[k, j], 2), :]
    both = [line_ref[pl.ds(n, NNZ, stride=2), :] for n in range(2)]
    return jnp.concatenate(both, axis=1).astype(bf16)


def along(tile, u):
    return jnp.broadcast_to(tile[u:u + 1], tile.shape)


def inverse_of(x):
    guess = pl.reciprocal(x, approx=True)
    guess = guess * (2.0 - x * guess)
    return guess * (2.0 - x * guess)


def map_kernel(core_ref, map_ref, own_ref, other_ref, near_ref, far_ref, full_ref, res_ref, psel_ref, ens_ref, parts_ref, table_ref, line_ref, scale_ref, rows_ref, index_ref, sems, picked_ref, maps_ref, out_sems, *sys_refs):
    core = core_ref[0]
    near = near_ref.shape[0]
    wait = gathered(core == 0, own_ref, other_ref, rows_ref, map_ref, index_ref, sems)
    blocks = map_ref.shape[0]

    def chunk(i, carry):
        rows, low, high = chunk_rows(rows_ref, i)
        sd = rows[M:M + 1]
        at = pl.ds(pl.multiple_of(i * BLK, BLK), BLK)
        for n, part in enumerate(split3(rows * (1.0 / (sd * sd)))):
            parts_ref[n, :, at] = part.astype(bf16)
        low, high = low.T, high.T
        ens_ref[at, :] = jnp.concatenate([low, high], axis=1).astype(bf16)
        fill_table(table_ref, i, low, high)
        return carry

    by_parts(rows_ref.shape[0], wait, chunk)

    gram = 0.0
    for n in (2, 1, 0):
        gram = gram + dot(parts_ref[n], ens_ref[...])
    gram = gram[:M]

    def pick_own(k, carry):
        picked_ref[pl.ds(pl.multiple_of(k * NNZ, NNZ), NNZ), :] = pick(
            table_ref, index_ref, core * (blocks // 2) + k, line_ref
        )
        return carry

    wait(PARTS)
    lax.fori_loop(0, blocks // 2, pick_own, 0)
    outs = [pltpu.make_async_copy(picked_ref, psel_ref, out_sems.at[SYS])]
    outs[0].start()

    row = iota((M, MP), 0)
    lane = iota((M, MP), 1)
    for s in range(SYS):
        listed = None
        if s:
            listed = near_ref[s - 1:s, :] if s <= near else far_ref[s - 1 - near:s - near, :]
        scale, ud, ua = scaling(listed)
        scale_ref[s] = scale
        h = gram * scale
        hu = jnp.sum(h * ua, axis=1, keepdims=True)
        uh = jnp.sum(h * ud, axis=0, keepdims=True)
        uhu = jnp.sum(hu * ud, axis=0, keepdims=True)
        h = h - ud * (uh - 0.5 * uhu * ua) - (hu - 0.5 * uhu * ud) * ua
        sys_refs[s][...] = h + jnp.where(row == lane, 1.0, 0.0)

    prow = iota((PIV, MP), 0)
    plane = iota((PIV, MP), 1)
    dlane = iota((PIV, BLK), 1)
    trow = iota((8, BLK), 0)
    tlane = iota((8, BLK), 1)
    first = jnp.minimum(tlane // PIV, PACK - 1) * PIV
    inner = tlane - first

    def panel_step(kp, carry):
        k0 = kp * PIV
        at = pl.ds(pl.multiple_of(k0, 8), PIV)
        packs = []
        for g in range(SYS // PACK):
            pack = jnp.zeros((PIV, BLK), f32)
            for q in range(PACK):
                moved = pltpu.roll(sys_refs[PACK * g + q][at, :], lax.rem(MP - k0 + q * PIV, MP), 1)[:, :BLK]
                pack = jnp.where((dlane >= q * PIV) & (dlane < (q + 1) * PIV), moved, pack)
            packs.append(pack)
        starts = packs
        tiles = [[pack[8 * i:8 * i + 8] for i in range(PIV // 8)] for pack in packs]
        for j in range(PIV // 8):
            cols = [
                [[jnp.take_along_axis(tile, first + 8 * j + u, axis=1) for u in range(8)] for tile in group]
                for group in tiles
            ]
            for u in range(8):
                at_lane = inner == 8 * j + u
                for group, col in zip(tiles, cols):
                    lead = col[j][u]
                    scale = inverse_of(along(lead, u))
                    t = group[j]
                    line = jnp.where(at_lane, 1.0, along(t, u)) * scale
                    group[j] = jnp.where(trow == u, line, jnp.where(at_lane, 0.0, t) - lead * line)
                    for v in range(u + 1, 8):
                        c = col[j][v]
                        line = along(c, u) * scale
                        col[j][v] = jnp.where(trow == u, line, c - lead * line)
            done = (inner >= 8 * j) & (inner < 8 * j + 8)
            for group, col in zip(tiles, cols):
                for i in range(PIV // 8):
                    if i != j:
                        tile = jnp.where(done, 0.0, group[i])
                        for u in range(8):
                            tile = tile - col[i][u] * group[j][u:u + 1]
                        group[i] = tile
        packs = [jnp.concatenate(group, axis=0) for group in tiles]
        inside = (lane >= k0) & (lane < k0 + PIV)
        pad = jnp.zeros((BLK - 3 * PIV, MP), f32)
        inverses, blocks_, panels, wanted, lines = [], [], [], [], []
        for s in range(SYS):
            back = (BLK - (s % PACK) * PIV) % BLK
            for kept, source in ((inverses, packs), (blocks_, starts)):
                moved = source[s // PACK]
                if back:
                    moved = pltpu.roll(moved, back, 1)
                kept.append(lhs6(jnp.where(dlane < PIV, moved, 0.0)))
            panels.append(sys_refs[s][at, :])
            wanted.append(jnp.where(plane == prow + k0, -1.0, jnp.where(inside[:PIV], 0.0, panels[s])))
        for s in range(SYS):
            lines.append(dot(inverses[s], rhs6(wanted[s])))
        for s in range(SYS):
            lines[s] = lines[s] + dot(inverses[s], rhs6(wanted[s] - dot(blocks_[s], rhs6(lines[s]))))
        for s in range(SYS):
            hi, mid, lo = split3(panels[s])
            left = jnp.concatenate([hi, hi, hi, pad, mid, mid, lo, pad], axis=0).astype(bf16)
            change = lax.dot_general(left, rhs6(lines[s]), (((0,), (0,)), ((), ())), preferred_element_type=f32)
            sys_refs[s][...] = jnp.where(inside, 0.0, sys_refs[s][...]) - change[:M]
            sys_refs[s][at, :] = lines[s]
        return carry

    lax.fori_loop(0, M // PIV, panel_step, 0)

    for s in range(SYS):
        scale = scale_ref[s]
        value = (-sys_refs[s][...] - scale * ((M - 1) / M)) * scale
        value = jnp.concatenate([value, jnp.zeros((MP - M, MP), f32)], axis=0)
        hi = value.astype(bf16)
        maps_ref[s] = jnp.concatenate([hi, (value - hi.astype(f32)).astype(bf16)], axis=0)
        outs.append(pltpu.make_async_copy(maps_ref.at[s], res_ref.at[s - 1] if s else full_ref, out_sems.at[s]))
        outs[-1].start()
    for copy in outs:
        copy.wait()


def select_kernel(half_ref, core_ref, map_ref, own_ref, other_ref, isel_ref, table_ref, line_ref, rows_ref, index_ref, sems):
    wait = gathered(core_ref[0] == 1, own_ref, other_ref, rows_ref, map_ref, index_ref, sems)
    blocks = map_ref.shape[0] // 2

    def chunk(i, carry):
        _, low, high = chunk_rows(rows_ref, i)
        fill_table(table_ref, i, low.T, high.T)
        return carry

    by_parts(rows_ref.shape[0], wait, chunk)
    wait(PARTS)

    def pick_pair(k, carry):
        for n in range(2):
            for j in range(NNZ):
                at = 2 * (n * NNZ + j)
                line_ref[at:at + 2, :] = table_ref[pl.ds(2 * index_ref[half_ref[0] * blocks + 2 * k + n, j], 2), :]
        at = pl.ds(pl.multiple_of(k * BLK, BLK), BLK)
        for n in range(2):
            isel_ref[n * BLK:(n + 1) * BLK, at] = line_ref[pl.ds(n, BLK, stride=2), :].T.astype(bf16)
        return carry

    lax.fori_loop(0, blocks // 2, pick_pair, 0, unroll=2)


def change_block(isel_ref, screened_ref, cells_ref, new_ref, g):
    picked = isel_ref[:ROWS, g // 2 * BLK:(g // 2 + 1) * BLK]
    none = jnp.zeros((NNZ, 2 * BLK), bf16)
    rows = [none, screened_ref[g]] if g % 2 else [screened_ref[g], none]
    change = dot(picked, jnp.concatenate(rows, axis=0))
    at = slice(g * BLK, (g + 1) * BLK)
    for p in range(2):
        new_ref[p, :, at] = cells_ref[p, :, at].astype(f32) + change[:M, p * BLK:(p + 1) * BLK]


def gain_kernel(core_ref, psel_ref, isel_ref, full_ref, mine_ref, theirs_ref, params_ref, screened_ref, out_ref, cols_ref, maps_ref, sems):
    def bring(r):
        if r == 0:
            ref = full_ref
        elif r < SYS:
            ref = mine_ref.at[r - 1]
        else:
            ref = theirs_ref.at[r - SYS]
        return pltpu.make_async_copy(ref, maps_ref.at[r], sems.at[r])

    @pl.when(pl.program_id(0) == 0)
    def _():
        for r in range(MAPS):
            bring(r).start()
        for r in range(MAPS):
            bring(r).wait()

    x = psel_ref[...]
    sd = x[:, M:M + 1].astype(f32)
    weight = 1.0 / (sd * sd)
    x = jnp.concatenate([x, x], axis=1)

    for r in range(MAPS):
        total = (dot(x, maps_ref[r]) * weight).astype(bf16)
        for g in range(GROUP):
            cols_ref[g, r * NNZ:(r + 1) * NNZ, :] = total[g * NNZ:(g + 1) * NNZ]

    def gains(g, carry):
        at = pl.ds(pl.multiple_of(g * BLK, BLK), BLK)
        cells = jnp.concatenate([params_ref[0, :, at], params_ref[1, :, at]], axis=1)
        every = dot(cols_ref[g][:, :M], cells)
        full = every[:NNZ]
        spread = jnp.zeros_like(full)
        for r in range(1, MAPS):
            off = every[r * NNZ:(r + 1) * NNZ] - full
            spread = spread + off * off
        squared = full * full
        screened_ref[g] = (squared / (squared + spread * (1.0 / NB) + screen_floor) * full).astype(bf16)
        return carry

    lax.fori_loop(0, GROUP, gains, 0, unroll=GROUP)
    for g in range(GROUP):
        change_block(isel_ref, screened_ref, params_ref, out_ref, g)


def change_kernel(half_ref, isel_ref, screened_ref, params_ref, so_far_ref, out_ref, cells_ref, new_ref, in_sems, out_sems):
    blocks = screened_ref.shape[0]
    width = GROUP * BLK
    steps = blocks // GROUP
    start = pl.multiple_of(half_ref[0] * (blocks * BLK), BLK)

    def here(n):
        return pl.ds(n * width, width)

    def there(n):
        return pl.ds(pl.multiple_of(start + n * width, BLK), width)

    def bring(n, p):
        return pltpu.make_async_copy(params_ref.at[p, :, there(n)], cells_ref.at[p, :, here(n)], in_sems.at[n, p])

    def send(n, p):
        return pltpu.make_async_copy(new_ref.at[p, :, here(n)], out_ref.at[p, :, there(n)], out_sems.at[n, p])

    for n in range(steps):
        for p in range(2):
            bring(n, p).start()
    for n in range(steps):
        for p in range(2):
            bring(n, p).wait()
        for g in range(n * GROUP, (n + 1) * GROUP):
            change_block(isel_ref, screened_ref, cells_ref, new_ref, g)
        for p in range(2):
            send(n, p).start()
    for n in range(steps):
        for p in range(2):
            send(n, p).wait()


vmem = pl.BlockSpec(memory_space=pltpu.VMEM)
smem = pl.BlockSpec(memory_space=pltpu.SMEM)
hbm = pl.BlockSpec(memory_space=pl.ANY)
limit = pltpu.CompilerParams(vmem_limit_bytes=56 * 1024 * 1024)


def pack(core, predicted, perturbation, observed, obs_sd, slabs):
    whole = jax.ShapeDtypeStruct((slabs, ROWS, BLK), bf16)
    return pl.pallas_call(
        pack_kernel,
        out_shape=whole,
        in_specs=[smem, vmem, vmem, vmem, vmem],
        out_specs=vmem,
        compiler_params=limit,
        name="pack",
    )(core, predicted, perturbation, observed[None], obs_sd[None])


def make_maps(core, block_map, own, other, near, far):
    blocks = block_map.shape[0]
    data = own.shape[0] * BLK
    return pl.pallas_call(
        map_kernel,
        out_shape=(
            jax.ShapeDtypeStruct((2 * MP, MP), bf16),
            jax.ShapeDtypeStruct((SYS - 1, 2 * MP, MP), bf16),
            jax.ShapeDtypeStruct((blocks // 2 * NNZ, MP), bf16),
        ),
        in_specs=[smem, hbm, hbm, hbm, vmem, vmem],
        out_specs=(hbm, hbm, hbm),
        scratch_shapes=[
            pltpu.VMEM((data, MP), bf16),
            pltpu.VMEM((3, ROWS, data), bf16),
            pltpu.VMEM((2 * data, BLK), f32),
            pltpu.VMEM((2 * NNZ, BLK), f32),
            pltpu.VMEM((SYS, M, MP), f32),
            pltpu.VMEM(own.shape, bf16),
            pltpu.SMEM(block_map.shape, jnp.int32),
            pltpu.SemaphoreType.DMA((PARTS + 1,)),
            pltpu.VMEM((blocks // 2 * NNZ, MP), bf16),
            pltpu.VMEM((SYS, 2 * MP, MP), bf16),
            pltpu.SemaphoreType.DMA((SYS + 1,)),
        ] + [pltpu.VMEM((M, MP), f32)] * SYS,
        compiler_params=limit,
        cost_estimate=pl.CostEstimate(flops=20_000_000_000, bytes_accessed=8_000_000, transcendentals=0),
        name="maps",
    )(core, block_map, own, other, near, far)


def select(half, core, block_map, own, other):
    blocks = block_map.shape[0] // 2
    data = own.shape[0] * BLK
    return pl.pallas_call(
        select_kernel,
        out_shape=jax.ShapeDtypeStruct((MP, blocks * NNZ), bf16),
        in_specs=[smem, smem, hbm, hbm, hbm],
        out_specs=vmem,
        scratch_shapes=[
            pltpu.VMEM((2 * data, BLK), f32),
            pltpu.VMEM((4 * NNZ, BLK), f32),
            pltpu.VMEM(own.shape, bf16),
            pltpu.SMEM(block_map.shape, jnp.int32),
            pltpu.SemaphoreType.DMA((PARTS + 1,)),
        ],
        compiler_params=limit,
        cost_estimate=pl.CostEstimate(flops=8_000_000_000, bytes_accessed=8_000_000, transcendentals=0),
        name="select",
    )(half, core, block_map, own, other)


def screen(core, psel, isel, full, mine, theirs, params):
    blocks = params.shape[2] // BLK // 2
    steps = blocks // GROUP
    cells = pl.BlockSpec((2, M, GROUP * BLK), lambda i, c: (0, 0, c[0] * steps + i))
    rows = pl.BlockSpec((GROUP * NNZ, MP), lambda i, c: (i, 0))
    return pl.pallas_call(
        gain_kernel,
        out_shape=(
            jax.ShapeDtypeStruct((blocks, NNZ, 2 * BLK), bf16),
            jax.ShapeDtypeStruct(params.shape, f32),
        ),
        grid_spec=pltpu.PrefetchScalarGridSpec(
            num_scalar_prefetch=1,
            grid=(steps,),
            in_specs=[rows, pl.BlockSpec((MP, GROUP * NNZ), lambda i, c: (0, i)), hbm, hbm, hbm, cells],
            out_specs=(pl.BlockSpec((GROUP, NNZ, 2 * BLK), lambda i, c: (i, 0, 0)), cells),
            scratch_shapes=[
                pltpu.VMEM((GROUP, MAPS * NNZ, MP), bf16),
                pltpu.VMEM((MAPS, 2 * MP, MP), bf16),
                pltpu.SemaphoreType.DMA((MAPS,)),
            ],
        ),
        compiler_params=limit,
        cost_estimate=pl.CostEstimate(flops=20_000_000_000, bytes_accessed=16_000_000, transcendentals=0),
        name="gains",
    )(core, psel, isel, full, mine, theirs, params)


def update(half, isel, screened, params, so_far):
    blocks = screened.shape[0]
    steps = blocks // GROUP
    return pl.pallas_call(
        change_kernel,
        out_shape=jax.ShapeDtypeStruct(params.shape, f32),
        in_specs=[smem, vmem, vmem, hbm, hbm],
        out_specs=hbm,
        scratch_shapes=[
            pltpu.VMEM((2, M, blocks * BLK), bf16),
            pltpu.VMEM((2, M, blocks * BLK), f32),
            pltpu.SemaphoreType.DMA((steps, 2)),
            pltpu.SemaphoreType.DMA((steps, 2)),
        ],
        input_output_aliases={4: 0},
        compiler_params=limit,
        cost_estimate=pl.CostEstimate(flops=5_000_000_000, bytes_accessed=10_000_000, transcendentals=0),
        name="change",
    )(half, isel, screened, params, so_far)


def on_device(params, predicted, perturbation, observed, obs_sd, members, block_map):
    boot = lax.axis_index("boot")
    core = lax.rem(boot, 2)
    core_arg = core.reshape(1).astype(jnp.int32)
    slabs = lax.axis_size("slab")
    pair = [(i, i ^ 1) for i in range(4)]
    far = [(i, i ^ 2) for i in range(4)]

    far_members = lax.ppermute(members, "boot", far)
    whole = pack(core_arg, predicted, perturbation, observed, obs_sd, slabs)
    whole, far_members = lax.optimization_barrier((whole, far_members))
    own = lax.all_to_all(whole, "slab", 0, 0)
    other = lax.ppermute(own, "boot", pair)

    full, mine, psel = make_maps(core_arg, block_map, own, other, members, far_members)
    late_map, mine = lax.optimization_barrier((block_map, mine))
    theirs = lax.ppermute(mine, "boot", pair)
    isel = select(core_arg, core_arg, late_map, own, other)
    isel, psel = lax.optimization_barrier((isel, psel))
    screened, so_far = screen(core_arg, psel, isel, full, mine, theirs, params)
    last_map, screened = lax.optimization_barrier((block_map, screened))
    screened_other = lax.ppermute(screened, "boot", pair)
    isel_other = select(1 - core_arg, core_arg, last_map, own, other)
    return update(1 - core_arg, isel_other, screened_other, params, so_far)


def solution(mesh):
    return jax.shard_map(
        on_device,
        mesh=mesh,
        in_specs=(
            P(None, None, "slab"),
            P(None, "slab"),
            P(None, "slab"),
            P("slab"),
            P("slab"),
            P("boot", None),
            P("slab", None),
        ),
        out_specs=P(None, None, "slab"),
        check_vma=False,
    )
```

```python
from functools import partial
import math

import jax
import jax.numpy as jnp
from jax import lax
from jax.experimental import pallas as pl
from jax.experimental.pallas import tpu as pltpu
from jax.sharding import PartitionSpec as P

M = 200
NB = 16
BLK = 128
NNZ = 64
MP = 256
ROWS = 208
PIV = 40
SYS = 9
PARTS = 4
PACK = 3
MAPS = 17
GROUP = 8

screen_floor = 1e-05
f32 = jnp.float32
bf16 = jnp.bfloat16


def iota(shape, dim):
    return lax.broadcasted_iota(jnp.int32, shape, dim)


def split3(x):
    hi = x.astype(bf16).astype(f32)
    rest = x - hi
    mid = rest.astype(bf16).astype(f32)
    return hi, mid, rest - mid


def lhs6(c):
    hi, mid, lo = split3(c)
    left = hi + pltpu.roll(hi, PIV, 1) + pltpu.roll(hi, 2 * PIV, 1)
    right = mid + pltpu.roll(mid, PIV, 1) + pltpu.roll(lo, 2 * PIV, 1)
    return jnp.concatenate([left, right], axis=1).astype(bf16)


def rhs6(r):
    hi, mid, lo = split3(r)
    pad = jnp.zeros((BLK - 3 * PIV, MP), f32)
    return jnp.concatenate([hi, mid, lo, pad, hi, mid, hi, pad], axis=0).astype(bf16)


def dot(a, b):
    return jnp.dot(a, b, preferred_element_type=f32)


def scaling(listed):
    lane = iota((M, MP), 1)
    if listed is None:
        down = jnp.ones((M, 1), f32)
        across = jnp.where(lane[:1] < M, 1.0, 0.0)
    else:
        down = jnp.sqrt(jnp.sum(jnp.where(iota((M, M), 0) == listed, 1.0, 0.0), axis=1, keepdims=True))
        across = jnp.sum(jnp.where(iota((M, MP), 0) == lane, down, 0.0), axis=0, keepdims=True)
    root = 1.0 / math.sqrt(M)
    return down * (1.0 / (M - 1)) * across, down * root, across * root


def pack_kernel(core_ref, pred_ref, pert_ref, obs_ref, sd_ref, out_ref):
    sd = sd_ref[...].astype(f32)
    ens = pred_ref[...].astype(f32)
    innov = obs_ref[...].astype(f32) + sd * pert_ref[...].astype(f32) - ens
    rows = jnp.where(core_ref[0] == 0, ens, innov)
    tail = jnp.concatenate([sd, jnp.zeros((ROWS - M - 1, BLK), f32)], axis=0)
    part = jnp.concatenate([rows, tail], axis=0).astype(bf16)
    for i in range(out_ref.shape[0]):
        out_ref[i] = part


def gathered(own_first, own_ref, other_ref, ens_ref, innov_ref, map_ref, index_ref, sems):
    step = ens_ref.shape[0] // PARTS

    def copy(source, target, n):
        at = pl.ds(n % PARTS * step, step)
        return pltpu.make_async_copy(source.at[at], target.at[at], sems.at[n])

    def start(first_ref, second_ref):
        for n in range(PARTS):
            copy(first_ref, ens_ref, n).start()
        index_copy.start()
        for n in range(PARTS):
            copy(second_ref, innov_ref, PARTS + n).start()

    index_copy = pltpu.make_async_copy(map_ref, index_ref, sems.at[2 * PARTS])

    @pl.when(own_first)
    def _():
        start(own_ref, other_ref)

    @pl.when(jnp.logical_not(own_first))
    def _():
        start(other_ref, own_ref)

    def wait(n):
        if n == 2 * PARTS:
            index_copy.wait()
        else:
            copy(own_ref, ens_ref if n < PARTS else innov_ref, n).wait()

    return wait


def chunk_rows(rows_ref, i):
    rows = rows_ref[i].astype(f32)
    high = jnp.concatenate([rows[BLK:], jnp.zeros((MP - ROWS, BLK), f32)], axis=0)
    return rows, rows[:BLK], high


def by_parts(count, first, wait, chunk):
    step = count // PARTS
    for n in range(PARTS):
        wait(first + n)
        lax.fori_loop(n * step, (n + 1) * step, chunk, 0, unroll=4)


def fill_table(t_ref, i, low, high):
    base = pl.multiple_of(i * (2 * BLK), 8)
    t_ref[pl.ds(base, BLK, stride=2), :] = low
    t_ref[pl.ds(base + 1, BLK, stride=2), :] = high


def along(tile, u):
    return jnp.broadcast_to(tile[u:u + 1], tile.shape)


def inverse_of(x):
    guess = pl.reciprocal(x, approx=True)
    guess = guess * (2.0 - x * guess)
    return guess * (2.0 - x * guess)


def map_kernel(
    core_ref, map_ref, own_ref, other_ref, near_ref, far_ref, full_ref, res_ref, psel_ref, isel_ref,
    ens_ref, parts_ref, ptab_ref, itab_ref, pline_ref, iline_ref, scale_ref, rows_ref, late_ref, index_ref,
    sems, maps_ref, out_sems, *sys_refs
):
    core = core_ref[0]
    blocks = map_ref.shape[0]
    wait = gathered(core == 0, own_ref, other_ref, rows_ref, late_ref, map_ref, index_ref, sems)
    near = near_ref.shape[0]

    def chunk(i, carry):
        rows, low, high = chunk_rows(rows_ref, i)
        sd = rows[M:M + 1]
        at = pl.ds(pl.multiple_of(i * BLK, BLK), BLK)
        for n, part in enumerate(split3(rows * (1.0 / (sd * sd)))):
            parts_ref[n, :, at] = part.astype(bf16)
        low, high = low.T, high.T
        ens_ref[at, :] = jnp.concatenate([low, high], axis=1).astype(bf16)
        fill_table(ptab_ref, i, low, high)
        return carry

    by_parts(rows_ref.shape[0], 0, wait, chunk)

    def late_chunk(i, carry):
        _, low, high = chunk_rows(late_ref, i)
        fill_table(itab_ref, i, low.T, high.T)
        return carry

    by_parts(late_ref.shape[0], PARTS, wait, late_chunk)
    wait(2 * PARTS)

    gram = 0.0
    for n in (2, 1, 0):
        gram = gram + dot(parts_ref[n], ens_ref[...])
    gram = gram[:M]

    ipanel = -(-blocks // (M // PIV))
    ppanel = -(-(blocks // 2) // (M // PIV))
    share = -(-(ipanel + ppanel) * NNZ // PIV)

    def pick(kp, t):
        for n in range(t * share, min((t + 1) * share, (ipanel + ppanel) * NNZ)):
            b, j = n // NNZ, n % NNZ
            if b < ipanel:
                k = jnp.minimum(kp * ipanel + b, blocks - 1)
                at = index_ref[k, j]
                iline_ref[pl.ds(k * (2 * NNZ) + 2 * j, 2), :] = itab_ref[pl.ds(2 * at, 2), :]
            else:
                k = jnp.minimum(kp * ppanel + b - ipanel, blocks // 2 - 1)
                at = index_ref[core * (blocks // 2) + k, j]
                pline_ref[pl.ds(k * (2 * NNZ) + 2 * j, 2), :] = ptab_ref[pl.ds(2 * at, 2), :]

    row = iota((M, MP), 0)
    lane = iota((M, MP), 1)
    for s in range(SYS):
        listed = None
        if s:
            listed = near_ref[s - 1:s, :] if s <= near else far_ref[s - 1 - near:s - near, :]
        scale, ud, ua = scaling(listed)
        scale_ref[s] = scale
        h = gram * scale
        hu = jnp.sum(h * ua, axis=1, keepdims=True)
        uh = jnp.sum(h * ud, axis=0, keepdims=True)
        uhu = jnp.sum(hu * ud, axis=0, keepdims=True)
        h = h - ud * (uh - 0.5 * uhu * ua) - (hu - 0.5 * uhu * ud) * ua
        sys_refs[s][...] = h + jnp.where(row == lane, 1.0, 0.0)

    prow = iota((PIV, MP), 0)
    plane = iota((PIV, MP), 1)
    dlane = iota((PIV, BLK), 1)
    trow = iota((8, BLK), 0)
    tlane = iota((8, BLK), 1)
    first = jnp.minimum(tlane // PIV, PACK - 1) * PIV
    inner = tlane - first

    def panel_step(kp, carry):
        k0 = kp * PIV
        at = pl.ds(pl.multiple_of(k0, 8), PIV)
        packs = []
        for g in range(SYS // PACK):
            pack = jnp.zeros((PIV, BLK), f32)
            for q in range(PACK):
                moved = pltpu.roll(sys_refs[PACK * g + q][at, :], lax.rem(MP - k0 + q * PIV, MP), 1)[:, :BLK]
                pack = jnp.where((dlane >= q * PIV) & (dlane < (q + 1) * PIV), moved, pack)
            packs.append(pack)
        starts = packs
        tiles = [[pack[8 * i:8 * i + 8] for i in range(PIV // 8)] for pack in packs]
        for j in range(PIV // 8):
            cols = [
                [[jnp.take_along_axis(tile, first + 8 * j + u, axis=1) for u in range(8)] for tile in group]
                for group in tiles
            ]
            for u in range(8):
                at_lane = inner == 8 * j + u
                for group, col in zip(tiles, cols):
                    lead = col[j][u]
                    scale = inverse_of(along(lead, u))
                    t = group[j]
                    line = jnp.where(at_lane, 1.0, along(t, u)) * scale
                    group[j] = jnp.where(trow == u, line, jnp.where(at_lane, 0.0, t) - lead * line)
                    for v in range(u + 1, 8):
                        c = col[j][v]
                        line = along(c, u) * scale
                        col[j][v] = jnp.where(trow == u, line, c - lead * line)
                pick(kp, 8 * j + u)
            done = (inner >= 8 * j) & (inner < 8 * j + 8)
            for group, col in zip(tiles, cols):
                for i in range(PIV // 8):
                    if i != j:
                        tile = jnp.where(done, 0.0, group[i])
                        for u in range(8):
                            tile = tile - col[i][u] * group[j][u:u + 1]
                        group[i] = tile
        packs = [jnp.concatenate(group, axis=0) for group in tiles]
        inside = (lane >= k0) & (lane < k0 + PIV)
        pad = jnp.zeros((BLK - 3 * PIV, MP), f32)
        inverses, blocks_, panels, wanted, lines = [], [], [], [], []
        for s in range(SYS):
            back = (BLK - (s % PACK) * PIV) % BLK
            for kept, source in ((inverses, packs), (blocks_, starts)):
                moved = source[s // PACK]
                if back:
                    moved = pltpu.roll(moved, back, 1)
                kept.append(lhs6(jnp.where(dlane < PIV, moved, 0.0)))
            panels.append(sys_refs[s][at, :])
            wanted.append(jnp.where(plane == prow + k0, -1.0, jnp.where(inside[:PIV], 0.0, panels[s])))
        for s in range(SYS):
            lines.append(dot(inverses[s], rhs6(wanted[s])))
        for s in range(SYS):
            lines[s] = lines[s] + dot(inverses[s], rhs6(wanted[s] - dot(blocks_[s], rhs6(lines[s]))))
        for s in range(SYS):
            hi, mid, lo = split3(panels[s])
            left = jnp.concatenate([hi, hi, hi, pad, mid, mid, lo, pad], axis=0).astype(bf16)
            change = lax.dot_general(left, rhs6(lines[s]), (((0,), (0,)), ((), ())), preferred_element_type=f32)
            sys_refs[s][...] = jnp.where(inside, 0.0, sys_refs[s][...]) - change[:M]
            sys_refs[s][at, :] = lines[s]
        return carry

    lax.fori_loop(0, M // PIV, panel_step, 0)

    outs = [
        pltpu.make_async_copy(pline_ref, psel_ref, out_sems.at[SYS]),
        pltpu.make_async_copy(iline_ref, isel_ref, out_sems.at[SYS + 1]),
    ]
    for copy in outs:
        copy.start()
    for s in range(SYS):
        scale = scale_ref[s]
        value = (-sys_refs[s][...] - scale * ((M - 1) / M)) * scale
        value = jnp.concatenate([value, jnp.zeros((MP - M, MP), f32)], axis=0)
        hi = value.astype(bf16)
        maps_ref[s] = jnp.concatenate([hi, (value - hi.astype(f32)).astype(bf16)], axis=0)
        outs.append(pltpu.make_async_copy(maps_ref.at[s], res_ref.at[s - 1] if s else full_ref, out_sems.at[s]))
        outs[-1].start()
    for copy in outs:
        copy.wait()


def arrange_kernel(pline_ref, iline_ref, psel_ref, isel_ref):
    for n in range(2):
        lanes = slice(n * BLK, (n + 1) * BLK)
        psel_ref[:, lanes] = pline_ref[pl.ds(n, psel_ref.shape[0], stride=2), :].astype(bf16)
        for k in range(isel_ref.shape[1] // BLK):
            at = slice(k * BLK, (k + 1) * BLK)
            isel_ref[lanes, at] = iline_ref[pl.ds(2 * k * BLK + n, BLK, stride=2), :].T.astype(bf16)


def change_block(isel_ref, screened_ref, cells_ref, new_ref, g):
    picked = isel_ref[:ROWS, g // 2 * BLK:(g // 2 + 1) * BLK]
    none = jnp.zeros((NNZ, 2 * BLK), bf16)
    rows = [none, screened_ref[g]] if g % 2 else [screened_ref[g], none]
    change = dot(picked, jnp.concatenate(rows, axis=0))
    at = slice(g * BLK, (g + 1) * BLK)
    for p in range(2):
        new_ref[p, :, at] = cells_ref[p, :, at].astype(f32) + change[:M, p * BLK:(p + 1) * BLK]


def gain_kernel(core_ref, psel_ref, isel_ref, full_ref, mine_ref, theirs_ref, params_ref, screened_ref, out_ref, cols_ref, maps_ref, sems):
    refs = [full_ref] + [mine_ref.at[r] for r in range(SYS - 1)] + [theirs_ref.at[r] for r in range(SYS - 1)]
    copies = [pltpu.make_async_copy(ref, maps_ref.at[r], sems.at[r]) for r, ref in enumerate(refs)]
    opening = pl.program_id(0) == 0

    @pl.when(opening)
    def _():
        for copy in copies:
            copy.start()

    x = psel_ref[...]
    sd = x[:, M:M + 1].astype(f32)
    weight = 1.0 / (sd * sd)
    x = jnp.concatenate([x, x], axis=1)

    for some in (range(4), range(4, 10), range(10, MAPS)):
        @pl.when(opening)
        def _():
            for r in some:
                copies[r].wait()

        for r in some:
            total = (dot(x, maps_ref[r]) * weight).astype(bf16)
            for g in range(GROUP):
                cols_ref[g, r * NNZ:(r + 1) * NNZ, :] = total[g * NNZ:(g + 1) * NNZ]

    def gains(g, carry):
        at = pl.ds(pl.multiple_of(g * BLK, BLK), BLK)
        cells = jnp.concatenate([params_ref[0, :, at], params_ref[1, :, at]], axis=1)
        every = dot(cols_ref[g][:, :M], cells)
        full = every[:NNZ]
        spread = jnp.zeros_like(full)
        for r in range(1, MAPS):
            off = every[r * NNZ:(r + 1) * NNZ] - full
            spread = spread + off * off
        squared = full * full
        screened_ref[g] = (squared / (squared + spread * (1.0 / NB) + screen_floor) * full).astype(bf16)
        return carry

    lax.fori_loop(0, GROUP, gains, 0, unroll=GROUP)
    for g in range(GROUP):
        change_block(isel_ref, screened_ref, params_ref, out_ref, g)


def change_kernel(half_ref, all_ref, theirs_ref, params_ref, so_far_ref, out_ref, isel_ref, screened_ref, cells_ref, new_ref, sems, in_sems, out_sems):
    blocks = screened_ref.shape[0]
    width = GROUP * BLK
    steps = blocks // GROUP
    start = pl.multiple_of(half_ref[0] * (blocks * BLK), BLK)

    def here(n):
        return pl.ds(n * width, width)

    def there(n):
        return pl.ds(pl.multiple_of(start + n * width, BLK), width)

    def bring(n, p):
        return pltpu.make_async_copy(params_ref.at[p, :, there(n)], cells_ref.at[p, :, here(n)], in_sems.at[n, p])

    def send(n, p):
        return pltpu.make_async_copy(new_ref.at[p, :, here(n)], out_ref.at[p, :, there(n)], out_sems.at[n, p])

    at = pl.ds(pl.multiple_of(half_ref[0] * (blocks * NNZ), BLK), blocks * NNZ)
    both = [
        pltpu.make_async_copy(all_ref.at[:, at], isel_ref, sems.at[0]),
        pltpu.make_async_copy(theirs_ref, screened_ref, sems.at[1]),
    ]
    for copy in both:
        copy.start()
    for n in range(steps):
        for p in range(2):
            bring(n, p).start()
    for copy in both:
        copy.wait()
    for n in range(steps):
        for p in range(2):
            bring(n, p).wait()
        for g in range(n * GROUP, (n + 1) * GROUP):
            change_block(isel_ref, screened_ref, cells_ref, new_ref, g)
        for p in range(2):
            send(n, p).start()
    for n in range(steps):
        for p in range(2):
            send(n, p).wait()


vmem = pl.BlockSpec(memory_space=pltpu.VMEM)
smem = pl.BlockSpec(memory_space=pltpu.SMEM)
hbm = pl.BlockSpec(memory_space=pl.ANY)
limit = pltpu.CompilerParams(vmem_limit_bytes=62 * 1024 * 1024)


def pack(core, predicted, perturbation, observed, obs_sd, slabs):
    whole = jax.ShapeDtypeStruct((slabs, ROWS, BLK), bf16)
    return pl.pallas_call(
        pack_kernel,
        out_shape=whole,
        in_specs=[smem, vmem, vmem, vmem, vmem],
        out_specs=vmem,
        compiler_params=limit,
        name="pack",
    )(core, predicted, perturbation, observed[None], obs_sd[None])


def make_maps(core, block_map, own, other, near, far):
    blocks = block_map.shape[0]
    data = own.shape[0] * BLK
    return pl.pallas_call(
        map_kernel,
        out_shape=(
            jax.ShapeDtypeStruct((2 * MP, MP), bf16),
            jax.ShapeDtypeStruct((SYS - 1, 2 * MP, MP), bf16),
            jax.ShapeDtypeStruct((blocks * NNZ, BLK), f32),
            jax.ShapeDtypeStruct((2 * blocks * NNZ, BLK), f32),
        ),
        in_specs=[smem, hbm, hbm, hbm, vmem, vmem],
        out_specs=(hbm, hbm, hbm, hbm),
        scratch_shapes=[
            pltpu.VMEM((data, MP), bf16),
            pltpu.VMEM((3, ROWS, data), bf16),
            pltpu.VMEM((2 * data, BLK), f32),
            pltpu.VMEM((2 * data, BLK), f32),
            pltpu.VMEM((blocks * NNZ, BLK), f32),
            pltpu.VMEM((2 * blocks * NNZ, BLK), f32),
            pltpu.VMEM((SYS, M, MP), f32),
            pltpu.VMEM(own.shape, bf16),
            pltpu.VMEM(own.shape, bf16),
            pltpu.SMEM(block_map.shape, jnp.int32),
            pltpu.SemaphoreType.DMA((2 * PARTS + 1,)),
            pltpu.VMEM((SYS, 2 * MP, MP), bf16),
            pltpu.SemaphoreType.DMA((SYS + 2,)),
        ] + [pltpu.VMEM((M, MP), f32)] * SYS,
        compiler_params=limit,
        cost_estimate=pl.CostEstimate(flops=20_000_000_000, bytes_accessed=8_000_000, transcendentals=0),
        name="maps",
    )(core, block_map, own, other, near, far)


def arrange(pline, iline):
    steps = 4
    prows, irows = pline.shape[0] // steps, iline.shape[0] // steps
    return pl.pallas_call(
        arrange_kernel,
        out_shape=(
            jax.ShapeDtypeStruct((pline.shape[0] // 2, MP), bf16),
            jax.ShapeDtypeStruct((MP, iline.shape[0] // 2), bf16),
        ),
        grid=(steps,),
        in_specs=[pl.BlockSpec((prows, BLK), lambda i: (i, 0)), pl.BlockSpec((irows, BLK), lambda i: (i, 0))],
        out_specs=(
            pl.BlockSpec((prows // 2, MP), lambda i: (i, 0)),
            pl.BlockSpec((MP, irows // 2), lambda i: (0, i)),
        ),
        compiler_params=limit,
        cost_estimate=pl.CostEstimate(flops=6_000_000_000, bytes_accessed=9_000_000, transcendentals=0),
        name="arrange",
    )(pline, iline)


def screen(core, psel, isel, full, mine, theirs, params):
    blocks = params.shape[2] // BLK // 2
    steps = blocks // GROUP
    cells = pl.BlockSpec((2, M, GROUP * BLK), lambda i, c: (0, 0, c[0] * steps + i))
    rows = pl.BlockSpec((GROUP * NNZ, MP), lambda i, c: (i, 0))
    return pl.pallas_call(
        gain_kernel,
        out_shape=(
            jax.ShapeDtypeStruct((blocks, NNZ, 2 * BLK), bf16),
            jax.ShapeDtypeStruct(params.shape, f32),
        ),
        grid_spec=pltpu.PrefetchScalarGridSpec(
            num_scalar_prefetch=1,
            grid=(steps,),
            in_specs=[rows, pl.BlockSpec((MP, GROUP * NNZ), lambda i, c: (0, c[0] * steps + i)), hbm, hbm, hbm, cells],
            out_specs=(pl.BlockSpec((GROUP, NNZ, 2 * BLK), lambda i, c: (i, 0, 0)), cells),
            scratch_shapes=[
                pltpu.VMEM((GROUP, MAPS * NNZ, MP), bf16),
                pltpu.VMEM((MAPS, 2 * MP, MP), bf16),
                pltpu.SemaphoreType.DMA((MAPS,)),
            ],
        ),
        compiler_params=limit,
        cost_estimate=pl.CostEstimate(flops=20_000_000_000, bytes_accessed=16_000_000, transcendentals=0),
        name="gains",
    )(core, psel, isel, full, mine, theirs, params)


def update(half, isel, screened, params, so_far):
    blocks = screened.shape[0]
    steps = blocks // GROUP
    return pl.pallas_call(
        change_kernel,
        out_shape=jax.ShapeDtypeStruct(params.shape, f32),
        in_specs=[smem, hbm, hbm, hbm, hbm],
        out_specs=hbm,
        scratch_shapes=[
            pltpu.VMEM((MP, blocks * NNZ), bf16),
            pltpu.VMEM(screened.shape, bf16),
            pltpu.VMEM((2, M, blocks * BLK), bf16),
            pltpu.VMEM((2, M, blocks * BLK), f32),
            pltpu.SemaphoreType.DMA((2,)),
            pltpu.SemaphoreType.DMA((steps, 2)),
            pltpu.SemaphoreType.DMA((steps, 2)),
        ],
        input_output_aliases={4: 0},
        compiler_params=limit,
        cost_estimate=pl.CostEstimate(flops=5_000_000_000, bytes_accessed=10_000_000, transcendentals=0),
        name="change",
    )(half, isel, screened, params, so_far)


def on_device(params, predicted, perturbation, observed, obs_sd, members, block_map):
    boot = lax.axis_index("boot")
    core = lax.rem(boot, 2)
    core_arg = core.reshape(1).astype(jnp.int32)
    slabs = lax.axis_size("slab")
    pair = [(i, i ^ 1) for i in range(4)]
    far = [(i, i ^ 2) for i in range(4)]

    far_members = lax.ppermute(members, "boot", far)
    whole = pack(core_arg, predicted, perturbation, observed, obs_sd, slabs)
    whole, far_members = lax.optimization_barrier((whole, far_members))
    own = lax.all_to_all(whole, "slab", 0, 0)
    other = lax.ppermute(own, "boot", pair)

    full, mine, pline, iline = make_maps(core_arg, block_map, own, other, members, far_members)
    theirs = lax.ppermute(mine, "boot", pair)
    psel, isel = arrange(pline, iline)
    screened, so_far = screen(core_arg, psel, isel, full, mine, theirs, params)
    screened_other = lax.ppermute(screened, "boot", pair)
    return update(1 - core_arg, isel, screened_other, params, so_far)


def solution(mesh):
    return jax.shard_map(
        on_device,
        mesh=mesh,
        in_specs=(
            P(None, None, "slab"),
            P(None, "slab"),
            P(None, "slab"),
            P("slab"),
            P("slab"),
            P("boot", None),
            P("slab", None),
        ),
        out_specs=P(None, None, "slab"),
        check_vma=False,
    )
```

```python
from functools import partial
import math

import jax
import jax.numpy as jnp
from jax import lax
from jax.experimental import pallas as pl
from jax.experimental.pallas import tpu as pltpu
from jax.sharding import PartitionSpec as P

M = 200
NB = 16
BLK = 128
NNZ = 64
MP = 256
ROWS = 208
PIV = 40
SYS = 9
PARTS = 4
PACK = 3
MAPS = 17
GROUP = 8

screen_floor = 1e-05
f32 = jnp.float32
bf16 = jnp.bfloat16


def iota(shape, dim):
    return lax.broadcasted_iota(jnp.int32, shape, dim)


def split3(x):
    hi = x.astype(bf16).astype(f32)
    rest = x - hi
    mid = rest.astype(bf16).astype(f32)
    return hi, mid, rest - mid


def lhs6(c):
    hi, mid, lo = split3(c)
    left = hi + pltpu.roll(hi, PIV, 1) + pltpu.roll(hi, 2 * PIV, 1)
    right = mid + pltpu.roll(mid, PIV, 1) + pltpu.roll(lo, 2 * PIV, 1)
    return jnp.concatenate([left, right], axis=1).astype(bf16)


def rhs6(r):
    hi, mid, lo = split3(r)
    pad = jnp.zeros((BLK - 3 * PIV, MP), f32)
    return jnp.concatenate([hi, mid, lo, pad, hi, mid, hi, pad], axis=0).astype(bf16)


def dot(a, b):
    return jnp.dot(a, b, preferred_element_type=f32)


def scaling(listed):
    lane = iota((M, MP), 1)
    if listed is None:
        down = jnp.ones((M, 1), f32)
        across = jnp.where(lane[:1] < M, 1.0, 0.0)
    else:
        down = jnp.sqrt(jnp.sum(jnp.where(iota((M, M), 0) == listed, 1.0, 0.0), axis=1, keepdims=True))
        across = jnp.sum(jnp.where(iota((M, MP), 0) == lane, down, 0.0), axis=0, keepdims=True)
    root = 1.0 / math.sqrt(M)
    return down * (1.0 / (M - 1)) * across, down * root, across * root


def pack_kernel(core_ref, pred_ref, pert_ref, obs_ref, sd_ref, out_ref):
    sd = sd_ref[...].astype(f32)
    ens = pred_ref[...].astype(f32)
    innov = obs_ref[...].astype(f32) + sd * pert_ref[...].astype(f32) - ens
    rows = jnp.where(core_ref[0] == 0, ens, innov)
    tail = jnp.concatenate([sd, jnp.zeros((ROWS - M - 1, BLK), f32)], axis=0)
    part = jnp.concatenate([rows, tail], axis=0).astype(bf16)
    for i in range(out_ref.shape[0]):
        out_ref[i] = part


def gathered(own_first, own_ref, other_ref, ens_ref, innov_ref, map_ref, index_ref, sems):
    step = ens_ref.shape[0] // PARTS

    def copy(source, target, n):
        at = pl.ds(n % PARTS * step, step)
        return pltpu.make_async_copy(source.at[at], target.at[at], sems.at[n])

    def start(first_ref, second_ref):
        for n in range(PARTS):
            copy(first_ref, ens_ref, n).start()
        index_copy.start()
        for n in range(PARTS):
            copy(second_ref, innov_ref, PARTS + n).start()

    index_copy = pltpu.make_async_copy(map_ref, index_ref, sems.at[2 * PARTS])

    @pl.when(own_first)
    def _():
        start(own_ref, other_ref)

    @pl.when(jnp.logical_not(own_first))
    def _():
        start(other_ref, own_ref)

    def wait(n):
        if n == 2 * PARTS:
            index_copy.wait()
        else:
            copy(own_ref, ens_ref if n < PARTS else innov_ref, n).wait()

    return wait


def chunk_rows(rows_ref, i):
    rows = rows_ref[i].astype(f32)
    high = jnp.concatenate([rows[BLK:], jnp.zeros((MP - ROWS, BLK), f32)], axis=0)
    return rows, rows[:BLK], high


def by_parts(count, first, wait, chunk):
    step = count // PARTS
    for n in range(PARTS):
        wait(first + n)
        lax.fori_loop(n * step, (n + 1) * step, chunk, 0, unroll=4)


def fill_table(t_ref, i, low, high):
    base = pl.multiple_of(i * (2 * BLK), 8)
    t_ref[pl.ds(base, BLK, stride=2), :] = low
    t_ref[pl.ds(base + 1, BLK, stride=2), :] = high


def along(tile, u):
    return jnp.broadcast_to(tile[u:u + 1], tile.shape)


def inverse_of(x):
    guess = pl.reciprocal(x, approx=True)
    guess = guess * (2.0 - x * guess)
    return guess * (2.0 - x * guess)


def map_kernel(
    core_ref, map_ref, own_ref, other_ref, near_ref, far_ref, full_ref, res_ref, psel_ref, isel_ref,
    ens_ref, parts_ref, ptab_ref, itab_ref, pline_ref, iline_ref, scale_ref, rows_ref, late_ref, index_ref,
    sems, maps_ref, out_sems, *sys_refs
):
    core = core_ref[0]
    blocks = map_ref.shape[0]
    wait = gathered(core == 0, own_ref, other_ref, rows_ref, late_ref, map_ref, index_ref, sems)
    near = near_ref.shape[0]

    def chunk(i, carry):
        rows, low, high = chunk_rows(rows_ref, i)
        sd = rows[M:M + 1]
        at = pl.ds(pl.multiple_of(i * BLK, BLK), BLK)
        for n, part in enumerate(split3(rows * (1.0 / (sd * sd)))[:2]):
            parts_ref[n, :, at] = part.astype(bf16)
        low, high = low.T, high.T
        ens_ref[at, :] = jnp.concatenate([low, high], axis=1).astype(bf16)
        fill_table(ptab_ref, i, low, high)
        return carry

    by_parts(rows_ref.shape[0], 0, wait, chunk)

    def late_chunk(i, carry):
        _, low, high = chunk_rows(late_ref, i)
        fill_table(itab_ref, i, low.T, high.T)
        return carry

    by_parts(late_ref.shape[0], PARTS, wait, late_chunk)
    wait(2 * PARTS)

    gram = 0.0
    for n in (1, 0):
        gram = gram + dot(parts_ref[n], ens_ref[...])
    gram = gram[:M]

    ipanel = -(-blocks // (M // PIV))
    ppanel = -(-(blocks // 2) // (M // PIV))
    share = -(-(ipanel + ppanel) * NNZ // PIV)

    def pick(kp, t):
        for n in range(t * share, min((t + 1) * share, (ipanel + ppanel) * NNZ)):
            b, j = n // NNZ, n % NNZ
            if b < ipanel:
                k = jnp.minimum(kp * ipanel + b, blocks - 1)
                at = index_ref[k, j]
                iline_ref[pl.ds(k * (2 * NNZ) + 2 * j, 2), :] = itab_ref[pl.ds(2 * at, 2), :]
            else:
                k = jnp.minimum(kp * ppanel + b - ipanel, blocks // 2 - 1)
                at = index_ref[core * (blocks // 2) + k, j]
                pline_ref[pl.ds(k * (2 * NNZ) + 2 * j, 2), :] = ptab_ref[pl.ds(2 * at, 2), :]

    row = iota((M, MP), 0)
    lane = iota((M, MP), 1)
    for s in range(SYS):
        listed = None
        if s:
            listed = near_ref[s - 1:s, :] if s <= near else far_ref[s - 1 - near:s - near, :]
        scale, ud, ua = scaling(listed)
        scale_ref[s] = scale
        h = gram * scale
        hu = jnp.sum(h * ua, axis=1, keepdims=True)
        uh = jnp.sum(h * ud, axis=0, keepdims=True)
        uhu = jnp.sum(hu * ud, axis=0, keepdims=True)
        h = h - ud * (uh - 0.5 * uhu * ua) - (hu - 0.5 * uhu * ud) * ua
        sys_refs[s][...] = h + jnp.where(row == lane, 1.0, 0.0)

    prow = iota((PIV, MP), 0)
    plane = iota((PIV, MP), 1)
    dlane = iota((PIV, BLK), 1)
    trow = iota((8, BLK), 0)
    tlane = iota((8, BLK), 1)
    first = jnp.minimum(tlane // PIV, PACK - 1) * PIV
    inner = tlane - first

    def panel_step(kp, carry):
        k0 = kp * PIV
        at = pl.ds(pl.multiple_of(k0, 8), PIV)
        packs = []
        for g in range(SYS // PACK):
            pack = jnp.zeros((PIV, BLK), f32)
            for q in range(PACK):
                moved = pltpu.roll(sys_refs[PACK * g + q][at, :], lax.rem(MP - k0 + q * PIV, MP), 1)[:, :BLK]
                pack = jnp.where((dlane >= q * PIV) & (dlane < (q + 1) * PIV), moved, pack)
            packs.append(pack)
        starts = packs
        tiles = [[pack[8 * i:8 * i + 8] for i in range(PIV // 8)] for pack in packs]
        for j in range(PIV // 8):
            cols = [
                [[jnp.take_along_axis(tile, first + 8 * j + u, axis=1) for u in range(8)] for tile in group]
                for group in tiles
            ]
            for u in range(8):
                at_lane = inner == 8 * j + u
                for group, col in zip(tiles, cols):
                    lead = col[j][u]
                    scale = inverse_of(along(lead, u))
                    t = group[j]
                    line = jnp.where(at_lane, 1.0, along(t, u)) * scale
                    group[j] = jnp.where(trow == u, line, jnp.where(at_lane, 0.0, t) - lead * line)
                    for v in range(u + 1, 8):
                        c = col[j][v]
                        line = along(c, u) * scale
                        col[j][v] = jnp.where(trow == u, line, c - lead * line)
                pick(kp, 8 * j + u)
            done = (inner >= 8 * j) & (inner < 8 * j + 8)
            for group, col in zip(tiles, cols):
                for i in range(PIV // 8):
                    if i != j:
                        tile = jnp.where(done, 0.0, group[i])
                        for u in range(8):
                            tile = tile - col[i][u] * group[j][u:u + 1]
                        group[i] = tile
        packs = [jnp.concatenate(group, axis=0) for group in tiles]
        inside = (lane >= k0) & (lane < k0 + PIV)
        pad = jnp.zeros((BLK - 3 * PIV, MP), f32)
        inverses, blocks_, panels, wanted, lines = [], [], [], [], []
        for s in range(SYS):
            back = (BLK - (s % PACK) * PIV) % BLK
            for kept, source in ((inverses, packs), (blocks_, starts)):
                moved = source[s // PACK]
                if back:
                    moved = pltpu.roll(moved, back, 1)
                kept.append(lhs6(jnp.where(dlane < PIV, moved, 0.0)))
            panels.append(sys_refs[s][at, :])
            wanted.append(jnp.where(plane == prow + k0, -1.0, jnp.where(inside[:PIV], 0.0, panels[s])))
        for s in range(SYS):
            lines.append(dot(inverses[s], rhs6(wanted[s])))
        for s in range(SYS):
            lines[s] = lines[s] + dot(inverses[s], rhs6(wanted[s] - dot(blocks_[s], rhs6(lines[s]))))
        for s in range(SYS):
            hi, mid, lo = split3(panels[s])
            left = jnp.concatenate([hi, hi, hi, pad, mid, mid, lo, pad], axis=0).astype(bf16)
            change = lax.dot_general(left, rhs6(lines[s]), (((0,), (0,)), ((), ())), preferred_element_type=f32)
            sys_refs[s][...] = jnp.where(inside, 0.0, sys_refs[s][...]) - change[:M]
            sys_refs[s][at, :] = lines[s]
        return carry

    lax.fori_loop(0, M // PIV, panel_step, 0)

    outs = [
        pltpu.make_async_copy(pline_ref, psel_ref, out_sems.at[SYS]),
        pltpu.make_async_copy(iline_ref, isel_ref, out_sems.at[SYS + 1]),
    ]
    for copy in outs:
        copy.start()
    for s in range(SYS):
        scale = scale_ref[s]
        value = (-sys_refs[s][...] - scale * ((M - 1) / M)) * scale
        value = jnp.concatenate([value, jnp.zeros((MP - M, MP), f32)], axis=0)
        hi = value.astype(bf16)
        maps_ref[s] = jnp.concatenate([hi, (value - hi.astype(f32)).astype(bf16)], axis=0)
        outs.append(pltpu.make_async_copy(maps_ref.at[s], res_ref.at[s - 1] if s else full_ref, out_sems.at[s]))
        outs[-1].start()
    for copy in outs:
        copy.wait()


def arrange_kernel(pline_ref, iline_ref, psel_ref, isel_ref):
    for n in range(2):
        lanes = slice(n * BLK, (n + 1) * BLK)
        psel_ref[:, lanes] = pline_ref[pl.ds(n, psel_ref.shape[0], stride=2), :].astype(bf16)
        for k in range(isel_ref.shape[1] // BLK):
            at = slice(k * BLK, (k + 1) * BLK)
            isel_ref[lanes, at] = iline_ref[pl.ds(2 * k * BLK + n, BLK, stride=2), :].T.astype(bf16)


def change_block(isel_ref, screened_ref, cells_ref, new_ref, g):
    picked = isel_ref[:ROWS, g // 2 * BLK:(g // 2 + 1) * BLK]
    none = jnp.zeros((NNZ, 2 * BLK), bf16)
    rows = [none, screened_ref[g]] if g % 2 else [screened_ref[g], none]
    change = dot(picked, jnp.concatenate(rows, axis=0))
    at = slice(g * BLK, (g + 1) * BLK)
    for p in range(2):
        new_ref[p, :, at] = cells_ref[p, :, at].astype(f32) + change[:M, p * BLK:(p + 1) * BLK]


def gain_kernel(core_ref, psel_ref, isel_ref, full_ref, mine_ref, theirs_ref, params_ref, screened_ref, out_ref, cols_ref, maps_ref, sems):
    refs = [full_ref] + [mine_ref.at[r] for r in range(SYS - 1)] + [theirs_ref.at[r] for r in range(SYS - 1)]
    copies = [pltpu.make_async_copy(ref, maps_ref.at[r], sems.at[r]) for r, ref in enumerate(refs)]
    opening = pl.program_id(0) == 0

    @pl.when(opening)
    def _():
        for copy in copies:
            copy.start()

    x = psel_ref[...]
    sd = x[:, M:M + 1].astype(f32)
    weight = 1.0 / (sd * sd)
    x = jnp.concatenate([x, x], axis=1)

    for some in (range(4), range(4, 10), range(10, MAPS)):
        @pl.when(opening)
        def _():
            for r in some:
                copies[r].wait()

        for r in some:
            total = (dot(x, maps_ref[r]) * weight).astype(bf16)
            for g in range(GROUP):
                cols_ref[g, r * NNZ:(r + 1) * NNZ, :] = total[g * NNZ:(g + 1) * NNZ]

    def gains(g, carry):
        at = pl.ds(pl.multiple_of(g * BLK, BLK), BLK)
        cells = jnp.concatenate([params_ref[0, :, at], params_ref[1, :, at]], axis=1)
        every = dot(cols_ref[g][:, :M], cells)
        full = every[:NNZ]
        spread = jnp.zeros_like(full)
        for r in range(1, MAPS):
            off = every[r * NNZ:(r + 1) * NNZ] - full
            spread = spread + off * off
        squared = full * full
        screened_ref[g] = (squared / (squared + spread * (1.0 / NB) + screen_floor) * full).astype(bf16)
        return carry

    lax.fori_loop(0, GROUP, gains, 0, unroll=GROUP)
    for g in range(GROUP):
        change_block(isel_ref, screened_ref, params_ref, out_ref, g)


def change_kernel(half_ref, all_ref, theirs_ref, params_ref, so_far_ref, out_ref, isel_ref, screened_ref, cells_ref, new_ref, sems, in_sems, out_sems):
    blocks = screened_ref.shape[0]
    width = GROUP * BLK
    steps = blocks // GROUP
    start = pl.multiple_of(half_ref[0] * (blocks * BLK), BLK)

    def here(n):
        return pl.ds(n * width, width)

    def there(n):
        return pl.ds(pl.multiple_of(start + n * width, BLK), width)

    def bring(n, p):
        return pltpu.make_async_copy(params_ref.at[p, :, there(n)], cells_ref.at[p, :, here(n)], in_sems.at[n, p])

    def send(n, p):
        return pltpu.make_async_copy(new_ref.at[p, :, here(n)], out_ref.at[p, :, there(n)], out_sems.at[n, p])

    at = pl.ds(pl.multiple_of(half_ref[0] * (blocks * NNZ), BLK), blocks * NNZ)
    both = [
        pltpu.make_async_copy(all_ref.at[:, at], isel_ref, sems.at[0]),
        pltpu.make_async_copy(theirs_ref, screened_ref, sems.at[1]),
    ]
    for copy in both:
        copy.start()
    for n in range(steps):
        for p in range(2):
            bring(n, p).start()
    for copy in both:
        copy.wait()
    for n in range(steps):
        for p in range(2):
            bring(n, p).wait()
        for g in range(n * GROUP, (n + 1) * GROUP):
            change_block(isel_ref, screened_ref, cells_ref, new_ref, g)
        for p in range(2):
            send(n, p).start()
    for n in range(steps):
        for p in range(2):
            send(n, p).wait()


vmem = pl.BlockSpec(memory_space=pltpu.VMEM)
smem = pl.BlockSpec(memory_space=pltpu.SMEM)
hbm = pl.BlockSpec(memory_space=pl.ANY)
limit = pltpu.CompilerParams(vmem_limit_bytes=64 * 1024 * 1024)


def pack(core, predicted, perturbation, observed, obs_sd, slabs):
    whole = jax.ShapeDtypeStruct((slabs, ROWS, BLK), bf16)
    return pl.pallas_call(
        pack_kernel,
        out_shape=whole,
        in_specs=[smem, vmem, vmem, vmem, vmem],
        out_specs=vmem,
        compiler_params=limit,
        name="pack",
    )(core, predicted, perturbation, observed[None], obs_sd[None])


def make_maps(core, block_map, own, other, near, far):
    blocks = block_map.shape[0]
    data = own.shape[0] * BLK
    return pl.pallas_call(
        map_kernel,
        out_shape=(
            jax.ShapeDtypeStruct((2 * MP, MP), bf16),
            jax.ShapeDtypeStruct((SYS - 1, 2 * MP, MP), bf16),
            jax.ShapeDtypeStruct((blocks * NNZ, BLK), f32),
            jax.ShapeDtypeStruct((2 * blocks * NNZ, BLK), f32),
        ),
        in_specs=[smem, hbm, hbm, hbm, vmem, vmem],
        out_specs=(hbm, hbm, hbm, hbm),
        scratch_shapes=[
            pltpu.VMEM((data, MP), bf16),
            pltpu.VMEM((2, ROWS, data), bf16),
            pltpu.VMEM((2 * data, BLK), f32),
            pltpu.VMEM((2 * data, BLK), f32),
            pltpu.VMEM((blocks * NNZ, BLK), f32),
            pltpu.VMEM((2 * blocks * NNZ, BLK), f32),
            pltpu.VMEM((SYS, M, MP), f32),
            pltpu.VMEM(own.shape, bf16),
            pltpu.VMEM(own.shape, bf16),
            pltpu.SMEM(block_map.shape, jnp.int32),
            pltpu.SemaphoreType.DMA((2 * PARTS + 1,)),
            pltpu.VMEM((SYS, 2 * MP, MP), bf16),
            pltpu.SemaphoreType.DMA((SYS + 2,)),
        ] + [pltpu.VMEM((M, MP), f32)] * SYS,
        compiler_params=limit,
        cost_estimate=pl.CostEstimate(flops=20_000_000_000, bytes_accessed=8_000_000, transcendentals=0),
        name="maps",
    )(core, block_map, own, other, near, far)


def arrange(pline, iline):
    steps = 4
    prows, irows = pline.shape[0] // steps, iline.shape[0] // steps
    return pl.pallas_call(
        arrange_kernel,
        out_shape=(
            jax.ShapeDtypeStruct((pline.shape[0] // 2, MP), bf16),
            jax.ShapeDtypeStruct((MP, iline.shape[0] // 2), bf16),
        ),
        grid=(steps,),
        in_specs=[pl.BlockSpec((prows, BLK), lambda i: (i, 0)), pl.BlockSpec((irows, BLK), lambda i: (i, 0))],
        out_specs=(
            pl.BlockSpec((prows // 2, MP), lambda i: (i, 0)),
            pl.BlockSpec((MP, irows // 2), lambda i: (0, i)),
        ),
        compiler_params=limit,
        cost_estimate=pl.CostEstimate(flops=6_000_000_000, bytes_accessed=9_000_000, transcendentals=0),
        name="arrange",
    )(pline, iline)


def screen(core, psel, isel, full, mine, theirs, params):
    blocks = params.shape[2] // BLK // 2
    steps = blocks // GROUP
    cells = pl.BlockSpec((2, M, GROUP * BLK), lambda i, c: (0, 0, c[0] * steps + i))
    rows = pl.BlockSpec((GROUP * NNZ, MP), lambda i, c: (i, 0))
    return pl.pallas_call(
        gain_kernel,
        out_shape=(
            jax.ShapeDtypeStruct((blocks, NNZ, 2 * BLK), bf16),
            jax.ShapeDtypeStruct(params.shape, f32),
        ),
        grid_spec=pltpu.PrefetchScalarGridSpec(
            num_scalar_prefetch=1,
            grid=(steps,),
            in_specs=[rows, pl.BlockSpec((MP, GROUP * NNZ), lambda i, c: (0, c[0] * steps + i)), hbm, hbm, hbm, cells],
            out_specs=(pl.BlockSpec((GROUP, NNZ, 2 * BLK), lambda i, c: (i, 0, 0)), cells),
            scratch_shapes=[
                pltpu.VMEM((GROUP, MAPS * NNZ, MP), bf16),
                pltpu.VMEM((MAPS, 2 * MP, MP), bf16),
                pltpu.SemaphoreType.DMA((MAPS,)),
            ],
        ),
        compiler_params=limit,
        cost_estimate=pl.CostEstimate(flops=20_000_000_000, bytes_accessed=16_000_000, transcendentals=0),
        name="gains",
    )(core, psel, isel, full, mine, theirs, params)


def update(half, isel, screened, params, so_far):
    blocks = screened.shape[0]
    steps = blocks // GROUP
    return pl.pallas_call(
        change_kernel,
        out_shape=jax.ShapeDtypeStruct(params.shape, f32),
        in_specs=[smem, hbm, hbm, hbm, hbm],
        out_specs=hbm,
        scratch_shapes=[
            pltpu.VMEM((MP, blocks * NNZ), bf16),
            pltpu.VMEM(screened.shape, bf16),
            pltpu.VMEM((2, M, blocks * BLK), bf16),
            pltpu.VMEM((2, M, blocks * BLK), f32),
            pltpu.SemaphoreType.DMA((2,)),
            pltpu.SemaphoreType.DMA((steps, 2)),
            pltpu.SemaphoreType.DMA((steps, 2)),
        ],
        input_output_aliases={4: 0},
        compiler_params=limit,
        cost_estimate=pl.CostEstimate(flops=5_000_000_000, bytes_accessed=10_000_000, transcendentals=0),
        name="change",
    )(half, isel, screened, params, so_far)


def on_device(params, predicted, perturbation, observed, obs_sd, members, block_map):
    boot = lax.axis_index("boot")
    core = lax.rem(boot, 2)
    core_arg = core.reshape(1).astype(jnp.int32)
    slabs = lax.axis_size("slab")
    pair = [(i, i ^ 1) for i in range(4)]
    far = [(i, i ^ 2) for i in range(4)]

    whole = pack(core_arg, predicted, perturbation, observed, obs_sd, slabs)
    own = lax.all_to_all(whole, "slab", 0, 0)
    own, late_members = lax.optimization_barrier((own, members))
    far_members = lax.ppermute(late_members, "boot", far)
    other = lax.ppermute(own, "boot", pair)

    full, mine, pline, iline = make_maps(core_arg, block_map, own, other, members, far_members)
    theirs = lax.ppermute(mine, "boot", pair)
    psel, isel = arrange(pline, iline)
    screened, so_far = screen(core_arg, psel, isel, full, mine, theirs, params)
    screened_other = lax.ppermute(screened, "boot", pair)
    return update(1 - core_arg, isel, screened_other, params, so_far)


def solution(mesh):
    return jax.shard_map(
        on_device,
        mesh=mesh,
        in_specs=(
            P(None, None, "slab"),
            P(None, "slab"),
            P(None, "slab"),
            P("slab"),
            P("slab"),
            P("boot", None),
            P("slab", None),
        ),
        out_specs=P(None, None, "slab"),
        check_vma=False,
    )
```

```python
from functools import partial
import math

import jax
import jax.numpy as jnp
from jax import lax
from jax.experimental import pallas as pl
from jax.experimental.pallas import tpu as pltpu
from jax.sharding import PartitionSpec as P

M = 200
NB = 16
BLK = 128
NNZ = 64
MP = 256
ROWS = 208
PIV = 40
SYS = 9
PARTS = 4
PACK = 3
MAPS = 17
GROUP = 8

screen_floor = 1e-05
f32 = jnp.float32
bf16 = jnp.bfloat16


def iota(shape, dim):
    return lax.broadcasted_iota(jnp.int32, shape, dim)


def split3(x):
    hi = x.astype(bf16).astype(f32)
    rest = x - hi
    mid = rest.astype(bf16).astype(f32)
    return hi, mid, rest - mid


def lhs6(c):
    hi, mid, lo = split3(c)
    left = hi + pltpu.roll(hi, PIV, 1) + pltpu.roll(hi, 2 * PIV, 1)
    right = mid + pltpu.roll(mid, PIV, 1) + pltpu.roll(lo, 2 * PIV, 1)
    return jnp.concatenate([left, right], axis=1).astype(bf16)


def rhs6(r):
    hi, mid, lo = split3(r)
    pad = jnp.zeros((BLK - 3 * PIV, MP), f32)
    return jnp.concatenate([hi, mid, lo, pad, hi, mid, hi, pad], axis=0).astype(bf16)


def dot(a, b):
    return jnp.dot(a, b, preferred_element_type=f32)


def scaling(listed):
    lane = iota((M, MP), 1)
    if listed is None:
        down = jnp.ones((M, 1), f32)
        across = jnp.where(lane[:1] < M, 1.0, 0.0)
    else:
        down = jnp.sqrt(jnp.sum(jnp.where(iota((M, M), 0) == listed, 1.0, 0.0), axis=1, keepdims=True))
        across = jnp.sum(jnp.where(iota((M, MP), 0) == lane, down, 0.0), axis=0, keepdims=True)
    root = 1.0 / math.sqrt(M)
    return down * (1.0 / (M - 1)) * across, down * root, across * root


def pack_kernel(core_ref, pred_ref, pert_ref, obs_ref, sd_ref, out_ref):
    sd = sd_ref[...].astype(f32)
    ens = pred_ref[...].astype(f32)
    innov = obs_ref[...].astype(f32) + sd * pert_ref[...].astype(f32) - ens
    rows = jnp.where(core_ref[0] == 0, ens, innov)
    tail = jnp.concatenate([sd, jnp.zeros((ROWS - M - 1, BLK), f32)], axis=0)
    part = jnp.concatenate([rows, tail], axis=0).astype(bf16)
    for i in range(out_ref.shape[0]):
        out_ref[i] = part


def gathered(own_first, own_ref, other_ref, ens_ref, innov_ref, map_ref, index_ref, sems):
    step = ens_ref.shape[0] // PARTS

    def copy(source, target, n):
        at = pl.ds(n % PARTS * step, step)
        return pltpu.make_async_copy(source.at[at], target.at[at], sems.at[n])

    def start(first_ref, second_ref):
        for n in range(PARTS):
            copy(first_ref, ens_ref, n).start()
        index_copy.start()
        for n in range(PARTS):
            copy(second_ref, innov_ref, PARTS + n).start()

    index_copy = pltpu.make_async_copy(map_ref, index_ref, sems.at[2 * PARTS])

    @pl.when(own_first)
    def _():
        start(own_ref, other_ref)

    @pl.when(jnp.logical_not(own_first))
    def _():
        start(other_ref, own_ref)

    def wait(n):
        if n == 2 * PARTS:
            index_copy.wait()
        else:
            copy(own_ref, ens_ref if n < PARTS else innov_ref, n).wait()

    return wait


def chunk_rows(rows_ref, i):
    rows = rows_ref[i].astype(f32)
    high = jnp.concatenate([rows[BLK:], jnp.zeros((MP - ROWS, BLK), f32)], axis=0)
    return rows, rows[:BLK], high


def by_parts(count, first, wait, chunk):
    step = count // PARTS
    for n in range(PARTS):
        wait(first + n)
        lax.fori_loop(n * step, (n + 1) * step, chunk, 0, unroll=4)


def fill_table(t_ref, i, low, high):
    base = pl.multiple_of(i * (2 * BLK), 8)
    t_ref[pl.ds(base, BLK, stride=2), :] = low
    t_ref[pl.ds(base + 1, BLK, stride=2), :] = high


def along(tile, u):
    return jnp.broadcast_to(tile[u:u + 1], tile.shape)


def inverse_of(x):
    guess = pl.reciprocal(x, approx=True)
    guess = guess * (2.0 - x * guess)
    return guess * (2.0 - x * guess)


def map_kernel(
    core_ref, map_ref, own_ref, other_ref, near_ref, far_ref, full_ref, res_ref, psel_ref, isel_ref,
    ens_ref, parts_ref, ptab_ref, itab_ref, pline_ref, iline_ref, scale_ref, rows_ref, late_ref, index_ref,
    sems, maps_ref, out_sems, *sys_refs
):
    core = core_ref[0]
    blocks = map_ref.shape[0]
    wait = gathered(core == 0, own_ref, other_ref, rows_ref, late_ref, map_ref, index_ref, sems)
    near = near_ref.shape[0]

    def chunk(i, carry):
        rows, low, high = chunk_rows(rows_ref, i)
        sd = rows[M:M + 1]
        at = pl.ds(pl.multiple_of(i * BLK, BLK), BLK)
        for n, part in enumerate(split3(rows * (1.0 / (sd * sd)))[:2]):
            parts_ref[n, :, at] = part.astype(bf16)
        low, high = low.T, high.T
        ens_ref[at, :] = jnp.concatenate([low, high], axis=1).astype(bf16)
        fill_table(ptab_ref, i, low, high)
        return carry

    by_parts(rows_ref.shape[0], 0, wait, chunk)

    def late_chunk(i, carry):
        _, low, high = chunk_rows(late_ref, i)
        fill_table(itab_ref, i, low.T, high.T)
        return carry

    by_parts(late_ref.shape[0], PARTS, wait, late_chunk)
    wait(2 * PARTS)

    gram = 0.0
    for n in (1, 0):
        gram = gram + dot(parts_ref[n], ens_ref[...])
    gram = gram[:M]

    ipanel = -(-blocks // (M // PIV))
    ppanel = -(-(blocks // 2) // (M // PIV))
    share = -(-(ipanel + ppanel) * NNZ // PIV)

    def pick(kp, t):
        for n in range(t * share, min((t + 1) * share, (ipanel + ppanel) * NNZ)):
            b, j = n // NNZ, n % NNZ
            if b < ipanel:
                k = jnp.minimum(kp * ipanel + b, blocks - 1)
                at = index_ref[k, j]
                iline_ref[pl.ds(k * (2 * NNZ) + 2 * j, 2), :] = itab_ref[pl.ds(2 * at, 2), :]
            else:
                k = jnp.minimum(kp * ppanel + b - ipanel, blocks // 2 - 1)
                at = index_ref[core * (blocks // 2) + k, j]
                pline_ref[pl.ds(k * (2 * NNZ) + 2 * j, 2), :] = ptab_ref[pl.ds(2 * at, 2), :]

    row = iota((M, MP), 0)
    lane = iota((M, MP), 1)
    for s in range(SYS):
        listed = None
        if s:
            listed = near_ref[s - 1:s, :] if s <= near else far_ref[s - 1 - near:s - near, :]
        scale, ud, ua = scaling(listed)
        scale_ref[s] = scale
        h = gram * scale
        hu = jnp.sum(h * ua, axis=1, keepdims=True)
        uh = jnp.sum(h * ud, axis=0, keepdims=True)
        uhu = jnp.sum(hu * ud, axis=0, keepdims=True)
        h = h - ud * (uh - 0.5 * uhu * ua) - (hu - 0.5 * uhu * ud) * ua
        sys_refs[s][...] = h + jnp.where(row == lane, 1.0, 0.0)

    prow = iota((PIV, MP), 0)
    plane = iota((PIV, MP), 1)
    dlane = iota((PIV, BLK), 1)
    trow = iota((8, BLK), 0)
    tlane = iota((8, BLK), 1)
    first = jnp.minimum(tlane // PIV, PACK - 1) * PIV
    inner = tlane - first

    def panel_step(kp, carry):
        k0 = kp * PIV
        at = pl.ds(pl.multiple_of(k0, 8), PIV)
        packs = []
        for g in range(SYS // PACK):
            pack = jnp.zeros((PIV, BLK), f32)
            for q in range(PACK):
                moved = pltpu.roll(sys_refs[PACK * g + q][at, :], lax.rem(MP - k0 + q * PIV, MP), 1)[:, :BLK]
                pack = jnp.where((dlane >= q * PIV) & (dlane < (q + 1) * PIV), moved, pack)
            packs.append(pack)
        starts = packs
        tiles = [[pack[8 * i:8 * i + 8] for i in range(PIV // 8)] for pack in packs]
        for j in range(PIV // 8):
            cols = [
                [[jnp.take_along_axis(tile, first + 8 * j + u, axis=1) for u in range(8)] for tile in group]
                for group in tiles
            ]
            for u in range(8):
                at_lane = inner == 8 * j + u
                for group, col in zip(tiles, cols):
                    lead = col[j][u]
                    scale = inverse_of(along(lead, u))
                    t = group[j]
                    line = jnp.where(at_lane, 1.0, along(t, u)) * scale
                    group[j] = jnp.where(trow == u, line, jnp.where(at_lane, 0.0, t) - lead * line)
                    for v in range(u + 1, 8):
                        c = col[j][v]
                        line = along(c, u) * scale
                        col[j][v] = jnp.where(trow == u, line, c - lead * line)
                pick(kp, 8 * j + u)
            done = (inner >= 8 * j) & (inner < 8 * j + 8)
            for group, col in zip(tiles, cols):
                for i in range(PIV // 8):
                    if i != j:
                        tile = jnp.where(done, 0.0, group[i])
                        for u in range(8):
                            tile = tile - col[i][u] * group[j][u:u + 1]
                        group[i] = tile
        packs = [jnp.concatenate(group, axis=0) for group in tiles]
        inside = (lane >= k0) & (lane < k0 + PIV)
        pad = jnp.zeros((BLK - 3 * PIV, MP), f32)
        inverses, blocks_, panels, wanted, lines = [], [], [], [], []
        for s in range(SYS):
            back = (BLK - (s % PACK) * PIV) % BLK
            for kept, source in ((inverses, packs), (blocks_, starts)):
                moved = source[s // PACK]
                if back:
                    moved = pltpu.roll(moved, back, 1)
                kept.append(lhs6(jnp.where(dlane < PIV, moved, 0.0)))
            panels.append(sys_refs[s][at, :])
            wanted.append(jnp.where(plane == prow + k0, -1.0, jnp.where(inside[:PIV], 0.0, panels[s])))
        for s in range(SYS):
            lines.append(dot(inverses[s], rhs6(wanted[s])))
        for s in range(SYS):
            lines[s] = lines[s] + dot(inverses[s], rhs6(wanted[s] - dot(blocks_[s], rhs6(lines[s]))))
        for s in range(SYS):
            hi, mid, lo = split3(panels[s])
            left = jnp.concatenate([hi, hi, hi, pad, mid, mid, lo, pad], axis=0).astype(bf16)
            change = lax.dot_general(left, rhs6(lines[s]), (((0,), (0,)), ((), ())), preferred_element_type=f32)
            sys_refs[s][...] = jnp.where(inside, 0.0, sys_refs[s][...]) - change[:M]
            sys_refs[s][at, :] = lines[s]
        return carry

    lax.fori_loop(0, M // PIV, panel_step, 0)

    outs = [
        pltpu.make_async_copy(pline_ref, psel_ref, out_sems.at[SYS]),
        pltpu.make_async_copy(iline_ref, isel_ref, out_sems.at[SYS + 1]),
    ]
    for copy in outs:
        copy.start()
    for s in range(SYS):
        scale = scale_ref[s]
        value = (-sys_refs[s][...] - scale * ((M - 1) / M)) * scale
        value = jnp.concatenate([value, jnp.zeros((MP - M, MP), f32)], axis=0)
        hi = value.astype(bf16)
        maps_ref[s] = jnp.concatenate([hi, (value - hi.astype(f32)).astype(bf16)], axis=0)
        outs.append(pltpu.make_async_copy(maps_ref.at[s], res_ref.at[s - 1] if s else full_ref, out_sems.at[s]))
        outs[-1].start()
    for copy in outs:
        copy.wait()


def arrange_kernel(pline_ref, iline_ref, psel_ref, isel_ref):
    for n in range(2):
        lanes = slice(n * BLK, (n + 1) * BLK)
        psel_ref[:, lanes] = pline_ref[pl.ds(n, psel_ref.shape[0], stride=2), :].astype(bf16)
        for k in range(isel_ref.shape[1] // BLK):
            at = slice(k * BLK, (k + 1) * BLK)
            isel_ref[lanes, at] = iline_ref[pl.ds(2 * k * BLK + n, BLK, stride=2), :].T.astype(bf16)


def change_block(isel_ref, screened_ref, cells_ref, new_ref, g):
    picked = isel_ref[:ROWS, g // 2 * BLK:(g // 2 + 1) * BLK]
    none = jnp.zeros((NNZ, 2 * BLK), bf16)
    rows = [none, screened_ref[g]] if g % 2 else [screened_ref[g], none]
    change = dot(picked, jnp.concatenate(rows, axis=0))
    at = slice(g * BLK, (g + 1) * BLK)
    for p in range(2):
        new_ref[p, :, at] = cells_ref[p, :, at].astype(f32) + change[:M, p * BLK:(p + 1) * BLK]


def gain_kernel(core_ref, psel_ref, isel_ref, full_ref, mine_ref, theirs_ref, params_ref, screened_ref, out_ref, cols_ref, maps_ref, sems):
    refs = [full_ref] + [mine_ref.at[r] for r in range(SYS - 1)] + [theirs_ref.at[r] for r in range(SYS - 1)]
    copies = [pltpu.make_async_copy(ref, maps_ref.at[r], sems.at[r]) for r, ref in enumerate(refs)]
    opening = pl.program_id(0) == 0

    @pl.when(opening)
    def _():
        for copy in copies:
            copy.start()

    x = psel_ref[...]
    sd = x[:, M:M + 1].astype(f32)
    weight = 1.0 / (sd * sd)
    x = jnp.concatenate([x, x], axis=1)

    for some in (range(4), range(4, 10), range(10, MAPS)):
        @pl.when(opening)
        def _():
            for r in some:
                copies[r].wait()

        for r in some:
            total = (dot(x, maps_ref[r]) * weight).astype(bf16)
            for g in range(GROUP):
                cols_ref[g, r * NNZ:(r + 1) * NNZ, :] = total[g * NNZ:(g + 1) * NNZ]

    def gains(g, carry):
        at = pl.ds(pl.multiple_of(g * BLK, BLK), BLK)
        cells = jnp.concatenate([params_ref[0, :, at], params_ref[1, :, at]], axis=1)
        every = dot(cols_ref[g][:, :M], cells)
        full = every[:NNZ]
        spread = jnp.zeros_like(full)
        for r in range(1, MAPS):
            off = every[r * NNZ:(r + 1) * NNZ] - full
            spread = spread + off * off
        squared = full * full
        screened_ref[g] = (squared / (squared + spread * (1.0 / NB) + screen_floor) * full).astype(bf16)
        return carry

    lax.fori_loop(0, GROUP, gains, 0, unroll=GROUP)
    for g in range(GROUP):
        change_block(isel_ref, screened_ref, params_ref, out_ref, g)


def change_kernel(half_ref, all_ref, theirs_ref, params_ref, so_far_ref, out_ref, isel_ref, screened_ref, cells_ref, new_ref, sems, in_sems, out_sems):
    blocks = screened_ref.shape[0]
    width = GROUP * BLK
    steps = blocks // GROUP
    start = pl.multiple_of(half_ref[0] * (blocks * BLK), BLK)

    def here(n):
        return pl.ds(n * width, width)

    def there(n):
        return pl.ds(pl.multiple_of(start + n * width, BLK), width)

    def bring(n, p):
        return pltpu.make_async_copy(params_ref.at[p, :, there(n)], cells_ref.at[p, :, here(n)], in_sems.at[n, p])

    def send(n, p):
        return pltpu.make_async_copy(new_ref.at[p, :, here(n)], out_ref.at[p, :, there(n)], out_sems.at[n, p])

    at = pl.ds(pl.multiple_of(half_ref[0] * (blocks * NNZ), BLK), blocks * NNZ)
    both = [
        pltpu.make_async_copy(all_ref.at[:, at], isel_ref, sems.at[0]),
        pltpu.make_async_copy(theirs_ref, screened_ref, sems.at[1]),
    ]
    for copy in both:
        copy.start()
    for n in range(steps):
        for p in range(2):
            bring(n, p).start()
    for copy in both:
        copy.wait()
    for n in range(steps):
        for p in range(2):
            bring(n, p).wait()
        for g in range(n * GROUP, (n + 1) * GROUP):
            change_block(isel_ref, screened_ref, cells_ref, new_ref, g)
        for p in range(2):
            send(n, p).start()
    for n in range(steps):
        for p in range(2):
            send(n, p).wait()


vmem = pl.BlockSpec(memory_space=pltpu.VMEM)
smem = pl.BlockSpec(memory_space=pltpu.SMEM)
hbm = pl.BlockSpec(memory_space=pl.ANY)
limit = pltpu.CompilerParams(vmem_limit_bytes=62 * 1024 * 1024)
whole_limit = pltpu.CompilerParams(vmem_limit_bytes=64 * 1024 * 1024)


def pack(core, predicted, perturbation, observed, obs_sd, slabs):
    whole = jax.ShapeDtypeStruct((slabs, ROWS, BLK), bf16)
    return pl.pallas_call(
        pack_kernel,
        out_shape=whole,
        in_specs=[smem, vmem, vmem, vmem, vmem],
        out_specs=vmem,
        compiler_params=limit,
        name="pack",
    )(core, predicted, perturbation, observed[None], obs_sd[None])


def make_maps(core, block_map, own, other, near, far):
    blocks = block_map.shape[0]
    data = own.shape[0] * BLK
    return pl.pallas_call(
        map_kernel,
        out_shape=(
            jax.ShapeDtypeStruct((2 * MP, MP), bf16),
            jax.ShapeDtypeStruct((SYS - 1, 2 * MP, MP), bf16),
            jax.ShapeDtypeStruct((blocks * NNZ, BLK), f32),
            jax.ShapeDtypeStruct((2 * blocks * NNZ, BLK), f32),
        ),
        in_specs=[smem, hbm, hbm, hbm, vmem, vmem],
        out_specs=(hbm, hbm, hbm, hbm),
        scratch_shapes=[
            pltpu.VMEM((data, MP), bf16),
            pltpu.VMEM((2, ROWS, data), bf16),
            pltpu.VMEM((2 * data, BLK), f32),
            pltpu.VMEM((2 * data, BLK), f32),
            pltpu.VMEM((blocks * NNZ, BLK), f32),
            pltpu.VMEM((2 * blocks * NNZ, BLK), f32),
            pltpu.VMEM((SYS, M, MP), f32),
            pltpu.VMEM(own.shape, bf16),
            pltpu.VMEM(own.shape, bf16),
            pltpu.SMEM(block_map.shape, jnp.int32),
            pltpu.SemaphoreType.DMA((2 * PARTS + 1,)),
            pltpu.VMEM((SYS, 2 * MP, MP), bf16),
            pltpu.SemaphoreType.DMA((SYS + 2,)),
        ] + [pltpu.VMEM((M, MP), f32)] * SYS,
        compiler_params=limit,
        cost_estimate=pl.CostEstimate(flops=20_000_000_000, bytes_accessed=8_000_000, transcendentals=0),
        name="maps",
    )(core, block_map, own, other, near, far)


def arrange(pline, iline):
    steps = 4
    prows, irows = pline.shape[0] // steps, iline.shape[0] // steps
    return pl.pallas_call(
        arrange_kernel,
        out_shape=(
            jax.ShapeDtypeStruct((pline.shape[0] // 2, MP), bf16),
            jax.ShapeDtypeStruct((MP, iline.shape[0] // 2), bf16),
        ),
        grid=(steps,),
        in_specs=[pl.BlockSpec((prows, BLK), lambda i: (i, 0)), pl.BlockSpec((irows, BLK), lambda i: (i, 0))],
        out_specs=(
            pl.BlockSpec((prows // 2, MP), lambda i: (i, 0)),
            pl.BlockSpec((MP, irows // 2), lambda i: (0, i)),
        ),
        compiler_params=limit,
        cost_estimate=pl.CostEstimate(flops=6_000_000_000, bytes_accessed=9_000_000, transcendentals=0),
        name="arrange",
    )(pline, iline)


def screen(core, psel, isel, full, mine, theirs, params):
    blocks = params.shape[2] // BLK // 2
    steps = blocks // GROUP
    cells = pl.BlockSpec((2, M, GROUP * BLK), lambda i, c: (0, 0, c[0] * steps + i))
    rows = pl.BlockSpec((GROUP * NNZ, MP), lambda i, c: (i, 0))
    return pl.pallas_call(
        gain_kernel,
        out_shape=(
            jax.ShapeDtypeStruct((blocks, NNZ, 2 * BLK), bf16),
            jax.ShapeDtypeStruct(params.shape, f32),
        ),
        grid_spec=pltpu.PrefetchScalarGridSpec(
            num_scalar_prefetch=1,
            grid=(steps,),
            in_specs=[rows, pl.BlockSpec((MP, GROUP * NNZ), lambda i, c: (0, c[0] * steps + i)), hbm, hbm, hbm, cells],
            out_specs=(pl.BlockSpec((GROUP, NNZ, 2 * BLK), lambda i, c: (i, 0, 0)), cells),
            scratch_shapes=[
                pltpu.VMEM((GROUP, MAPS * NNZ, MP), bf16),
                pltpu.VMEM((MAPS, 2 * MP, MP), bf16),
                pltpu.SemaphoreType.DMA((MAPS,)),
            ],
        ),
        compiler_params=limit,
        cost_estimate=pl.CostEstimate(flops=20_000_000_000, bytes_accessed=16_000_000, transcendentals=0),
        name="gains",
    )(core, psel, isel, full, mine, theirs, params)


def update(half, isel, screened, params, so_far):
    blocks = screened.shape[0]
    steps = blocks // GROUP
    return pl.pallas_call(
        change_kernel,
        out_shape=jax.ShapeDtypeStruct(params.shape, f32),
        in_specs=[smem, hbm, hbm, hbm, hbm],
        out_specs=hbm,
        scratch_shapes=[
            pltpu.VMEM((MP, blocks * NNZ), bf16),
            pltpu.VMEM(screened.shape, bf16),
            pltpu.VMEM((2, M, blocks * BLK), bf16),
            pltpu.VMEM((2, M, blocks * BLK), f32),
            pltpu.SemaphoreType.DMA((2,)),
            pltpu.SemaphoreType.DMA((steps, 2)),
            pltpu.SemaphoreType.DMA((steps, 2)),
        ],
        input_output_aliases={4: 0},
        compiler_params=whole_limit,
        cost_estimate=pl.CostEstimate(flops=5_000_000_000, bytes_accessed=10_000_000, transcendentals=0),
        name="change",
    )(half, isel, screened, params, so_far)


def on_device(params, predicted, perturbation, observed, obs_sd, members, block_map):
    boot = lax.axis_index("boot")
    core = lax.rem(boot, 2)
    core_arg = core.reshape(1).astype(jnp.int32)
    slabs = lax.axis_size("slab")
    pair = [(i, i ^ 1) for i in range(4)]
    far = [(i, i ^ 2) for i in range(4)]

    whole = pack(core_arg, predicted, perturbation, observed, obs_sd, slabs)
    own = lax.all_to_all(whole, "slab", 0, 0)
    own, late_members = lax.optimization_barrier((own, members))
    far_members = lax.ppermute(late_members, "boot", far)
    other = lax.ppermute(own, "boot", pair)

    full, mine, pline, iline = make_maps(core_arg, block_map, own, other, members, far_members)
    theirs = lax.ppermute(mine, "boot", pair)
    psel, isel = arrange(pline, iline)
    screened, so_far = screen(core_arg, psel, isel, full, mine, theirs, params)
    screened_other = lax.ppermute(screened, "boot", pair)
    return update(1 - core_arg, isel, screened_other, params, so_far)


def solution(mesh):
    return jax.shard_map(
        on_device,
        mesh=mesh,
        in_specs=(
            P(None, None, "slab"),
            P(None, "slab"),
            P(None, "slab"),
            P("slab"),
            P("slab"),
            P("boot", None),
            P("slab", None),
        ),
        out_specs=P(None, None, "slab"),
        check_vma=False,
    )
```

```python
from functools import partial
import math

import jax
import jax.numpy as jnp
from jax import lax
from jax.experimental import pallas as pl
from jax.experimental.pallas import tpu as pltpu
from jax.sharding import PartitionSpec as P

M = 200
NB = 16
BLK = 128
NNZ = 64
MP = 256
ROWS = 208
PIV = 40
SYS = 9
PARTS = 4
PACK = 3
MAPS = 17
GROUP = 8

screen_floor = 1e-05
f32 = jnp.float32
bf16 = jnp.bfloat16


def iota(shape, dim):
    return lax.broadcasted_iota(jnp.int32, shape, dim)


def split3(x):
    hi = x.astype(bf16).astype(f32)
    rest = x - hi
    mid = rest.astype(bf16).astype(f32)
    return hi, mid, rest - mid


def lhs6(c):
    hi, mid, lo = split3(c)
    left = hi + pltpu.roll(hi, PIV, 1) + pltpu.roll(hi, 2 * PIV, 1)
    right = mid + pltpu.roll(mid, PIV, 1) + pltpu.roll(lo, 2 * PIV, 1)
    return jnp.concatenate([left, right], axis=1).astype(bf16)


def rhs6(r):
    hi, mid, lo = split3(r)
    pad = jnp.zeros((BLK - 3 * PIV, MP), f32)
    return jnp.concatenate([hi, mid, lo, pad, hi, mid, hi, pad], axis=0).astype(bf16)


def dot(a, b):
    return jnp.dot(a, b, preferred_element_type=f32)


def scaling(listed):
    lane = iota((M, MP), 1)
    if listed is None:
        down = jnp.ones((M, 1), f32)
        across = jnp.where(lane[:1] < M, 1.0, 0.0)
    else:
        down = jnp.sqrt(jnp.sum(jnp.where(iota((M, M), 0) == listed, 1.0, 0.0), axis=1, keepdims=True))
        across = jnp.sum(jnp.where(iota((M, MP), 0) == lane, down, 0.0), axis=0, keepdims=True)
    root = 1.0 / math.sqrt(M)
    return down * (1.0 / (M - 1)) * across, down * root, across * root


def pack_kernel(core_ref, pred_ref, pert_ref, obs_ref, sd_ref, out_ref):
    sd = sd_ref[...].astype(f32)
    ens = pred_ref[...].astype(f32)
    innov = obs_ref[...].astype(f32) + sd * pert_ref[...].astype(f32) - ens
    rows = jnp.where(core_ref[0] == 0, ens, innov)
    tail = jnp.concatenate([sd, jnp.zeros((ROWS - M - 1, BLK), f32)], axis=0)
    part = jnp.concatenate([rows, tail], axis=0).astype(bf16)
    for i in range(out_ref.shape[0]):
        out_ref[i] = part


def gathered(own_first, own_ref, other_ref, ens_ref, innov_ref, map_ref, index_ref, sems):
    step = ens_ref.shape[0] // PARTS

    def copy(source, target, n):
        at = pl.ds(n % PARTS * step, step)
        return pltpu.make_async_copy(source.at[at], target.at[at], sems.at[n])

    def start(first_ref, second_ref):
        for n in range(PARTS):
            copy(first_ref, ens_ref, n).start()
        index_copy.start()
        for n in range(PARTS):
            copy(second_ref, innov_ref, PARTS + n).start()

    index_copy = pltpu.make_async_copy(map_ref, index_ref, sems.at[2 * PARTS])

    @pl.when(own_first)
    def _():
        start(own_ref, other_ref)

    @pl.when(jnp.logical_not(own_first))
    def _():
        start(other_ref, own_ref)

    def wait(n):
        if n == 2 * PARTS:
            index_copy.wait()
        else:
            copy(own_ref, ens_ref if n < PARTS else innov_ref, n).wait()

    return wait


def chunk_rows(rows_ref, i):
    rows = rows_ref[i].astype(f32)
    high = jnp.concatenate([rows[BLK:], jnp.zeros((MP - ROWS, BLK), f32)], axis=0)
    return rows, rows[:BLK], high


def by_parts(count, first, wait, chunk):
    step = count // PARTS
    for n in range(PARTS):
        wait(first + n)
        lax.fori_loop(n * step, (n + 1) * step, chunk, 0, unroll=8)


def fill_table(t_ref, i, low, high):
    base = pl.multiple_of(i * (2 * BLK), 8)
    t_ref[pl.ds(base, BLK, stride=2), :] = low
    t_ref[pl.ds(base + 1, BLK, stride=2), :] = high


def along(tile, u):
    return jnp.broadcast_to(tile[u:u + 1], tile.shape)


def inverse_of(x):
    guess = pl.reciprocal(x, approx=True)
    guess = guess * (2.0 - x * guess)
    return guess * (2.0 - x * guess)


def map_kernel(
    core_ref, map_ref, own_ref, other_ref, near_ref, far_ref, full_ref, res_ref, psel_ref, isel_ref,
    ens_ref, parts_ref, ptab_ref, itab_ref, pline_ref, iline_ref, scale_ref, rows_ref, late_ref, index_ref,
    sems, maps_ref, out_sems, *sys_refs
):
    core = core_ref[0]
    blocks = map_ref.shape[0]
    wait = gathered(core == 0, own_ref, other_ref, rows_ref, late_ref, map_ref, index_ref, sems)
    near = near_ref.shape[0]

    def chunk(i, carry):
        rows, low, high = chunk_rows(rows_ref, i)
        sd = rows[M:M + 1]
        at = pl.ds(pl.multiple_of(i * BLK, BLK), BLK)
        for n, part in enumerate(split3(rows * (1.0 / (sd * sd)))[:2]):
            parts_ref[n, :, at] = part.astype(bf16)
        low, high = low.T, high.T
        ens_ref[at, :] = jnp.concatenate([low, high], axis=1).astype(bf16)
        fill_table(ptab_ref, i, low, high)
        return carry

    by_parts(rows_ref.shape[0], 0, wait, chunk)

    def late_chunk(i, carry):
        _, low, high = chunk_rows(late_ref, i)
        fill_table(itab_ref, i, low.T, high.T)
        return carry

    by_parts(late_ref.shape[0], PARTS, wait, late_chunk)
    wait(2 * PARTS)

    gram = 0.0
    for n in (1, 0):
        gram = gram + dot(parts_ref[n], ens_ref[...])
    gram = gram[:M]

    ipanel = -(-blocks // (M // PIV))
    ppanel = -(-(blocks // 2) // (M // PIV))
    share = -(-(ipanel + ppanel) * NNZ // PIV)

    def pick(kp, t):
        for n in range(t * share, min((t + 1) * share, (ipanel + ppanel) * NNZ)):
            b, j = n // NNZ, n % NNZ
            if b < ipanel:
                k = jnp.minimum(kp * ipanel + b, blocks - 1)
                at = index_ref[k, j]
                iline_ref[pl.ds(k * (2 * NNZ) + 2 * j, 2), :] = itab_ref[pl.ds(2 * at, 2), :]
            else:
                k = jnp.minimum(kp * ppanel + b - ipanel, blocks // 2 - 1)
                at = index_ref[core * (blocks // 2) + k, j]
                pline_ref[pl.ds(k * (2 * NNZ) + 2 * j, 2), :] = ptab_ref[pl.ds(2 * at, 2), :]

    row = iota((M, MP), 0)
    lane = iota((M, MP), 1)
    for s in range(SYS):
        listed = None
        if s:
            listed = near_ref[s - 1:s, :] if s <= near else far_ref[s - 1 - near:s - near, :]
        scale, ud, ua = scaling(listed)
        scale_ref[s] = scale
        h = gram * scale
        hu = jnp.sum(h * ua, axis=1, keepdims=True)
        uh = jnp.sum(h * ud, axis=0, keepdims=True)
        uhu = jnp.sum(hu * ud, axis=0, keepdims=True)
        h = h - ud * (uh - 0.5 * uhu * ua) - (hu - 0.5 * uhu * ud) * ua
        sys_refs[s][...] = h + jnp.where(row == lane, 1.0, 0.0)

    prow = iota((PIV, MP), 0)
    plane = iota((PIV, MP), 1)
    dlane = iota((PIV, BLK), 1)
    trow = iota((8, BLK), 0)
    tlane = iota((8, BLK), 1)
    first = jnp.minimum(tlane // PIV, PACK - 1) * PIV
    inner = tlane - first

    def panel_step(kp, carry):
        k0 = kp * PIV
        at = pl.ds(pl.multiple_of(k0, 8), PIV)
        packs = []
        for g in range(SYS // PACK):
            pack = jnp.zeros((PIV, BLK), f32)
            for q in range(PACK):
                moved = pltpu.roll(sys_refs[PACK * g + q][at, :], lax.rem(MP - k0 + q * PIV, MP), 1)[:, :BLK]
                pack = jnp.where((dlane >= q * PIV) & (dlane < (q + 1) * PIV), moved, pack)
            packs.append(pack)
        starts = packs
        tiles = [[pack[8 * i:8 * i + 8] for i in range(PIV // 8)] for pack in packs]
        for j in range(PIV // 8):
            cols = [
                [[jnp.take_along_axis(tile, first + 8 * j + u, axis=1) for u in range(8)] for tile in group]
                for group in tiles
            ]
            for u in range(8):
                at_lane = inner == 8 * j + u
                for group, col in zip(tiles, cols):
                    lead = col[j][u]
                    scale = inverse_of(along(lead, u))
                    t = group[j]
                    line = jnp.where(at_lane, 1.0, along(t, u)) * scale
                    group[j] = jnp.where(trow == u, line, jnp.where(at_lane, 0.0, t) - lead * line)
                    for v in range(u + 1, 8):
                        c = col[j][v]
                        line = along(c, u) * scale
                        col[j][v] = jnp.where(trow == u, line, c - lead * line)
                pick(kp, 8 * j + u)
            done = (inner >= 8 * j) & (inner < 8 * j + 8)
            for group, col in zip(tiles, cols):
                for i in range(PIV // 8):
                    if i != j:
                        tile = jnp.where(done, 0.0, group[i])
                        for u in range(8):
                            tile = tile - col[i][u] * group[j][u:u + 1]
                        group[i] = tile
        packs = [jnp.concatenate(group, axis=0) for group in tiles]
        inside = (lane >= k0) & (lane < k0 + PIV)
        pad = jnp.zeros((BLK - 3 * PIV, MP), f32)
        inverses, blocks_, panels, wanted, lines = [], [], [], [], []
        for s in range(SYS):
            back = (BLK - (s % PACK) * PIV) % BLK
            for kept, source in ((inverses, packs), (blocks_, starts)):
                moved = source[s // PACK]
                if back:
                    moved = pltpu.roll(moved, back, 1)
                kept.append(lhs6(jnp.where(dlane < PIV, moved, 0.0)))
            panels.append(sys_refs[s][at, :])
            wanted.append(jnp.where(plane == prow + k0, -1.0, jnp.where(inside[:PIV], 0.0, panels[s])))
        for s in range(SYS):
            lines.append(dot(inverses[s], rhs6(wanted[s])))
        offs = [wanted[s] - dot(blocks_[s], rhs6(lines[s])) for s in range(SYS)]
        for s in range(SYS):
            lines[s] = lines[s] + dot(inverses[s], rhs6(offs[s]))
        for s in range(SYS):
            hi, mid, lo = split3(panels[s])
            left = jnp.concatenate([hi, hi, hi, pad, mid, mid, lo, pad], axis=0).astype(bf16)
            change = lax.dot_general(left, rhs6(lines[s]), (((0,), (0,)), ((), ())), preferred_element_type=f32)
            sys_refs[s][...] = jnp.where(inside, 0.0, sys_refs[s][...]) - change[:M]
            sys_refs[s][at, :] = lines[s]
        return carry

    lax.fori_loop(0, M // PIV, panel_step, 0)

    outs = [
        pltpu.make_async_copy(pline_ref, psel_ref, out_sems.at[SYS]),
        pltpu.make_async_copy(iline_ref, isel_ref, out_sems.at[SYS + 1]),
    ]
    for copy in outs:
        copy.start()
    for s in range(SYS):
        scale = scale_ref[s]
        value = (-sys_refs[s][...] - scale * ((M - 1) / M)) * scale
        value = jnp.concatenate([value, jnp.zeros((MP - M, MP), f32)], axis=0)
        hi = value.astype(bf16)
        maps_ref[s] = jnp.concatenate([hi, (value - hi.astype(f32)).astype(bf16)], axis=0)
        outs.append(pltpu.make_async_copy(maps_ref.at[s], res_ref.at[s - 1] if s else full_ref, out_sems.at[s]))
        outs[-1].start()
    for copy in outs:
        copy.wait()


def arrange_kernel(pline_ref, iline_ref, psel_ref, isel_ref):
    for n in range(2):
        lanes = slice(n * BLK, (n + 1) * BLK)
        psel_ref[:, lanes] = pline_ref[pl.ds(n, psel_ref.shape[0], stride=2), :].astype(bf16)
        for k in range(isel_ref.shape[1] // BLK):
            at = slice(k * BLK, (k + 1) * BLK)
            isel_ref[lanes, at] = iline_ref[pl.ds(2 * k * BLK + n, BLK, stride=2), :].T.astype(bf16)


def change_block(isel_ref, screened_ref, cells_ref, new_ref, g):
    picked = isel_ref[:ROWS, g // 2 * BLK:(g // 2 + 1) * BLK]
    none = jnp.zeros((NNZ, 2 * BLK), bf16)
    rows = [none, screened_ref[g]] if g % 2 else [screened_ref[g], none]
    change = dot(picked, jnp.concatenate(rows, axis=0))
    at = slice(g * BLK, (g + 1) * BLK)
    for p in range(2):
        new_ref[p, :, at] = cells_ref[p, :, at].astype(f32) + change[:M, p * BLK:(p + 1) * BLK]


def gain_kernel(core_ref, psel_ref, isel_ref, full_ref, mine_ref, theirs_ref, params_ref, screened_ref, out_ref, cols_ref, maps_ref, sems):
    refs = [full_ref] + [mine_ref.at[r] for r in range(SYS - 1)] + [theirs_ref.at[r] for r in range(SYS - 1)]
    copies = [pltpu.make_async_copy(ref, maps_ref.at[r], sems.at[r]) for r, ref in enumerate(refs)]
    opening = pl.program_id(0) == 0

    @pl.when(opening)
    def _():
        for copy in copies:
            copy.start()

    x = psel_ref[...]
    sd = x[:, M:M + 1].astype(f32)
    weight = 1.0 / (sd * sd)
    x = jnp.concatenate([x, x], axis=1)

    for some in (range(4), range(4, 10), range(10, MAPS)):
        @pl.when(opening)
        def _():
            for r in some:
                copies[r].wait()

        for r in some:
            total = (dot(x, maps_ref[r]) * weight).astype(bf16)
            for g in range(GROUP):
                cols_ref[g, r * NNZ:(r + 1) * NNZ, :] = total[g * NNZ:(g + 1) * NNZ]

    def gains(g, carry):
        at = pl.ds(pl.multiple_of(g * BLK, BLK), BLK)
        cells = jnp.concatenate([params_ref[0, :, at], params_ref[1, :, at]], axis=1)
        every = dot(cols_ref[g][:, :M], cells)
        full = every[:NNZ]
        spread = jnp.zeros_like(full)
        for r in range(1, MAPS):
            off = every[r * NNZ:(r + 1) * NNZ] - full
            spread = spread + off * off
        squared = full * full
        screened_ref[g] = (squared / (squared + spread * (1.0 / NB) + screen_floor) * full).astype(bf16)
        return carry

    lax.fori_loop(0, GROUP, gains, 0, unroll=GROUP)
    for g in range(GROUP):
        change_block(isel_ref, screened_ref, params_ref, out_ref, g)


def change_kernel(half_ref, all_ref, theirs_ref, params_ref, so_far_ref, out_ref, isel_ref, screened_ref, cells_ref, new_ref, sems, in_sems, out_sems):
    blocks = screened_ref.shape[0]
    width = GROUP * BLK
    steps = blocks // GROUP
    start = pl.multiple_of(half_ref[0] * (blocks * BLK), BLK)

    def here(n):
        return pl.ds(n * width, width)

    def there(n):
        return pl.ds(pl.multiple_of(start + n * width, BLK), width)

    def bring(n, p):
        return pltpu.make_async_copy(params_ref.at[p, :, there(n)], cells_ref.at[p, :, here(n)], in_sems.at[n, p])

    def send(n, p):
        return pltpu.make_async_copy(new_ref.at[p, :, here(n)], out_ref.at[p, :, there(n)], out_sems.at[n, p])

    at = pl.ds(pl.multiple_of(half_ref[0] * (blocks * NNZ), BLK), blocks * NNZ)
    both = [
        pltpu.make_async_copy(all_ref.at[:, at], isel_ref, sems.at[0]),
        pltpu.make_async_copy(theirs_ref, screened_ref, sems.at[1]),
    ]
    for copy in both:
        copy.start()
    for n in range(steps):
        for p in range(2):
            bring(n, p).start()
    for copy in both:
        copy.wait()
    for n in range(steps):
        for p in range(2):
            bring(n, p).wait()
        for g in range(n * GROUP, (n + 1) * GROUP):
            change_block(isel_ref, screened_ref, cells_ref, new_ref, g)
        for p in range(2):
            send(n, p).start()
    for n in range(steps):
        for p in range(2):
            send(n, p).wait()


vmem = pl.BlockSpec(memory_space=pltpu.VMEM)
smem = pl.BlockSpec(memory_space=pltpu.SMEM)
hbm = pl.BlockSpec(memory_space=pl.ANY)
limit = pltpu.CompilerParams(vmem_limit_bytes=62 * 1024 * 1024)
whole_limit = pltpu.CompilerParams(vmem_limit_bytes=64 * 1024 * 1024)


def pack(core, predicted, perturbation, observed, obs_sd, slabs):
    whole = jax.ShapeDtypeStruct((slabs, ROWS, BLK), bf16)
    return pl.pallas_call(
        pack_kernel,
        out_shape=whole,
        in_specs=[smem, vmem, vmem, vmem, vmem],
        out_specs=vmem,
        compiler_params=limit,
        name="pack",
    )(core, predicted, perturbation, observed[None], obs_sd[None])


def make_maps(core, block_map, own, other, near, far):
    blocks = block_map.shape[0]
    data = own.shape[0] * BLK
    return pl.pallas_call(
        map_kernel,
        out_shape=(
            jax.ShapeDtypeStruct((2 * MP, MP), bf16),
            jax.ShapeDtypeStruct((SYS - 1, 2 * MP, MP), bf16),
            jax.ShapeDtypeStruct((blocks * NNZ, BLK), f32),
            jax.ShapeDtypeStruct((2 * blocks * NNZ, BLK), f32),
        ),
        in_specs=[smem, hbm, hbm, hbm, vmem, vmem],
        out_specs=(hbm, hbm, hbm, hbm),
        scratch_shapes=[
            pltpu.VMEM((data, MP), bf16),
            pltpu.VMEM((2, ROWS, data), bf16),
            pltpu.VMEM((2 * data, BLK), f32),
            pltpu.VMEM((2 * data, BLK), f32),
            pltpu.VMEM((blocks * NNZ, BLK), f32),
            pltpu.VMEM((2 * blocks * NNZ, BLK), f32),
            pltpu.VMEM((SYS, M, MP), f32),
            pltpu.VMEM(own.shape, bf16),
            pltpu.VMEM(own.shape, bf16),
            pltpu.SMEM(block_map.shape, jnp.int32),
            pltpu.SemaphoreType.DMA((2 * PARTS + 1,)),
            pltpu.VMEM((SYS, 2 * MP, MP), bf16),
            pltpu.SemaphoreType.DMA((SYS + 2,)),
        ] + [pltpu.VMEM((M, MP), f32)] * SYS,
        compiler_params=limit,
        cost_estimate=pl.CostEstimate(flops=20_000_000_000, bytes_accessed=8_000_000, transcendentals=0),
        name="maps",
    )(core, block_map, own, other, near, far)


def arrange(pline, iline):
    steps = 4
    prows, irows = pline.shape[0] // steps, iline.shape[0] // steps
    return pl.pallas_call(
        arrange_kernel,
        out_shape=(
            jax.ShapeDtypeStruct((pline.shape[0] // 2, MP), bf16),
            jax.ShapeDtypeStruct((MP, iline.shape[0] // 2), bf16),
        ),
        grid=(steps,),
        in_specs=[pl.BlockSpec((prows, BLK), lambda i: (i, 0)), pl.BlockSpec((irows, BLK), lambda i: (i, 0))],
        out_specs=(
            pl.BlockSpec((prows // 2, MP), lambda i: (i, 0)),
            pl.BlockSpec((MP, irows // 2), lambda i: (0, i)),
        ),
        compiler_params=limit,
        cost_estimate=pl.CostEstimate(flops=6_000_000_000, bytes_accessed=9_000_000, transcendentals=0),
        name="arrange",
    )(pline, iline)


def screen(core, psel, isel, full, mine, theirs, params):
    blocks = params.shape[2] // BLK // 2
    steps = blocks // GROUP
    cells = pl.BlockSpec((2, M, GROUP * BLK), lambda i, c: (0, 0, c[0] * steps + i))
    rows = pl.BlockSpec((GROUP * NNZ, MP), lambda i, c: (i, 0))
    return pl.pallas_call(
        gain_kernel,
        out_shape=(
            jax.ShapeDtypeStruct((blocks, NNZ, 2 * BLK), bf16),
            jax.ShapeDtypeStruct(params.shape, f32),
        ),
        grid_spec=pltpu.PrefetchScalarGridSpec(
            num_scalar_prefetch=1,
            grid=(steps,),
            in_specs=[rows, pl.BlockSpec((MP, GROUP * NNZ), lambda i, c: (0, c[0] * steps + i)), hbm, hbm, hbm, cells],
            out_specs=(pl.BlockSpec((GROUP, NNZ, 2 * BLK), lambda i, c: (i, 0, 0)), cells),
            scratch_shapes=[
                pltpu.VMEM((GROUP, MAPS * NNZ, MP), bf16),
                pltpu.VMEM((MAPS, 2 * MP, MP), bf16),
                pltpu.SemaphoreType.DMA((MAPS,)),
            ],
        ),
        compiler_params=limit,
        cost_estimate=pl.CostEstimate(flops=20_000_000_000, bytes_accessed=16_000_000, transcendentals=0),
        name="gains",
    )(core, psel, isel, full, mine, theirs, params)


def update(half, isel, screened, params, so_far):
    blocks = screened.shape[0]
    steps = blocks // GROUP
    return pl.pallas_call(
        change_kernel,
        out_shape=jax.ShapeDtypeStruct(params.shape, f32),
        in_specs=[smem, hbm, hbm, hbm, hbm],
        out_specs=hbm,
        scratch_shapes=[
            pltpu.VMEM((MP, blocks * NNZ), bf16),
            pltpu.VMEM(screened.shape, bf16),
            pltpu.VMEM((2, M, blocks * BLK), bf16),
            pltpu.VMEM((2, M, blocks * BLK), f32),
            pltpu.SemaphoreType.DMA((2,)),
            pltpu.SemaphoreType.DMA((steps, 2)),
            pltpu.SemaphoreType.DMA((steps, 2)),
        ],
        input_output_aliases={4: 0},
        compiler_params=whole_limit,
        cost_estimate=pl.CostEstimate(flops=5_000_000_000, bytes_accessed=10_000_000, transcendentals=0),
        name="change",
    )(half, isel, screened, params, so_far)


def on_device(params, predicted, perturbation, observed, obs_sd, members, block_map):
    boot = lax.axis_index("boot")
    core = lax.rem(boot, 2)
    core_arg = core.reshape(1).astype(jnp.int32)
    slabs = lax.axis_size("slab")
    pair = [(i, i ^ 1) for i in range(4)]
    far = [(i, i ^ 2) for i in range(4)]

    whole = pack(core_arg, predicted, perturbation, observed, obs_sd, slabs)
    own = lax.all_to_all(whole, "slab", 0, 0)
    own, late_members = lax.optimization_barrier((own, members))
    far_members = lax.ppermute(late_members, "boot", far)
    other = lax.ppermute(own, "boot", pair)

    full, mine, pline, iline = make_maps(core_arg, block_map, own, other, members, far_members)
    theirs = lax.ppermute(mine, "boot", pair)
    psel, isel = arrange(pline, iline)
    screened, so_far = screen(core_arg, psel, isel, full, mine, theirs, params)
    screened_other = lax.ppermute(screened, "boot", pair)
    return update(1 - core_arg, isel, screened_other, params, so_far)


def solution(mesh):
    return jax.shard_map(
        on_device,
        mesh=mesh,
        in_specs=(
            P(None, None, "slab"),
            P(None, "slab"),
            P(None, "slab"),
            P("slab"),
            P("slab"),
            P("boot", None),
            P("slab", None),
        ),
        out_specs=P(None, None, "slab"),
        check_vma=False,
    )
```

```python
from functools import partial
import math

import jax
import jax.numpy as jnp
from jax import lax
from jax.experimental import pallas as pl
from jax.experimental.pallas import tpu as pltpu
from jax.sharding import PartitionSpec as P

M = 200
NB = 16
BLK = 128
NNZ = 64
MP = 256
ROWS = 208
PIV = 40
SYS = 9
PARTS = 4
PACK = 3
MAPS = 17
GROUP = 8

screen_floor = 1e-05
f32 = jnp.float32
bf16 = jnp.bfloat16


def iota(shape, dim):
    return lax.broadcasted_iota(jnp.int32, shape, dim)


def split3(x):
    hi = x.astype(bf16).astype(f32)
    rest = x - hi
    mid = rest.astype(bf16).astype(f32)
    return hi, mid, rest - mid


def lhs6(c):
    hi, mid, lo = split3(c)
    left = hi + pltpu.roll(hi, PIV, 1) + pltpu.roll(hi, 2 * PIV, 1)
    right = mid + pltpu.roll(mid, PIV, 1) + pltpu.roll(lo, 2 * PIV, 1)
    return jnp.concatenate([left, right], axis=1).astype(bf16)


def rhs6(r):
    hi, mid, lo = split3(r)
    pad = jnp.zeros((BLK - 3 * PIV, MP), f32)
    return jnp.concatenate([hi, mid, lo, pad, hi, mid, hi, pad], axis=0).astype(bf16)


def dot(a, b):
    return jnp.dot(a, b, preferred_element_type=f32)


def scaling(listed):
    lane = iota((M, MP), 1)
    if listed is None:
        down = jnp.ones((M, 1), f32)
        across = jnp.where(lane[:1] < M, 1.0, 0.0)
    else:
        down = jnp.sqrt(jnp.sum(jnp.where(iota((M, M), 0) == listed, 1.0, 0.0), axis=1, keepdims=True))
        across = jnp.sum(jnp.where(iota((M, MP), 0) == lane, down, 0.0), axis=0, keepdims=True)
    root = 1.0 / math.sqrt(M)
    return down * (1.0 / (M - 1)) * across, down * root, across * root


def pack_kernel(core_ref, pred_ref, pert_ref, obs_ref, sd_ref, out_ref):
    sd = sd_ref[...].astype(f32)
    ens = pred_ref[...].astype(f32)
    innov = obs_ref[...].astype(f32) + sd * pert_ref[...].astype(f32) - ens
    rows = jnp.where(core_ref[0] == 0, ens, innov)
    tail = jnp.concatenate([sd, jnp.zeros((ROWS - M - 1, BLK), f32)], axis=0)
    part = jnp.concatenate([rows, tail], axis=0).astype(bf16)
    for i in range(out_ref.shape[0]):
        out_ref[i] = part


def gathered(own_first, own_ref, other_ref, ens_ref, innov_ref, map_ref, index_ref, sems):
    step = ens_ref.shape[0] // PARTS

    def copy(source, target, n):
        at = pl.ds(n % PARTS * step, step)
        return pltpu.make_async_copy(source.at[at], target.at[at], sems.at[n])

    def start(first_ref, second_ref):
        for n in range(PARTS):
            copy(first_ref, ens_ref, n).start()
        index_copy.start()
        for n in range(PARTS):
            copy(second_ref, innov_ref, PARTS + n).start()

    index_copy = pltpu.make_async_copy(map_ref, index_ref, sems.at[2 * PARTS])

    @pl.when(own_first)
    def _():
        start(own_ref, other_ref)

    @pl.when(jnp.logical_not(own_first))
    def _():
        start(other_ref, own_ref)

    def wait(n):
        if n == 2 * PARTS:
            index_copy.wait()
        else:
            copy(own_ref, ens_ref if n < PARTS else innov_ref, n).wait()

    return wait


def chunk_rows(rows_ref, i):
    rows = rows_ref[i].astype(f32)
    high = jnp.concatenate([rows[BLK:], jnp.zeros((MP - ROWS, BLK), f32)], axis=0)
    return rows, rows[:BLK], high


def by_parts(count, first, wait, chunk):
    step = count // PARTS
    for n in range(PARTS):
        wait(first + n)
        lax.fori_loop(n * step, (n + 1) * step, chunk, 0, unroll=8)


def fill_table(t_ref, i, low, high):
    base = pl.multiple_of(i * (2 * BLK), 8)
    t_ref[pl.ds(base, BLK, stride=2), :] = low
    t_ref[pl.ds(base + 1, BLK, stride=2), :] = high


def along(tile, u):
    return jnp.broadcast_to(tile[u:u + 1], tile.shape)


def inverse_of(x):
    guess = pl.reciprocal(x, approx=True)
    guess = guess * (2.0 - x * guess)
    return guess * (2.0 - x * guess)


def map_kernel(
    core_ref, map_ref, own_ref, other_ref, near_ref, far_ref, full_ref, res_ref, psel_ref, isel_ref,
    ens_ref, parts_ref, ptab_ref, itab_ref, pline_ref, iline_ref, scale_ref, rows_ref, late_ref, index_ref,
    sems, maps_ref, out_sems, *sys_refs
):
    core = core_ref[0]
    blocks = map_ref.shape[0]
    wait = gathered(core == 0, own_ref, other_ref, rows_ref, late_ref, map_ref, index_ref, sems)
    near = near_ref.shape[0]

    def chunk(i, carry):
        rows, low, high = chunk_rows(rows_ref, i)
        sd = rows[M:M + 1]
        at = pl.ds(pl.multiple_of(i * BLK, BLK), BLK)
        for n, part in enumerate(split3(rows * (1.0 / (sd * sd)))[:2]):
            parts_ref[n, :, at] = part.astype(bf16)
        low, high = low.T, high.T
        ens_ref[at, :] = jnp.concatenate([low, high], axis=1).astype(bf16)
        fill_table(ptab_ref, i, low, high)
        return carry

    by_parts(rows_ref.shape[0], 0, wait, chunk)

    def late_chunk(i, carry):
        _, low, high = chunk_rows(late_ref, i)
        fill_table(itab_ref, i, low.T, high.T)
        return carry

    by_parts(late_ref.shape[0], PARTS, wait, late_chunk)
    wait(2 * PARTS)

    gram = 0.0
    for n in (1, 0):
        gram = gram + dot(parts_ref[n], ens_ref[...])
    gram = gram[:M]

    ipanel = -(-blocks // (M // PIV))
    ppanel = -(-(blocks // 2) // (M // PIV))
    share = -(-(ipanel + ppanel) * NNZ // PIV)

    def pick(kp, t):
        for n in range(t * share, min((t + 1) * share, (ipanel + ppanel) * NNZ)):
            b, j = n // NNZ, n % NNZ
            if b < ipanel:
                k = jnp.minimum(kp * ipanel + b, blocks - 1)
                at = index_ref[k, j]
                iline_ref[pl.ds(k * (2 * NNZ) + 2 * j, 2), :] = itab_ref[pl.ds(2 * at, 2), :]
            else:
                k = jnp.minimum(kp * ppanel + b - ipanel, blocks // 2 - 1)
                at = index_ref[core * (blocks // 2) + k, j]
                pline_ref[pl.ds(k * (2 * NNZ) + 2 * j, 2), :] = ptab_ref[pl.ds(2 * at, 2), :]

    row = iota((M, MP), 0)
    lane = iota((M, MP), 1)
    for s in range(SYS):
        listed = None
        if s:
            listed = near_ref[s - 1:s, :] if s <= near else far_ref[s - 1 - near:s - near, :]
        scale, ud, ua = scaling(listed)
        scale_ref[s] = scale
        h = gram * scale
        hu = jnp.sum(h * ua, axis=1, keepdims=True)
        uh = jnp.sum(h * ud, axis=0, keepdims=True)
        uhu = jnp.sum(hu * ud, axis=0, keepdims=True)
        h = h - ud * (uh - 0.5 * uhu * ua) - (hu - 0.5 * uhu * ud) * ua
        sys_refs[s][...] = h + jnp.where(row == lane, 1.0, 0.0)

    prow = iota((PIV, MP), 0)
    plane = iota((PIV, MP), 1)
    dlane = iota((PIV, BLK), 1)
    trow = iota((8, BLK), 0)
    tlane = iota((8, BLK), 1)
    first = jnp.minimum(tlane // PIV, PACK - 1) * PIV
    inner = tlane - first

    def panel_step(kp, carry):
        k0 = kp * PIV
        at = pl.ds(pl.multiple_of(k0, 8), PIV)
        packs = []
        for g in range(SYS // PACK):
            pack = jnp.zeros((PIV, BLK), f32)
            for q in range(PACK):
                moved = pltpu.roll(sys_refs[PACK * g + q][at, :], lax.rem(MP - k0 + q * PIV, MP), 1)[:, :BLK]
                pack = jnp.where((dlane >= q * PIV) & (dlane < (q + 1) * PIV), moved, pack)
            packs.append(pack)
        starts = packs
        tiles = [[pack[8 * i:8 * i + 8] for i in range(PIV // 8)] for pack in packs]
        for j in range(PIV // 8):
            cols = [
                [[jnp.take_along_axis(tile, first + 8 * j + u, axis=1) for u in range(8)] for tile in group]
                for group in tiles
            ]
            for u in range(8):
                at_lane = inner == 8 * j + u
                for group, col in zip(tiles, cols):
                    lead = col[j][u]
                    scale = inverse_of(along(lead, u))
                    t = group[j]
                    line = jnp.where(at_lane, 1.0, along(t, u)) * scale
                    group[j] = jnp.where(trow == u, line, jnp.where(at_lane, 0.0, t) - lead * line)
                    for v in range(u + 1, 8):
                        c = col[j][v]
                        line = along(c, u) * scale
                        col[j][v] = jnp.where(trow == u, line, c - lead * line)
                pick(kp, 8 * j + u)
            done = (inner >= 8 * j) & (inner < 8 * j + 8)
            for group, col in zip(tiles, cols):
                for i in range(PIV // 8):
                    if i != j:
                        tile = jnp.where(done, 0.0, group[i])
                        for u in range(8):
                            tile = tile - col[i][u] * group[j][u:u + 1]
                        group[i] = tile
        packs = [jnp.concatenate(group, axis=0) for group in tiles]
        inside = (lane >= k0) & (lane < k0 + PIV)
        pad = jnp.zeros((BLK - 3 * PIV, MP), f32)
        inverses, blocks_, panels, wanted, lines = [], [], [], [], []
        for s in range(SYS):
            back = (BLK - (s % PACK) * PIV) % BLK
            for kept, source in ((inverses, packs), (blocks_, starts)):
                moved = source[s // PACK]
                if back:
                    moved = pltpu.roll(moved, back, 1)
                kept.append(lhs6(jnp.where(dlane < PIV, moved, 0.0)))
            panels.append(sys_refs[s][at, :])
            wanted.append(jnp.where(plane == prow + k0, -1.0, jnp.where(inside[:PIV], 0.0, panels[s])))
        for s in range(SYS):
            lines.append(dot(inverses[s], rhs6(wanted[s])))
        offs = [wanted[s] - dot(blocks_[s], rhs6(lines[s])) for s in range(SYS)]
        for s in range(SYS):
            lines[s] = lines[s] + dot(inverses[s], rhs6(offs[s]))
        for s in range(SYS):
            hi, mid, lo = split3(panels[s])
            left = jnp.concatenate([hi, hi, hi, pad, mid, mid, lo, pad], axis=0).astype(bf16)
            change = lax.dot_general(left, rhs6(lines[s]), (((0,), (0,)), ((), ())), preferred_element_type=f32)
            sys_refs[s][...] = jnp.where(inside, 0.0, sys_refs[s][...]) - change[:M]
            sys_refs[s][at, :] = lines[s]
        return carry

    lax.fori_loop(0, M // PIV, panel_step, 0)

    outs = [
        pltpu.make_async_copy(pline_ref.at[pl.ds(0, psel_ref.shape[0])], psel_ref, out_sems.at[SYS]),
        pltpu.make_async_copy(iline_ref.at[pl.ds(0, isel_ref.shape[0])], isel_ref, out_sems.at[SYS + 1]),
    ]
    for copy in outs:
        copy.start()
    for s in range(SYS):
        scale = scale_ref[s]
        value = (-sys_refs[s][...] - scale * ((M - 1) / M)) * scale
        value = jnp.concatenate([value, jnp.zeros((MP - M, MP), f32)], axis=0)
        hi = value.astype(bf16)
        maps_ref[s] = jnp.concatenate([hi, (value - hi.astype(f32)).astype(bf16)], axis=0)
        outs.append(pltpu.make_async_copy(maps_ref.at[s], res_ref.at[s - 1] if s else full_ref, out_sems.at[s]))
        outs[-1].start()
    for copy in outs:
        copy.wait()


def arrange_kernel(pline_ref, iline_ref, psel_ref, isel_ref):
    for n in range(2):
        lanes = slice(n * BLK, (n + 1) * BLK)
        psel_ref[:, lanes] = pline_ref[pl.ds(n, psel_ref.shape[0], stride=2), :].astype(bf16)
        for k in range(isel_ref.shape[1] // BLK):
            at = slice(k * BLK, (k + 1) * BLK)
            isel_ref[lanes, at] = iline_ref[pl.ds(2 * k * BLK + n, BLK, stride=2), :].T.astype(bf16)


def change_block(isel_ref, screened_ref, cells_ref, new_ref, g):
    picked = isel_ref[:ROWS, g // 2 * BLK:(g // 2 + 1) * BLK]
    none = jnp.zeros((NNZ, 2 * BLK), bf16)
    rows = [none, screened_ref[g]] if g % 2 else [screened_ref[g], none]
    change = dot(picked, jnp.concatenate(rows, axis=0))
    at = slice(g * BLK, (g + 1) * BLK)
    for p in range(2):
        new_ref[p, :, at] = cells_ref[p, :, at].astype(f32) + change[:M, p * BLK:(p + 1) * BLK]


def gain_kernel(core_ref, psel_ref, isel_ref, full_ref, mine_ref, theirs_ref, params_ref, screened_ref, out_ref, cols_ref, maps_ref, sems):
    refs = [full_ref] + [mine_ref.at[r] for r in range(SYS - 1)] + [theirs_ref.at[r] for r in range(SYS - 1)]
    copies = [pltpu.make_async_copy(ref, maps_ref.at[r], sems.at[r]) for r, ref in enumerate(refs)]
    opening = pl.program_id(0) == 0

    @pl.when(opening)
    def _():
        for copy in copies:
            copy.start()

    x = psel_ref[...]
    sd = x[:, M:M + 1].astype(f32)
    weight = 1.0 / (sd * sd)
    x = jnp.concatenate([x, x], axis=1)

    for some in (range(4), range(4, 10), range(10, MAPS)):
        @pl.when(opening)
        def _():
            for r in some:
                copies[r].wait()

        for r in some:
            total = (dot(x, maps_ref[r]) * weight).astype(bf16)
            for g in range(GROUP):
                cols_ref[g, r * NNZ:(r + 1) * NNZ, :] = total[g * NNZ:(g + 1) * NNZ]

    def gains(g, carry):
        at = pl.ds(pl.multiple_of(g * BLK, BLK), BLK)
        cells = jnp.concatenate([params_ref[0, :, at], params_ref[1, :, at]], axis=1)
        every = dot(cols_ref[g][:, :M], cells)
        full = every[:NNZ]
        spread = jnp.zeros_like(full)
        for r in range(1, MAPS):
            off = every[r * NNZ:(r + 1) * NNZ] - full
            spread = spread + off * off
        squared = full * full
        screened_ref[g] = (squared / (squared + spread * (1.0 / NB) + screen_floor) * full).astype(bf16)
        return carry

    lax.fori_loop(0, GROUP, gains, 0, unroll=GROUP)
    for g in range(GROUP):
        change_block(isel_ref, screened_ref, params_ref, out_ref, g)


def change_kernel(half_ref, all_ref, theirs_ref, params_ref, so_far_ref, out_ref, isel_ref, screened_ref, cells_ref, new_ref, sems, in_sems, out_sems):
    blocks = screened_ref.shape[0]
    width = GROUP * BLK
    steps = blocks // GROUP
    start = pl.multiple_of(half_ref[0] * (blocks * BLK), BLK)

    def here(n):
        return pl.ds(n * width, width)

    def there(n):
        return pl.ds(pl.multiple_of(start + n * width, BLK), width)

    def bring(n, p):
        return pltpu.make_async_copy(params_ref.at[p, :, there(n)], cells_ref.at[p, :, here(n)], in_sems.at[n, p])

    def send(n, p):
        return pltpu.make_async_copy(new_ref.at[p, :, here(n)], out_ref.at[p, :, there(n)], out_sems.at[n, p])

    at = pl.ds(pl.multiple_of(half_ref[0] * (blocks * NNZ), BLK), blocks * NNZ)
    both = [
        pltpu.make_async_copy(all_ref.at[:, at], isel_ref, sems.at[0]),
        pltpu.make_async_copy(theirs_ref, screened_ref, sems.at[1]),
    ]
    for copy in both:
        copy.start()
    for n in range(steps):
        for p in range(2):
            bring(n, p).start()
    for copy in both:
        copy.wait()
    for n in range(steps):
        for p in range(2):
            bring(n, p).wait()
        for g in range(n * GROUP, (n + 1) * GROUP):
            change_block(isel_ref, screened_ref, cells_ref, new_ref, g)
        for p in range(2):
            send(n, p).start()
    for n in range(steps):
        for p in range(2):
            send(n, p).wait()


vmem = pl.BlockSpec(memory_space=pltpu.VMEM)
smem = pl.BlockSpec(memory_space=pltpu.SMEM)
hbm = pl.BlockSpec(memory_space=pl.ANY)
limit = pltpu.CompilerParams(vmem_limit_bytes=62 * 1024 * 1024)
whole_limit = pltpu.CompilerParams(vmem_limit_bytes=64 * 1024 * 1024)


def pack(core, predicted, perturbation, observed, obs_sd, slabs):
    whole = jax.ShapeDtypeStruct((slabs, ROWS, BLK), bf16)
    return pl.pallas_call(
        pack_kernel,
        out_shape=whole,
        in_specs=[smem, vmem, vmem, vmem, vmem],
        out_specs=vmem,
        compiler_params=limit,
        name="pack",
    )(core, predicted, perturbation, observed[None], obs_sd[None])


def make_maps(core, block_map, own, other, near, far):
    blocks = block_map.shape[0]
    data = own.shape[0] * BLK
    return pl.pallas_call(
        map_kernel,
        out_shape=(
            jax.ShapeDtypeStruct((2 * MP, MP), bf16),
            jax.ShapeDtypeStruct((SYS - 1, 2 * MP, MP), bf16),
            jax.ShapeDtypeStruct((blocks * NNZ, BLK), f32),
            jax.ShapeDtypeStruct((2 * blocks * NNZ, BLK), f32),
        ),
        in_specs=[smem, hbm, hbm, hbm, vmem, vmem],
        out_specs=(hbm, hbm, hbm, hbm),
        scratch_shapes=[
            pltpu.VMEM((data, MP), bf16),
            pltpu.VMEM((2, ROWS, data), bf16),
            pltpu.VMEM((2 * data + 8, BLK), f32),
            pltpu.VMEM((2 * data + 8, BLK), f32),
            pltpu.VMEM((blocks * NNZ + 8, BLK), f32),
            pltpu.VMEM((2 * blocks * NNZ + 8, BLK), f32),
            pltpu.VMEM((SYS, M, MP), f32),
            pltpu.VMEM(own.shape, bf16),
            pltpu.VMEM(own.shape, bf16),
            pltpu.SMEM(block_map.shape, jnp.int32),
            pltpu.SemaphoreType.DMA((2 * PARTS + 1,)),
            pltpu.VMEM((SYS, 2 * MP, MP), bf16),
            pltpu.SemaphoreType.DMA((SYS + 2,)),
        ] + [pltpu.VMEM((M, MP), f32)] * SYS,
        compiler_params=limit,
        cost_estimate=pl.CostEstimate(flops=20_000_000_000, bytes_accessed=8_000_000, transcendentals=0),
        name="maps",
    )(core, block_map, own, other, near, far)


def arrange(pline, iline):
    steps = 4
    prows, irows = pline.shape[0] // steps, iline.shape[0] // steps
    return pl.pallas_call(
        arrange_kernel,
        out_shape=(
            jax.ShapeDtypeStruct((pline.shape[0] // 2, MP), bf16),
            jax.ShapeDtypeStruct((MP, iline.shape[0] // 2), bf16),
        ),
        grid=(steps,),
        in_specs=[pl.BlockSpec((prows, BLK), lambda i: (i, 0)), pl.BlockSpec((irows, BLK), lambda i: (i, 0))],
        out_specs=(
            pl.BlockSpec((prows // 2, MP), lambda i: (i, 0)),
            pl.BlockSpec((MP, irows // 2), lambda i: (0, i)),
        ),
        compiler_params=limit,
        cost_estimate=pl.CostEstimate(flops=6_000_000_000, bytes_accessed=9_000_000, transcendentals=0),
        name="arrange",
    )(pline, iline)


def screen(core, psel, isel, full, mine, theirs, params):
    blocks = params.shape[2] // BLK // 2
    steps = blocks // GROUP
    cells = pl.BlockSpec((2, M, GROUP * BLK), lambda i, c: (0, 0, c[0] * steps + i))
    rows = pl.BlockSpec((GROUP * NNZ, MP), lambda i, c: (i, 0))
    return pl.pallas_call(
        gain_kernel,
        out_shape=(
            jax.ShapeDtypeStruct((blocks, NNZ, 2 * BLK), bf16),
            jax.ShapeDtypeStruct(params.shape, f32),
        ),
        grid_spec=pltpu.PrefetchScalarGridSpec(
            num_scalar_prefetch=1,
            grid=(steps,),
            in_specs=[rows, pl.BlockSpec((MP, GROUP * NNZ), lambda i, c: (0, c[0] * steps + i)), hbm, hbm, hbm, cells],
            out_specs=(pl.BlockSpec((GROUP, NNZ, 2 * BLK), lambda i, c: (i, 0, 0)), cells),
            scratch_shapes=[
                pltpu.VMEM((GROUP, MAPS * NNZ, MP), bf16),
                pltpu.VMEM((MAPS, 2 * MP, MP), bf16),
                pltpu.SemaphoreType.DMA((MAPS,)),
            ],
        ),
        compiler_params=limit,
        cost_estimate=pl.CostEstimate(flops=20_000_000_000, bytes_accessed=16_000_000, transcendentals=0),
        name="gains",
    )(core, psel, isel, full, mine, theirs, params)


def update(half, isel, screened, params, so_far):
    blocks = screened.shape[0]
    steps = blocks // GROUP
    return pl.pallas_call(
        change_kernel,
        out_shape=jax.ShapeDtypeStruct(params.shape, f32),
        in_specs=[smem, hbm, hbm, hbm, hbm],
        out_specs=hbm,
        scratch_shapes=[
            pltpu.VMEM((MP, blocks * NNZ), bf16),
            pltpu.VMEM(screened.shape, bf16),
            pltpu.VMEM((2, M, blocks * BLK), bf16),
            pltpu.VMEM((2, M, blocks * BLK), f32),
            pltpu.SemaphoreType.DMA((2,)),
            pltpu.SemaphoreType.DMA((steps, 2)),
            pltpu.SemaphoreType.DMA((steps, 2)),
        ],
        input_output_aliases={4: 0},
        compiler_params=whole_limit,
        cost_estimate=pl.CostEstimate(flops=5_000_000_000, bytes_accessed=10_000_000, transcendentals=0),
        name="change",
    )(half, isel, screened, params, so_far)


def on_device(params, predicted, perturbation, observed, obs_sd, members, block_map):
    boot = lax.axis_index("boot")
    core = lax.rem(boot, 2)
    core_arg = core.reshape(1).astype(jnp.int32)
    slabs = lax.axis_size("slab")
    pair = [(i, i ^ 1) for i in range(4)]
    far = [(i, i ^ 2) for i in range(4)]

    whole = pack(core_arg, predicted, perturbation, observed, obs_sd, slabs)
    own = lax.all_to_all(whole, "slab", 0, 0)
    own, late_members = lax.optimization_barrier((own, members))
    far_members = lax.ppermute(late_members, "boot", far)
    other = lax.ppermute(own, "boot", pair)

    full, mine, pline, iline = make_maps(core_arg, block_map, own, other, members, far_members)
    theirs = lax.ppermute(mine, "boot", pair)
    psel, isel = arrange(pline, iline)
    screened, so_far = screen(core_arg, psel, isel, full, mine, theirs, params)
    screened_other = lax.ppermute(screened, "boot", pair)
    return update(1 - core_arg, isel, screened_other, params, so_far)


def solution(mesh):
    return jax.shard_map(
        on_device,
        mesh=mesh,
        in_specs=(
            P(None, None, "slab"),
            P(None, "slab"),
            P(None, "slab"),
            P("slab"),
            P("slab"),
            P("boot", None),
            P("slab", None),
        ),
        out_specs=P(None, None, "slab"),
        check_vma=False,
    )
```
